128 devices in a mesh: prow: 8 (over y, core), pcol: 16 (over x, z).
Axes of the slice: x: 4, y: 4, z: 4, core: 2. Of those that a mesh axis runs over, the one named last changes fastest.
Arguments:
- front: float32 [4, 8, 512, 2, 16, 512], P(None, 'prow', None, None, 'pcol'), as said below
- child_blocks: bfloat16 [8, 16, 16, 3, 256, 256], P('prow', 'pcol'), may hold values from -0.015625 to 0.015625
- row_map: int32 [2, 60], replicated, may hold values from 0 to 63, as said below
- slot_table: int32 [8, 16, 16, 3], replicated, may hold values from -1 to 7199, as said below
- struct_mask: int32 [64, 64], replicated, may hold values 0 or 1
Outputs:
- factored: float32 [4, 8, 512, 2, 16, 512], P(None, 'prow', None, None, 'pcol')
The draws below stay inside these ranges and needn't reach their ends.
Inputs may be any that keep to these rules, and one draw needn't show every extreme that they name: `front`: with the children's blocks added, the lower triangle of the leading 2 * 512 rows and columns defines a symmetric positive definite matrix; diagonal entries are of order one, the others far smaller. Each row of row_map is strictly increasing. `slot_table`: every code c * 60 * 60 + i * 60 + j with c in 0..1 and i >= j appears in exactly one slot; a slot [p, s, q, k] holds a block whose front row lies in panel-wide block rows of grid row p and whose front column lies in panel-wide block columns of grid column q; the other slots hold -1; some grid row p and grid column q receive 3 blocks from every s.
All inputs are finite; a program needn't handle non-finite values.
Results may differ from the reference program's by a relative error of at most 0.00089.
Values may be sent and summed in bfloat16 or wider, within the bound.
No kernel may reach another device: no remote copies, remote signals or barrier semaphores. Data moves between devices by JAX's collectives and lax.ppermute only.
A program may use at most 192 MiB of HBM per device.

```python
import jax
import jax.numpy as jnp
import numpy as np
from jax import lax

F = 16384
BLK = 256
PW = 512
NB = 32
NBR = 4
NBC = 2
NSB = 64
MISS = 4
CNB = 60
NPAN = 2
CAP = 3
N_PROW = 8
N_PCOL = 16


def draw_front(key, part):
    factor_key, noise_key, shift_key = jax.random.split(key, 3)
    inner = F // 8
    leading = NPAN * PW
    factors = jnp.clip(jax.random.normal(factor_key, (F, inner), jnp.float32), -6.0, 6.0)
    noise = jnp.clip(jax.random.normal(noise_key, (F, F), jnp.float32), -6.0, 6.0)
    row_scale = jnp.ones((F,), jnp.float32)
    shift = jax.random.uniform(shift_key, (F,), jnp.float32, 0.75, 1.25)
    on_diagonal = lax.broadcasted_iota(jnp.int32, (F, F), 0) == lax.broadcasted_iota(jnp.int32, (F, F), 1)
    far_part = noise * (row_scale[:, None] / inner ** 0.5)
    far_part = far_part + jnp.where(on_diagonal, row_scale[:, None], jnp.float32(0.0))
    left_part = jnp.dot(factors, factors[:leading].T, precision=lax.Precision.HIGHEST) / inner
    full_matrix = far_part.at[:, :leading].set(left_part)
    full_matrix = full_matrix + jnp.where(on_diagonal, shift[:, None], jnp.float32(0.0))
    return full_matrix.reshape(NBR, N_PROW, PW, NBC, N_PCOL, PW)


def child_layout(key):
    base_key = jax.random.fold_in(key, 7031)
    sub_index = jnp.arange(NSB, dtype=jnp.int32)
    wide_index = sub_index // 2
    guarded = (wide_index % N_PROW == N_PROW - 1) | (wide_index % N_PCOL == 0)
    map_rows = []
    for child_id in range(2):
        ranking = jax.random.permutation(jax.random.fold_in(base_key, child_id), NSB).astype(jnp.int32)
        ranking = ranking + guarded.astype(jnp.int32) * NSB
        ordering = jnp.argsort(ranking, stable=True)
        kept = jnp.ones((NSB,), dtype=bool).at[ordering[:MISS]].set(False)
        map_rows.append(jnp.nonzero(kept, size=CNB)[0].astype(jnp.int32))
    row_map = jnp.stack(map_rows)
    tri_rows, tri_cols = np.tril_indices(CNB)
    pair_count = tri_rows.shape[0]
    owners = jnp.asarray(np.concatenate([np.zeros(pair_count, np.int32), np.ones(pair_count, np.int32)]))
    child_rows = jnp.asarray(np.concatenate([tri_rows, tri_rows]).astype(np.int32))
    child_cols = jnp.asarray(np.concatenate([tri_cols, tri_cols]).astype(np.int32))
    parent_row = row_map[owners, child_rows]
    parent_col = row_map[owners, child_cols]
    target_row = parent_row // 2 % N_PROW
    target_col = parent_col // 2 % N_PCOL
    group_ids = target_row * N_PCOL + target_col
    groups_total = N_PROW * N_PCOL
    one_hot = (group_ids[:, None] == jnp.arange(groups_total, dtype=jnp.int32)[None, :]).astype(jnp.int32)
    earlier = jnp.cumsum(one_hot, axis=0) - one_hot
    group_rank = jnp.sum(earlier * one_hot, axis=1)
    slot_width = N_PCOL * CAP
    favour = jax.random.randint(jax.random.fold_in(base_key, 2), (N_PROW, N_PCOL), 0, 4)
    jitter = jax.random.randint(jax.random.fold_in(base_key, 3), (groups_total, slot_width), 0, 64)
    positions = jnp.arange(slot_width, dtype=jnp.int32)
    group_favour = jnp.repeat(favour, N_PCOL, axis=0)[:, positions // CAP]
    scores = (group_favour * 64 + jitter) * slot_width + positions[None, :]
    slot_order = jnp.argsort(scores, axis=1, stable=True).astype(jnp.int32)
    chosen_slot = slot_order[group_ids, group_rank]
    source_col = chosen_slot // CAP
    slot_pos = chosen_slot % CAP
    code_value = owners * CNB * CNB + child_rows * CNB + child_cols
    slot_table = jnp.full((N_PROW, N_PCOL, N_PCOL, CAP), -1, jnp.int32)
    slot_table = slot_table.at[target_row, source_col, target_col, slot_pos].set(code_value)
    return (row_map, slot_table)


def draw_row_map(key, part):
    return child_layout(key)[0]


def draw_slot_table(key, part):
    return child_layout(key)[1]


def place_ends(drawn, own_key, least, largest):
    index_at = [jax.random.randint(jax.random.fold_in(own_key, axis), (), 0, length) for axis, length in enumerate(drawn.shape)]
    main_axis = drawn.shape.index(max(drawn.shape))
    next_to = index_at[:main_axis] + [(index_at[main_axis] + 1) % drawn.shape[main_axis]] + index_at[main_axis + 1:]
    return drawn.at[tuple(index_at)].set(least).at[tuple(next_to)].set(largest)


def levels(key, shape, cuts, least, high):
    gain, own = 1.0, jax.random.fold_in(key, 6)
    for dim, blocks in cuts:
        heights = jnp.exp(jax.random.uniform(jax.random.fold_in(own, dim), (blocks,), jnp.float32, least / len(cuts), high / len(cuts)))
        gain = gain * jnp.repeat(heights, shape[dim] // blocks).reshape([-1 if axis == dim else 1 for axis in range(len(shape))])
    return gain


def centred(stream_key, dims, spread, reach, cuts=(), kind=jnp.bfloat16):
    values = jax.random.normal(stream_key, dims, jnp.float32) * spread
    if len(cuts) > 0:
        values = levels(stream_key, dims, cuts, -0.22, 0.18) * values
    return jnp.clip(values, min=-reach, max=reach).astype(kind)


def setup_inputs(seed: int = 0) -> dict:
    key_list = jax.random.split(jax.random.key(seed), 6)
    front = draw_front(jax.random.fold_in(key_list[5], 71), 0)
    child_blocks = centred(key_list[1], (N_PROW, N_PCOL, N_PCOL, CAP, BLK, BLK), 0.003, 0.015625, ((0, 8), (1, 16)))
    row_map = draw_row_map(jax.random.fold_in(key_list[5], 71), 0)
    slot_table = draw_slot_table(jax.random.fold_in(key_list[5], 71), 0)
    struct_mask = place_ends((jax.random.randint(key_list[4], (NSB, NSB), 0, 4) < 3).astype(jnp.int32), jax.random.fold_in(key_list[4], 1), 0, 1)
    return {"front": front, "child_blocks": child_blocks, "row_map": row_map, "slot_table": slot_table, "struct_mask": struct_mask}


def reference(front, child_blocks, row_map, slot_table, struct_mask):
    matrix = front.reshape(F, F)
    quarters = matrix.reshape(NSB, BLK, NSB, BLK)
    flat_map = row_map.reshape(-1)
    for grid_row in range(N_PROW):
        slot_codes = slot_table[grid_row].reshape(-1)
        is_live = slot_codes >= 0
        code_value = jnp.maximum(slot_codes, 0)
        child_id = code_value // (CNB * CNB)
        child_row = code_value // CNB % CNB
        child_col = code_value % CNB
        parent_row = jnp.where(is_live, flat_map[child_id * CNB + child_row], 0).astype(jnp.int32)
        parent_col = jnp.where(is_live, flat_map[child_id * CNB + child_col], 0).astype(jnp.int32)
        pieces = child_blocks[grid_row].reshape(-1, BLK, BLK).astype(jnp.float32)
        pieces = jnp.where(is_live[:, None, None], pieces, jnp.float32(0.0))
        quarters = quarters.at[parent_row, :, parent_col, :].add(pieces)
    matrix = quarters.reshape(F, F)
    sub_index = jnp.arange(NSB) // 2
    low_blocks = sub_index[:, None] >= sub_index[None, :]
    weight = jnp.where((struct_mask > 0) & low_blocks, jnp.float32(1.0), jnp.float32(0.0))
    for panel_num in range(NPAN):
        start_col = panel_num * PW
        end_col = start_col + PW
        diag_block = matrix[start_col:end_col, start_col:end_col]
        symmetric = jnp.tril(diag_block) + jnp.tril(diag_block, -1).T
        factor = jnp.linalg.cholesky(symmetric)
        below = matrix[end_col:, start_col:end_col]
        solved = jax.scipy.linalg.solve_triangular(factor, below.T, lower=True).T
        matrix = matrix.at[start_col:end_col, start_col:end_col].set(factor)
        matrix = matrix.at[end_col:, start_col:end_col].set(solved)
        rounded = solved.astype(jnp.bfloat16).astype(jnp.float32)
        update = jnp.dot(rounded, rounded.T, precision=lax.Precision.HIGHEST)
        rest_blocks = NSB - 2 * (panel_num + 1)
        trail_weight = weight[2 * (panel_num + 1):, 2 * (panel_num + 1):]
        update = update.reshape(rest_blocks, BLK, rest_blocks, BLK) * trail_weight[:, None, :, None]
        matrix = matrix.at[end_col:, end_col:].add(-update.reshape(rest_blocks * BLK, rest_blocks * BLK))
    block_index = jnp.arange(NB)
    keep_blocks = jnp.where(block_index[:, None] >= block_index[None, :], jnp.float32(1.0), jnp.float32(0.0))
    matrix = (matrix.reshape(NB, PW, NB, PW) * keep_blocks[:, None, :, None]).reshape(F, F)
    return matrix.reshape(NBR, N_PROW, PW, NBC, N_PCOL, PW)
```

```python
import functools

import jax
import jax.numpy as jnp
from jax import lax
from jax.experimental import pallas as pl
from jax.experimental.pallas import tpu as pltpu
from jax.sharding import PartitionSpec as P

F32 = jnp.float32
BF16 = jnp.bfloat16
CNB = 60
NN = (((1,), (0,)), ((), ()))
NT = (((1,), (1,)), ((), ()))
MIB = 2**20
VMEM = pl.BlockSpec(memory_space=pltpu.VMEM)
SMEM = pl.BlockSpec(memory_space=pltpu.SMEM)


def split(x):
    high = x.astype(BF16)
    return high, (x - high.astype(F32)).astype(BF16)


def dot1(a, b, dims):
    return lax.dot_general(a, b, dims, preferred_element_type=F32)


def dot3(a, b, dims):
    ah, al = split(a)
    bh, bl = split(b)
    return dot1(ah, bh, dims) + (dot1(al, bh, dims) + dot1(ah, bl, dims))


def factor_base(S):
    n = S.shape[0]
    wide = 2 * n // 128
    lane = lax.broadcasted_iota(jnp.int32, (n, n), 1)
    sub = lax.broadcasted_iota(jnp.int32, (n, n), 0)
    M = jnp.concatenate([S, jnp.where(lane == sub, F32(1), F32(0))], axis=1)
    row = lax.broadcasted_iota(jnp.int32, (8, 1), 0)
    across = lambda v: jnp.concatenate([v] * wide, axis=1)
    done = []
    for o in range(0, n, 8):
        R = M[0:8]
        cols = [jnp.broadcast_to(R[:, o + j : o + j + 1], (8, 128)) for j in range(8)]
        D = [[jnp.broadcast_to(cols[j][i : i + 1], (8, 128)) for j in range(i + 1)] for i in range(8)]
        Y = [jnp.broadcast_to(R[i : i + 1], (8, 2 * n)) for i in range(8)]
        low = [[None] * 8 for _ in range(8)]
        inv = [None] * 8
        for j in range(8):
            inv[j] = 1.0 / D[j][j]
            for i in range(j + 1, 8):
                low[i][j] = D[i][j] * inv[j]
            for i in range(j + 1, 8):
                for m in range(j + 1, i + 1):
                    D[i][m] = D[i][m] - low[i][j] * D[m][j]
                Y[i] = Y[i] - across(low[i][j]) * Y[j]
        out = None
        for j in range(8):
            scaled = Y[j] * across(lax.rsqrt(D[j][j]))
            out = scaled if out is None else jnp.where(row == j, scaled, out)
        done.append(out)
        if o + 8 == n:
            break
        Z = [None] * 8
        for i in range(7, -1, -1):
            Z[i] = Y[i] * across(inv[i])
            for m in range(i + 1, 8):
                Z[i] = Z[i] - across(low[m][i]) * Z[m]
        step = Z[0]
        for i in range(1, 8):
            step = jnp.where(row == i, Z[i], step)
        parts = [jnp.zeros((o, 2 * n), F32)] if o else []
        parts += [step, jnp.zeros((n - o - 8, 2 * n), F32)]
        M = M[8:] - dot3(M[8:, :n], jnp.concatenate(parts, axis=0), NN)
    done = jnp.concatenate(done, axis=0)
    return jnp.where(lane >= sub, done[:, :n], F32(0)), jnp.where(lane <= sub, done[:, n:], F32(0))


def factor_whole(a_ref, l_ref, w_ref):
    n = a_ref.shape[0]
    b = 128
    w_ref[...] = jnp.zeros((n, n), F32)
    l_ref[...] = jnp.zeros((n, n), F32)
    lane = lax.broadcasted_iota(jnp.int32, (b, b), 1)
    sub = lax.broadcasted_iota(jnp.int32, (b, b), 0)
    for k in range(0, n, b):
        s = slice(k, k + b)
        D = a_ref[s, s]
        U, W = factor_base(jnp.where(sub >= lane, D, D.T))
        l_ref[s, s] = U.T
        w_ref[s, s] = W
        if k:
            T = dot3(l_ref[s, :k], w_ref[:k, :k], NN)
            w_ref[s, :k] = -dot3(W, T, NN)
        if k + b < n:
            L = dot3(a_ref[k + b :, s], W, NT)
            l_ref[k + b :, s] = L
            for j in range(k + b, n, b):
                off = j - k - b
                a_ref[j:, j : j + b] = a_ref[j:, j : j + b] - dot3(L[off:], L[off : off + b], NT)


def factor_first_kernel(d_ref, l_ref, w_ref, a_ref):
    a_ref[...] = d_ref[...]
    factor_whole(a_ref, l_ref, w_ref)


def factor_second_kernel(mask_ref, below_ref, d_ref, w0_ref, p_ref, l_ref, w_ref, a_ref):
    panel = dot3(below_ref[...], w0_ref[...], NT).astype(BF16)
    p_ref[...] = panel
    n = panel.shape[0]
    h = n // 2
    for i in range(2):
        for j in range(i + 1):
            r, c = slice(i * h, (i + 1) * h), slice(j * h, (j + 1) * h)
            product = dot1(panel[r], panel[c], NT)
            a_ref[r, c] = d_ref[r, c] - jnp.where(mask_ref[i * 2 + j] > 0, product, F32(0))
    factor_whole(a_ref, l_ref, w_ref)


CHOL_COST = pl.CostEstimate(flops=20_000_000_000, bytes_accessed=3 * MIB, transcendentals=1024)


def factor_first(D):
    n = D.shape[0]
    return pl.pallas_call(
        factor_first_kernel,
        out_shape=[jax.ShapeDtypeStruct((n, n), F32)] * 2,
        in_specs=[VMEM],
        out_specs=[VMEM] * 2,
        scratch_shapes=[pltpu.VMEM((n, n), F32)],
        cost_estimate=CHOL_COST,
        compiler_params=pltpu.CompilerParams(vmem_limit_bytes=40 * MIB),
    )(D)


def factor_second(mask, below, D, W0):
    n = D.shape[0]
    return pl.pallas_call(
        factor_second_kernel,
        out_shape=[jax.ShapeDtypeStruct((n, n), BF16)] + [jax.ShapeDtypeStruct((n, n), F32)] * 2,
        in_specs=[SMEM, VMEM, VMEM, VMEM],
        out_specs=[VMEM] * 3,
        scratch_shapes=[pltpu.VMEM((n, n), F32)],
        cost_estimate=CHOL_COST,
        compiler_params=pltpu.CompilerParams(vmem_limit_bytes=40 * MIB),
    )(mask, below, D, W0)


def cut_kernel(x_ref, o_ref):
    strips, _, rows, width = o_ref.shape
    for c in range(width // 128):
        tile = x_ref[pl.ds(c, strips * rows, stride=8), :]
        o_ref[:, 0, :, c * 128 : (c + 1) * 128] = tile.reshape(strips, rows, 128)


def cut_strips(front_rows, first, count, strips):
    return pl.pallas_call(
        cut_kernel,
        grid=(count,),
        out_shape=jax.ShapeDtypeStruct((strips, count, 16, 512), F32),
        in_specs=[pl.BlockSpec((2048, 128), lambda i: (i + first, 0))],
        out_specs=pl.BlockSpec((strips, 1, 16, 512), lambda i: (0, i, 0, 0)),
        cost_estimate=pl.CostEstimate(flops=0, bytes_accessed=count * 2 * MIB, transcendentals=0),
    )(front_rows)


def join_kernel(first, slot_ref, f_ref, c_ref, o_ref):
    count = o_ref.shape[0]
    for i in range(count):
        for j in range(4):
            value = f_ref[j // 2, i, :, (j % 2) * 256 : (j % 2 + 1) * 256]
            for child in range(2):
                slot = slot_ref[((i + first) * 4 + j) * 2 + child]
                piece = c_ref[jnp.maximum(slot, 0)].astype(F32)
                value = value + jnp.where(slot >= 0, piece, F32(0))
            o_ref[i, :, j * 256 : (j + 1) * 256] = value


def join_strips(slots, front_strips, child_strips, first, count):
    return pl.pallas_call(
        functools.partial(join_kernel, first),
        out_shape=jax.ShapeDtypeStruct((count, 16, 1024), F32),
        in_specs=[SMEM, VMEM, VMEM],
        out_specs=VMEM,
        cost_estimate=pl.CostEstimate(flops=0, bytes_accessed=3 * MIB, transcendentals=0),
    )(slots, front_strips, child_strips)


def solve_first_kernel(keep_ref, d_ref, r_ref, w_ref, o_ref):
    width = w_ref.shape[0]
    b = jnp.concatenate(
        [d_ref[:, :, :width].reshape(32, width), r_ref[:, :, :width].reshape(96, width)], axis=0
    )
    x = dot3(b, w_ref[...], NT).reshape(8, 16, width)
    for i in range(8):
        o_ref[i] = jnp.where(keep_ref[i] > 0, x[i], F32(0)).astype(BF16)


def solve_second_kernel(keep_ref, d_ref, r_ref, p_ref, p10_ref, w_ref, o_ref):
    width = w_ref.shape[0]
    half = width // 2
    b = jnp.concatenate(
        [d_ref[:, :, width:].reshape(32, width), r_ref[:, :, width:].reshape(96, width)], axis=0
    )
    u = dot1(p_ref[...].reshape(128, width), p10_ref[...], NT)
    rows = []
    for i in range(8):
        s = slice(16 * i, 16 * i + 16)
        parts = []
        for j in range(2):
            c = slice(j * half, (j + 1) * half)
            parts.append(b[s, c] - jnp.where(keep_ref[8 + 2 * i + j] > 0, u[s, c], F32(0)))
        rows.append(jnp.concatenate(parts, axis=1))
    x = dot3(jnp.concatenate(rows, axis=0), w_ref[...], NT).reshape(8, 16, width)
    for i in range(8):
        o_ref[i] = jnp.where(keep_ref[i] > 0, x[i], F32(0)).astype(BF16)


def solve_strips(kernel, *operands):
    return pl.pallas_call(
        kernel,
        out_shape=jax.ShapeDtypeStruct((8, 16, 512), BF16),
        in_specs=[SMEM] + [VMEM] * (len(operands) - 1),
        out_specs=VMEM,
        cost_estimate=pl.CostEstimate(flops=400_000_000, bytes_accessed=2 * MIB, transcendentals=0),
    )(*operands)


def finish_kernel(slot_ref, flag_ref, f_ref, *refs):
    child = refs[:8]
    row_refs = refs[8:10]
    col_refs = refs[10:12]
    l_ref, w_ref, o_ref = refs[12:15]
    i = pl.program_id(0)
    rows = jnp.concatenate([ref[:, 0].reshape(256, 512) for ref in row_refs], axis=1)
    for lc in range(2):
        state = flag_ref[32 + i * 2 + lc]

        @pl.when(state > 0)
        def _():
            blocks = []
            for sc in range(2):
                j = lc * 2 + sc
                cols = jnp.concatenate([ref[sc, :, lc].reshape(256, 512) for ref in col_refs], axis=1)
                value = jnp.concatenate(
                    [f_ref[pl.ds(lc * 4 + sc * 2 + c, 256, stride=8), :] for c in range(2)], axis=1
                )
                for ch in range(2):
                    live = slot_ref[(i * 4 + j) * 2 + ch] >= 0
                    value = value + jnp.where(live, child[j * 2 + ch][0].astype(F32), F32(0))
                product = dot1(rows, cols, NT)
                blocks.append(value - jnp.where(flag_ref[i * 4 + j] > 0, product, F32(0)))
            block = jnp.concatenate(blocks, axis=1)

            def put(value):
                for c in range(4):
                    o_ref[pl.ds(lc * 4 + c, 256, stride=8), :] = value[:, c * 128 : (c + 1) * 128]

            @pl.when(state == 1)
            def _():
                put(block)

            if lc == 0:

                @pl.when(state == 2)
                def _():
                    put(dot3(block, w_ref[...], NT))

                @pl.when(state == 3)
                def _():
                    put(l_ref[pl.ds(pl.multiple_of(lax.rem(i, 2) * 256, 256), 256), :])

        @pl.when(state == 0)
        def _():
            for c in range(4):
                o_ref[pl.ds(lc * 4 + c, 256, stride=8), :] = jnp.zeros((256, 128), F32)


def finish(slots, flags, front_rows, arrived, row_panels, col_panels, L, W):
    def child_spec(k):
        return pl.BlockSpec((1, 256, 256), lambda i, s, f: (jnp.maximum(s[i * 8 + k], 0), 0, 0))

    whole = lambda shape: pl.BlockSpec(shape, lambda i, s, f: (0,) * len(shape))
    return pl.pallas_call(
        finish_kernel,
        grid_spec=pltpu.PrefetchScalarGridSpec(
            num_scalar_prefetch=2,
            grid=(8,),
            in_specs=[pl.BlockSpec((2048, 128), lambda i, s, f: (i, 0))]
            + [child_spec(k) for k in range(8)]
            + [pl.BlockSpec((16, 1, 16, 512), lambda i, s, f: (0, i, 0, 0))] * 2
            + [whole((2, 16, 2, 16, 512))] * 2
            + [whole((512, 512))] * 2,
            out_specs=pl.BlockSpec((2048, 128), lambda i, s, f: (i, 0)),
        ),
        out_shape=jax.ShapeDtypeStruct(front_rows.shape, F32),
        cost_estimate=pl.CostEstimate(flops=5_000_000_000, bytes_accessed=28 * MIB, transcendentals=0),
        compiler_params=pltpu.CompilerParams(vmem_limit_bytes=48 * MIB),
    )(slots, flags, front_rows, *([arrived] * 8), *row_panels, *col_panels, L, W)


def slot_of_targets(codes, row_map, rows, cols):
    index = jnp.arange(CNB, dtype=jnp.int32)

    def place(blocks):
        hit = row_map[None] == blocks[:, None, None]
        return jnp.sum(jnp.where(hit, index + 1, 0), axis=-1) - 1

    pi, pj = place(rows), place(cols)
    child = jnp.arange(2, dtype=jnp.int32) * (CNB * CNB)
    wanted = child + pi[:, None, :] * CNB + pj[None, :, :]
    known = (pi[:, None, :] >= 0) & (pj[None, :, :] >= 0)
    wanted = jnp.where(known, wanted, -2).reshape(-1)
    number = jnp.arange(codes.shape[0], dtype=jnp.int32)
    return jnp.sum(jnp.where(wanted[:, None] == codes[None, :], number + 1, 0), axis=-1) - 1


def spread(x, axis, count):
    return lax.all_to_all(jnp.broadcast_to(x[None], (count,) + x.shape), axis, 0, 0, tiled=True)


def local(front, child_blocks, row_map, slot_table, struct_mask):
    prow, pcol = lax.axis_size("prow"), lax.axis_size("pcol")
    p, q = lax.axis_index("prow"), lax.axis_index("pcol")
    core = p % 2
    front_rows = front.reshape(16384, 128)
    child = child_blocks[0, 0]

    pair = jnp.arange(2, dtype=jnp.int32)
    row_blocks = jnp.arange(4, dtype=jnp.int32) * prow + p
    col_blocks = jnp.arange(2, dtype=jnp.int32) * pcol + q
    sub_rows = (2 * row_blocks[:, None] + pair).reshape(-1)
    sub_cols = (2 * col_blocks[:, None] + pair).reshape(-1)

    cut_child = child[:2].reshape(6, 16, 16, 256).transpose(1, 0, 2, 3)
    got_child = lax.all_to_all(cut_child, "pcol", 0, 0, tiled=True).reshape(96, 16, 256)
    cut_top = cut_strips(front_rows, 0, 2, pcol)
    got_top = lax.all_to_all(cut_top, "pcol", 0, 0, tiled=True)[:2]

    my_codes = lax.dynamic_index_in_dim(slot_table, p, 0, False)
    strip_slots = slot_of_targets(my_codes[:, :2].reshape(-1), row_map, sub_rows, jnp.arange(4, dtype=jnp.int32))
    slots = slot_of_targets(
        lax.dynamic_index_in_dim(my_codes, q, 1, False).reshape(-1), row_map, sub_rows, sub_cols
    )
    row_mask = struct_mask[sub_rows]
    lower = row_blocks[:, None] >= col_blocks[None, :]
    mask = row_mask[:, sub_cols]
    state = jnp.where(lower, 1, 0)
    owner = (q < 2) & (jnp.arange(2) == 0)
    state = jnp.where(owner[None, :] & lower, jnp.where(row_blocks[:, None] == q, 3, 2), state)
    flags = jnp.concatenate([mask.reshape(-1), jnp.repeat(state, 2, axis=0).reshape(-1)]).astype(jnp.int32)
    keep0 = (sub_rows >= 2).astype(jnp.int32)
    keep1 = jnp.concatenate([(sub_rows >= 4).astype(jnp.int32), row_mask[:, 2:4].reshape(-1)])

    top = join_strips(strip_slots, got_top, got_child, 0, 2)

    half_top = lax.all_to_all(jnp.tile(top, (prow // 2, 1, 1)), "prow", 0, 0, tiled=True)
    swap = [(i, i ^ 1) for i in range(prow)]

    def assemble(strip):
        mine = spread(strip, "pcol", pcol).reshape(256, -1)
        other = lax.ppermute(mine, "prow", swap)
        return jnp.concatenate(
            [jnp.where(core == 0, mine, other), jnp.where(core == 0, other, mine)], axis=0
        )

    D0 = assemble(half_top[0, :, :512])
    half_rest, front_rest, D0 = lax.optimization_barrier((half_top[1], front_rows, D0))
    L0, W0 = factor_first(D0)
    rest1 = assemble(half_rest)
    cut_low = cut_strips(front_rows, 2, 6, pcol)
    cut_low, rest1 = lax.optimization_barrier((cut_low, rest1))
    got_low = lax.all_to_all(cut_low, "pcol", 0, 0, tiled=True)[:2]
    child, got_low = lax.optimization_barrier((child, got_low))
    arrived = lax.all_to_all(child, "pcol", 0, 0, tiled=True).reshape(48, 256, 256)

    P10, L1, W1 = factor_second(struct_mask[2:4, 2:4].reshape(-1), rest1[:, :512], rest1[:, 512:], W0)
    low = join_strips(strip_slots, got_low, got_child, 2, 6)
    P0 = solve_strips(solve_first_kernel, keep0, top, low, W0)
    row0 = lax.all_gather(P0, "pcol")
    P1 = solve_strips(solve_second_kernel, keep1, top, low, P0, P10, W1)
    row1 = lax.all_gather(P1, "pcol")

    both = jnp.stack([P0, P1]).reshape(2, 4, 2, 16, 512).transpose(2, 0, 1, 3, 4)
    both = lax.all_to_all(jnp.tile(both, (prow // 2, 1, 1, 1, 1)), "prow", 0, 0, tiled=True)
    both = both.reshape(8, 2, 2, 2, 16, 512).transpose(3, 0, 1, 2, 4, 5).reshape(16, 2, 2, 16, 512)
    mine = lax.all_to_all(both, "pcol", 0, 0, tiled=True)
    other = lax.ppermute(mine, "prow", swap)
    ordered = jnp.stack([jnp.where(core == 0, mine, other), jnp.where(core == 0, other, mine)])

    L = jnp.where(q == 0, L0, L1)
    W = jnp.where(q == 0, W0, W1)
    out = finish(
        slots, flags, front_rows, arrived, (row0, row1), (ordered[:, :, 0], ordered[:, :, 1]), L, W
    )
    return out.reshape(front.shape)


def solution(mesh):
    in_specs = (
        P(None, "prow", None, None, "pcol", None),
        P("prow", "pcol", None, None, None, None),
        P(),
        P(),
        P(),
    )
    out_specs = P(None, "prow", None, None, "pcol", None)
    return jax.shard_map(local, mesh=mesh, in_specs=in_specs, out_specs=out_specs, check_vma=False)
```

```python
import functools

import jax
import jax.numpy as jnp
from jax import lax
from jax.experimental import pallas as pl
from jax.experimental.pallas import tpu as pltpu
from jax.sharding import PartitionSpec as P

F32 = jnp.float32
BF16 = jnp.bfloat16
CNB = 60
NN = (((1,), (0,)), ((), ()))
NT = (((1,), (1,)), ((), ()))
MIB = 2**20
VMEM = pl.BlockSpec(memory_space=pltpu.VMEM)
SMEM = pl.BlockSpec(memory_space=pltpu.SMEM)


def split(x):
    high = x.astype(BF16)
    return high, (x - high.astype(F32)).astype(BF16)


def dot1(a, b, dims):
    return lax.dot_general(a, b, dims, preferred_element_type=F32)


def dot3(a, b, dims):
    ah, al = split(a)
    bh, bl = split(b)
    return dot1(ah, bh, dims) + (dot1(al, bh, dims) + dot1(ah, bl, dims))


def factor_base(S):
    n = S.shape[0]
    wide = 2 * n // 128
    lane = lax.broadcasted_iota(jnp.int32, (n, n), 1)
    sub = lax.broadcasted_iota(jnp.int32, (n, n), 0)
    M = jnp.concatenate([S, jnp.where(lane == sub, F32(1), F32(0))], axis=1)
    row = lax.broadcasted_iota(jnp.int32, (8, 1), 0)
    across = lambda v: jnp.concatenate([v] * wide, axis=1)
    done = []
    for o in range(0, n, 8):
        R = M[0:8]
        cols = [jnp.broadcast_to(R[:, o + j : o + j + 1], (8, 128)) for j in range(8)]
        D = [[jnp.broadcast_to(cols[j][i : i + 1], (8, 128)) for j in range(i + 1)] for i in range(8)]
        Y = [jnp.broadcast_to(R[i : i + 1], (8, 2 * n)) for i in range(8)]
        low = [[None] * 8 for _ in range(8)]
        inv = [None] * 8
        for j in range(8):
            inv[j] = 1.0 / D[j][j]
            for i in range(j + 1, 8):
                low[i][j] = D[i][j] * inv[j]
            for i in range(j + 1, 8):
                for m in range(j + 1, i + 1):
                    D[i][m] = D[i][m] - low[i][j] * D[m][j]
                Y[i] = Y[i] - across(low[i][j]) * Y[j]
        out = None
        for j in range(8):
            scaled = Y[j] * across(lax.rsqrt(D[j][j]))
            out = scaled if out is None else jnp.where(row == j, scaled, out)
        done.append(out)
        if o + 8 == n:
            break
        Z = [None] * 8
        for i in range(7, -1, -1):
            Z[i] = Y[i] * across(inv[i])
            for m in range(i + 1, 8):
                Z[i] = Z[i] - across(low[m][i]) * Z[m]
        step = Z[0]
        for i in range(1, 8):
            step = jnp.where(row == i, Z[i], step)
        parts = [jnp.zeros((o, 2 * n), F32)] if o else []
        parts += [step, jnp.zeros((n - o - 8, 2 * n), F32)]
        M = M[8:] - dot3(M[8:, :n], jnp.concatenate(parts, axis=0), NN)
    done = jnp.concatenate(done, axis=0)
    return jnp.where(lane >= sub, done[:, :n], F32(0)), jnp.where(lane <= sub, done[:, n:], F32(0))


def factor_whole(a_ref, l_ref, w_ref):
    n = a_ref.shape[0]
    b = 128
    w_ref[...] = jnp.zeros((n, n), F32)
    l_ref[...] = jnp.zeros((n, n), F32)
    lane = lax.broadcasted_iota(jnp.int32, (b, b), 1)
    sub = lax.broadcasted_iota(jnp.int32, (b, b), 0)
    for k in range(0, n, b):
        s = slice(k, k + b)
        D = a_ref[s, s]
        U, W = factor_base(jnp.where(sub >= lane, D, D.T))
        l_ref[s, s] = U.T
        w_ref[s, s] = W
        if k:
            T = dot3(l_ref[s, :k], w_ref[:k, :k], NN)
            w_ref[s, :k] = -dot3(W, T, NN)
        if k + b < n:
            L = dot3(a_ref[k + b :, s], W, NT)
            l_ref[k + b :, s] = L
            for j in range(k + b, n, b):
                off = j - k - b
                a_ref[j:, j : j + b] = a_ref[j:, j : j + b] - dot3(L[off:], L[off : off + b], NT)


def place_rows(at_ref, pieces, put):
    core, x, z = at_ref[0], at_ref[1], at_ref[2]
    for ref, sub in zip(pieces, (core, 1 - core)):
        for i in range(4):
            for j in range(4):
                strip = lax.rem(x + i, 4) * 4 + lax.rem(z + j, 4)
                put(pl.ds(pl.multiple_of(sub * 256 + strip * 16, 16), 16), ref[i, j])


def factor_first_kernel(at_ref, mine_ref, other_ref, l_ref, w_ref, a_ref):
    def put(rows, value):
        a_ref[rows, :] = value

    place_rows(at_ref, (mine_ref, other_ref), put)
    factor_whole(a_ref, l_ref, w_ref)


def factor_second_kernel(at_ref, mask_ref, mine_ref, other_ref, w0_ref, p_ref, l_ref, w_ref, a_ref, b_ref):
    n = a_ref.shape[0]

    def put(rows, value):
        b_ref[rows, :] = value[:, :n]
        a_ref[rows, :] = value[:, n:]

    place_rows(at_ref, (mine_ref, other_ref), put)
    panel = dot3(b_ref[...], w0_ref[...], NT).astype(BF16)
    p_ref[...] = panel
    h = n // 2
    for i in range(2):
        for j in range(i + 1):
            r, c = slice(i * h, (i + 1) * h), slice(j * h, (j + 1) * h)
            product = dot1(panel[r], panel[c], NT)
            a_ref[r, c] = a_ref[r, c] - jnp.where(mask_ref[i * 2 + j] > 0, product, F32(0))
    factor_whole(a_ref, l_ref, w_ref)


CHOL_COST = pl.CostEstimate(flops=20_000_000_000, bytes_accessed=3 * MIB, transcendentals=1024)


def factor_first(at, mine, other):
    n = mine.shape[-1]
    return pl.pallas_call(
        factor_first_kernel,
        out_shape=[jax.ShapeDtypeStruct((n, n), F32)] * 2,
        in_specs=[SMEM, VMEM, VMEM],
        out_specs=[VMEM] * 2,
        scratch_shapes=[pltpu.VMEM((n, n), F32)],
        cost_estimate=CHOL_COST,
        compiler_params=pltpu.CompilerParams(vmem_limit_bytes=40 * MIB),
    )(at, mine, other)


def factor_second(at, mask, mine, other, W0):
    n = W0.shape[0]
    return pl.pallas_call(
        factor_second_kernel,
        out_shape=[jax.ShapeDtypeStruct((n, n), BF16)] + [jax.ShapeDtypeStruct((n, n), F32)] * 2,
        in_specs=[SMEM, SMEM, VMEM, VMEM, VMEM],
        out_specs=[VMEM] * 3,
        scratch_shapes=[pltpu.VMEM((n, n), F32)] * 2,
        cost_estimate=CHOL_COST,
        compiler_params=pltpu.CompilerParams(vmem_limit_bytes=40 * MIB),
    )(at, mask, mine, other, W0)


def cut_kernel(x_ref, o_ref):
    strips, _, rows, width = o_ref.shape
    for c in range(width // 128):
        tile = x_ref[pl.ds(c, strips * rows, stride=8), :]
        o_ref[:, 0, :, c * 128 : (c + 1) * 128] = tile.reshape(strips, rows, 128)


def cut_strips(front_rows, first, count, strips):
    return pl.pallas_call(
        cut_kernel,
        grid=(count,),
        out_shape=jax.ShapeDtypeStruct((strips, count, 16, 512), F32),
        in_specs=[pl.BlockSpec((2048, 128), lambda i: (i + first, 0))],
        out_specs=pl.BlockSpec((strips, 1, 16, 512), lambda i: (0, i, 0, 0)),
        cost_estimate=pl.CostEstimate(flops=0, bytes_accessed=count * 2 * MIB, transcendentals=0),
    )(front_rows)


def join_kernel(first, slot_ref, f_ref, c_ref, o_ref):
    count = o_ref.shape[0]
    for i in range(count):
        for j in range(4):
            value = f_ref[j // 2, i, :, (j % 2) * 256 : (j % 2 + 1) * 256]
            for child in range(2):
                slot = slot_ref[((i + first) * 4 + j) * 2 + child]
                piece = c_ref[jnp.maximum(slot, 0)].astype(F32)
                value = value + jnp.where(slot >= 0, piece, F32(0))
            o_ref[i, :, j * 256 : (j + 1) * 256] = value


def join_strips(slots, front_strips, child_strips, first, count):
    return pl.pallas_call(
        functools.partial(join_kernel, first),
        out_shape=jax.ShapeDtypeStruct((count, 16, 1024), F32),
        in_specs=[SMEM, VMEM, VMEM],
        out_specs=VMEM,
        cost_estimate=pl.CostEstimate(flops=0, bytes_accessed=3 * MIB, transcendentals=0),
    )(slots, front_strips, child_strips)


def solve_first_kernel(keep_ref, d_ref, r_ref, w_ref, o_ref):
    width = w_ref.shape[0]
    b = jnp.concatenate(
        [d_ref[:, :, :width].reshape(32, width), r_ref[:, :, :width].reshape(96, width)], axis=0
    )
    x = dot3(b, w_ref[...], NT).reshape(8, 16, width)
    for i in range(8):
        o_ref[i] = jnp.where(keep_ref[i] > 0, x[i], F32(0)).astype(BF16)


def solve_second_kernel(keep_ref, d_ref, r_ref, p_ref, p10_ref, w_ref, o_ref):
    width = w_ref.shape[0]
    half = width // 2
    b = jnp.concatenate(
        [d_ref[:, :, width:].reshape(32, width), r_ref[:, :, width:].reshape(96, width)], axis=0
    )
    u = dot1(p_ref[...].reshape(128, width), p10_ref[...], NT)
    rows = []
    for i in range(8):
        s = slice(16 * i, 16 * i + 16)
        parts = []
        for j in range(2):
            c = slice(j * half, (j + 1) * half)
            parts.append(b[s, c] - jnp.where(keep_ref[8 + 2 * i + j] > 0, u[s, c], F32(0)))
        rows.append(jnp.concatenate(parts, axis=1))
    x = dot3(jnp.concatenate(rows, axis=0), w_ref[...], NT).reshape(8, 16, width)
    for i in range(8):
        o_ref[i] = jnp.where(keep_ref[i] > 0, x[i], F32(0)).astype(BF16)


def solve_strips(kernel, *operands):
    return pl.pallas_call(
        kernel,
        out_shape=jax.ShapeDtypeStruct((8, 16, 512), BF16),
        in_specs=[SMEM] + [VMEM] * (len(operands) - 1),
        out_specs=VMEM,
        cost_estimate=pl.CostEstimate(flops=400_000_000, bytes_accessed=2 * MIB, transcendentals=0),
    )(*operands)


def deal_kernel(y_ref, *refs):
    o_ref = refs[-1]
    for panel in range(2):
        for k in range(4):
            row = lax.rem(y_ref[0] + k, 4) * 2
            for c in range(2):
                for lr in range(4):
                    o_ref[(lr % 2) * 8 + row + c, panel, lr // 2] = refs[panel * 4 + k][c, lr]


def deal(y, first, second):
    return pl.pallas_call(
        deal_kernel,
        out_shape=jax.ShapeDtypeStruct((16, 2, 2, 16, 512), BF16),
        in_specs=[SMEM] + [VMEM] * 8,
        out_specs=VMEM,
        cost_estimate=pl.CostEstimate(flops=0, bytes_accessed=4 * MIB, transcendentals=0),
    )(y, *first, *second)


def finish_kernel(slot_ref, flag_ref, f_ref, *refs):
    child = refs[:8]
    row_refs = refs[8:10]
    col_refs = refs[10:12]
    l_ref, w_ref, o_ref = refs[12:15]
    i = pl.program_id(0)
    rows = jnp.concatenate([ref[:, 0].reshape(256, 512) for ref in row_refs], axis=1)
    for lc in range(2):
        state = flag_ref[32 + i * 2 + lc]

        @pl.when(state > 0)
        def _():
            blocks = []
            for sc in range(2):
                j = lc * 2 + sc
                cols = jnp.concatenate([ref[sc, :, lc].reshape(256, 512) for ref in col_refs], axis=1)
                value = jnp.concatenate(
                    [f_ref[pl.ds(lc * 4 + sc * 2 + c, 256, stride=8), :] for c in range(2)], axis=1
                )
                for ch in range(2):
                    live = slot_ref[(i * 4 + j) * 2 + ch] >= 0
                    value = value + jnp.where(live, child[j * 2 + ch][0].astype(F32), F32(0))
                product = dot1(rows, cols, NT)
                blocks.append(value - jnp.where(flag_ref[i * 4 + j] > 0, product, F32(0)))
            block = jnp.concatenate(blocks, axis=1)

            def put(value):
                for c in range(4):
                    o_ref[pl.ds(lc * 4 + c, 256, stride=8), :] = value[:, c * 128 : (c + 1) * 128]

            @pl.when(state == 1)
            def _():
                put(block)

            if lc == 0:

                @pl.when(state == 2)
                def _():
                    put(dot3(block, w_ref[...], NT))

                @pl.when(state == 3)
                def _():
                    put(l_ref[pl.ds(pl.multiple_of(lax.rem(i, 2) * 256, 256), 256), :])

        @pl.when(state == 0)
        def _():
            for c in range(4):
                o_ref[pl.ds(lc * 4 + c, 256, stride=8), :] = jnp.zeros((256, 128), F32)


def finish(slots, flags, front_rows, arrived, row_panels, col_panels, L, W):
    def child_spec(k):
        return pl.BlockSpec((1, 256, 256), lambda i, s, f: (jnp.maximum(s[i * 8 + k], 0), 0, 0))

    whole = lambda shape: pl.BlockSpec(shape, lambda i, s, f: (0,) * len(shape))
    return pl.pallas_call(
        finish_kernel,
        grid_spec=pltpu.PrefetchScalarGridSpec(
            num_scalar_prefetch=2,
            grid=(8,),
            in_specs=[pl.BlockSpec((2048, 128), lambda i, s, f: (i, 0))]
            + [child_spec(k) for k in range(8)]
            + [pl.BlockSpec((16, 1, 16, 512), lambda i, s, f: (0, i, 0, 0))] * 2
            + [whole((2, 16, 2, 16, 512))] * 2
            + [whole((512, 512))] * 2,
            out_specs=pl.BlockSpec((2048, 128), lambda i, s, f: (i, 0)),
        ),
        out_shape=jax.ShapeDtypeStruct(front_rows.shape, F32),
        cost_estimate=pl.CostEstimate(flops=5_000_000_000, bytes_accessed=28 * MIB, transcendentals=0),
        compiler_params=pltpu.CompilerParams(vmem_limit_bytes=48 * MIB),
    )(slots, flags, front_rows, *([arrived] * 8), *row_panels, *col_panels, L, W)


def slot_of_targets(codes, row_map, rows, cols):
    index = jnp.arange(CNB, dtype=jnp.int32)

    def place(blocks):
        hit = row_map[None] == blocks[:, None, None]
        return jnp.sum(jnp.where(hit, index + 1, 0), axis=-1) - 1

    pi, pj = place(rows), place(cols)
    child = jnp.arange(2, dtype=jnp.int32) * (CNB * CNB)
    wanted = child + pi[:, None, :] * CNB + pj[None, :, :]
    known = (pi[:, None, :] >= 0) & (pj[None, :, :] >= 0)
    wanted = jnp.where(known, wanted, -2).reshape(-1)
    number = jnp.arange(codes.shape[0], dtype=jnp.int32)
    return jnp.sum(jnp.where(wanted[:, None] == codes[None, :], number + 1, 0), axis=-1) - 1


def local(front, child_blocks, row_map, slot_table, struct_mask):
    prow, pcol = lax.axis_size("prow"), lax.axis_size("pcol")
    p, q = lax.axis_index("prow"), lax.axis_index("pcol")
    core = p % 2
    front_rows = front.reshape(16384, 128)
    child = child_blocks[0, 0]

    pair = jnp.arange(2, dtype=jnp.int32)
    row_blocks = jnp.arange(4, dtype=jnp.int32) * prow + p
    col_blocks = jnp.arange(2, dtype=jnp.int32) * pcol + q
    sub_rows = (2 * row_blocks[:, None] + pair).reshape(-1)
    sub_cols = (2 * col_blocks[:, None] + pair).reshape(-1)

    cut_child = child[:2].reshape(6, 16, 16, 256).transpose(1, 0, 2, 3)
    got_child = lax.all_to_all(cut_child, "pcol", 0, 0, tiled=True).reshape(96, 16, 256)
    cut_top = cut_strips(front_rows, 0, 2, pcol)
    got_top = lax.all_to_all(cut_top, "pcol", 0, 0, tiled=True)[:2]

    my_codes = lax.dynamic_index_in_dim(slot_table, p, 0, False)
    strip_slots = slot_of_targets(my_codes[:, :2].reshape(-1), row_map, sub_rows, jnp.arange(4, dtype=jnp.int32))
    slots = slot_of_targets(
        lax.dynamic_index_in_dim(my_codes, q, 1, False).reshape(-1), row_map, sub_rows, sub_cols
    )
    row_mask = struct_mask[sub_rows]
    lower = row_blocks[:, None] >= col_blocks[None, :]
    mask = row_mask[:, sub_cols]
    state = jnp.where(lower, 1, 0)
    owner = (q < 2) & (jnp.arange(2) == 0)
    state = jnp.where(owner[None, :] & lower, jnp.where(row_blocks[:, None] == q, 3, 2), state)
    flags = jnp.concatenate([mask.reshape(-1), jnp.repeat(state, 2, axis=0).reshape(-1)]).astype(jnp.int32)
    keep0 = (sub_rows >= 2).astype(jnp.int32)
    keep1 = jnp.concatenate([(sub_rows >= 4).astype(jnp.int32), row_mask[:, 2:4].reshape(-1)])

    top = join_strips(strip_slots, got_top, got_child, 0, 2)

    y, x, z = p // 2, q // 4, q % 4
    at = jnp.stack([core, x, z]).astype(jnp.int32)
    swap = [(i, i ^ 1) for i in range(8)]
    along_y = lambda k: [(2 * ((i + k) % 4) + c, 2 * i + c) for i in range(4) for c in range(2)]
    along_x = lambda k: [(4 * ((i + k) % 4) + j, 4 * i + j) for i in range(4) for j in range(4)]
    along_z = lambda k: [(4 * j + (i + k) % 4, 4 * j + i) for i in range(4) for j in range(4)]
    got = lax.ppermute(jnp.where(core == 0, top[1], top[0]), "prow", swap)
    kept = jnp.where(core == 0, top[0], top[1])
    first = jnp.where(core == 0, kept, got)[:, :512]
    rest = jnp.where(core == 0, got, kept)
    both = jnp.concatenate([first, rest], axis=1)
    sent = [lax.ppermute(both, "prow", [(c, 2 * k + c) for c in range(2)]) for k in range(1, 4)]
    both = jnp.where(y == 0, both, sent[0] + sent[1] + sent[2])

    def assemble(strip):
        ring = jnp.stack([strip] + [lax.ppermute(strip, "pcol", along_z(k)) for k in range(1, 4)])
        mine = jnp.stack([ring] + [lax.ppermute(ring, "pcol", along_x(k)) for k in range(1, 4)])
        return mine, lax.ppermute(mine, "prow", swap)

    def gather_columns(strips):
        halves = strips.reshape(4, 2, 16, 512)
        even, odd = halves[:, 0], halves[:, 1]
        got = lax.ppermute(jnp.where(core == 0, odd, even), "prow", swap)
        kept = jnp.where(core == 0, even, odd)
        chip = jnp.where(core == 0, jnp.stack([kept, got]), jnp.stack([got, kept]))
        return [chip] + [lax.ppermute(chip, "prow", along_y(k)) for k in range(1, 4)]

    top0 = assemble(both[:, :512])
    top1 = assemble(both[:, 512:])

    cut_low = cut_strips(front_rows, 2, 6, pcol)
    cut_low, top = lax.optimization_barrier((cut_low, top))
    got_low = lax.all_to_all(cut_low, "pcol", 0, 0, tiled=True)[:2]
    child, got_low = lax.optimization_barrier((child, got_low))
    arrived = lax.all_to_all(child, "pcol", 0, 0, tiled=True).reshape(48, 256, 256)

    L0, W0 = factor_first(at, *top0)
    low = join_strips(strip_slots, got_low, got_child, 2, 6)
    P0 = solve_strips(solve_first_kernel, keep0, top, low, W0)
    row0 = lax.all_gather(P0, "pcol")
    P0, top1 = lax.optimization_barrier((P0, top1))
    cols0 = gather_columns(P0)
    P10, L1, W1 = factor_second(at, struct_mask[2:4, 2:4].reshape(-1), *top1, W0)
    P1 = solve_strips(solve_second_kernel, keep1, top, low, P0, P10, W1)
    row1 = lax.all_gather(P1, "pcol")
    cols1 = gather_columns(P1)

    dealt = deal(y.reshape(1).astype(jnp.int32), cols0, cols1)
    dealt, arrived = lax.optimization_barrier((dealt, arrived))
    mine = lax.all_to_all(dealt, "pcol", 0, 0, tiled=True)
    other = lax.ppermute(mine, "prow", swap)
    ordered = jnp.stack([jnp.where(core == 0, mine, other), jnp.where(core == 0, other, mine)])

    L = jnp.where(q == 0, L0, L1)
    W = jnp.where(q == 0, W0, W1)
    out = finish(
        slots, flags, front_rows, arrived, (row0, row1), (ordered[:, :, 0], ordered[:, :, 1]), L, W
    )
    return out.reshape(front.shape)


def solution(mesh):
    in_specs = (
        P(None, "prow", None, None, "pcol", None),
        P("prow", "pcol", None, None, None, None),
        P(),
        P(),
        P(),
    )
    out_specs = P(None, "prow", None, None, "pcol", None)
    return jax.shard_map(local, mesh=mesh, in_specs=in_specs, out_specs=out_specs, check_vma=False)
```

```python
import functools

import jax
import jax.numpy as jnp
from jax import lax
from jax.experimental import pallas as pl
from jax.experimental.pallas import tpu as pltpu
from jax.sharding import PartitionSpec as P

F32 = jnp.float32
BF16 = jnp.bfloat16
CNB = 60
NN = (((1,), (0,)), ((), ()))
NT = (((1,), (1,)), ((), ()))
MIB = 2**20
VMEM = pl.BlockSpec(memory_space=pltpu.VMEM)
SMEM = pl.BlockSpec(memory_space=pltpu.SMEM)


def split(x):
    high = x.astype(BF16)
    return high, (x - high.astype(F32)).astype(BF16)


def dot1(a, b, dims):
    return lax.dot_general(a, b, dims, preferred_element_type=F32)


def dot3(a, b, dims):
    ah, al = split(a)
    bh, bl = split(b)
    return dot1(ah, bh, dims) + (dot1(al, bh, dims) + dot1(ah, bl, dims))


def factor_base(S):
    n = S.shape[0]
    wide = 2 * n // 128
    lane = lax.broadcasted_iota(jnp.int32, (n, n), 1)
    sub = lax.broadcasted_iota(jnp.int32, (n, n), 0)
    M = jnp.concatenate([S, jnp.where(lane == sub, F32(1), F32(0))], axis=1)
    row = lax.broadcasted_iota(jnp.int32, (8, 1), 0)
    across = lambda v: jnp.concatenate([v] * wide, axis=1)
    done = []
    for o in range(0, n, 8):
        R = M[0:8]
        cols = [jnp.broadcast_to(R[:, o + j : o + j + 1], (8, 128)) for j in range(8)]
        D = [[jnp.broadcast_to(cols[j][i : i + 1], (8, 128)) for j in range(i + 1)] for i in range(8)]
        Y = [jnp.broadcast_to(R[i : i + 1], (8, 2 * n)) for i in range(8)]
        low = [[None] * 8 for _ in range(8)]
        inv = [None] * 8
        for j in range(8):
            inv[j] = 1.0 / D[j][j]
            for i in range(j + 1, 8):
                low[i][j] = D[i][j] * inv[j]
            for i in range(j + 1, 8):
                for m in range(j + 1, i + 1):
                    D[i][m] = D[i][m] - low[i][j] * D[m][j]
                Y[i] = Y[i] - across(low[i][j]) * Y[j]
        out = None
        for j in range(8):
            scaled = Y[j] * across(lax.rsqrt(D[j][j]))
            out = scaled if out is None else jnp.where(row == j, scaled, out)
        done.append(out)
        if o + 8 == n:
            break
        Z = [None] * 8
        for i in range(7, -1, -1):
            Z[i] = Y[i] * across(inv[i])
            for m in range(i + 1, 8):
                Z[i] = Z[i] - across(low[m][i]) * Z[m]
        step = Z[0]
        for i in range(1, 8):
            step = jnp.where(row == i, Z[i], step)
        parts = [jnp.zeros((o, 2 * n), F32)] if o else []
        parts += [step, jnp.zeros((n - o - 8, 2 * n), F32)]
        M = M[8:] - dot3(M[8:, :n], jnp.concatenate(parts, axis=0), NN)
    done = jnp.concatenate(done, axis=0)
    return jnp.where(lane >= sub, done[:, :n], F32(0)), jnp.where(lane <= sub, done[:, n:], F32(0))


def factor_whole(a_ref, l_ref, w_ref):
    n = a_ref.shape[0]
    b = 128
    w_ref[...] = jnp.zeros((n, n), F32)
    l_ref[...] = jnp.zeros((n, n), F32)
    lane = lax.broadcasted_iota(jnp.int32, (b, b), 1)
    sub = lax.broadcasted_iota(jnp.int32, (b, b), 0)
    for k in range(0, n, b):
        s = slice(k, k + b)
        D = a_ref[s, s]
        U, W = factor_base(jnp.where(sub >= lane, D, D.T))
        l_ref[s, s] = U.T
        w_ref[s, s] = W
        if k:
            T = dot3(l_ref[s, :k], w_ref[:k, :k], NN)
            w_ref[s, :k] = -dot3(W, T, NN)
        if k + b < n:
            L = dot3(a_ref[k + b :, s], W, NT)
            l_ref[k + b :, s] = L
            for j in range(k + b, n, b):
                off = j - k - b
                a_ref[j:, j : j + b] = a_ref[j:, j : j + b] - dot3(L[off:], L[off : off + b], NT)


def place_rows(at_ref, pieces, put):
    core, x, z = at_ref[0], at_ref[1], at_ref[2]
    for ref, sub in zip(pieces, (core, 1 - core)):
        for i in range(4):
            for j in range(4):
                strip = lax.rem(x + i, 4) * 4 + lax.rem(z + j, 4)
                put(pl.ds(pl.multiple_of(sub * 256 + strip * 16, 16), 16), ref[i, j])


def factor_first_kernel(at_ref, mine_ref, other_ref, l_ref, w_ref, a_ref):
    n = a_ref.shape[0]

    def put(rows, value):
        a_ref[rows, :] = value[:, :n]

    place_rows(at_ref, (mine_ref, other_ref), put)
    factor_whole(a_ref, l_ref, w_ref)


def factor_second_kernel(at_ref, mask_ref, mine_ref, other_ref, w0_ref, p_ref, l_ref, w_ref, a_ref, b_ref):
    n = a_ref.shape[0]

    def put(rows, value):
        b_ref[rows, :] = value[:, n : 2 * n]
        a_ref[rows, :] = value[:, 2 * n :]

    place_rows(at_ref, (mine_ref, other_ref), put)
    panel = dot3(b_ref[...], w0_ref[...], NT).astype(BF16)
    p_ref[...] = panel
    h = n // 2
    for i in range(2):
        for j in range(i + 1):
            r, c = slice(i * h, (i + 1) * h), slice(j * h, (j + 1) * h)
            product = dot1(panel[r], panel[c], NT)
            a_ref[r, c] = a_ref[r, c] - jnp.where(mask_ref[i * 2 + j] > 0, product, F32(0))
    factor_whole(a_ref, l_ref, w_ref)


CHOL_COST = pl.CostEstimate(flops=20_000_000_000, bytes_accessed=3 * MIB, transcendentals=1024)


def factor_first(at, mine, other):
    n = mine.shape[-1] // 3
    return pl.pallas_call(
        factor_first_kernel,
        out_shape=[jax.ShapeDtypeStruct((n, n), F32)] * 2,
        in_specs=[SMEM, VMEM, VMEM],
        out_specs=[VMEM] * 2,
        scratch_shapes=[pltpu.VMEM((n, n), F32)],
        cost_estimate=CHOL_COST,
        compiler_params=pltpu.CompilerParams(vmem_limit_bytes=40 * MIB),
    )(at, mine, other)


def factor_second(at, mask, mine, other, W0):
    n = W0.shape[0]
    return pl.pallas_call(
        factor_second_kernel,
        out_shape=[jax.ShapeDtypeStruct((n, n), BF16)] + [jax.ShapeDtypeStruct((n, n), F32)] * 2,
        in_specs=[SMEM, SMEM, VMEM, VMEM, VMEM],
        out_specs=[VMEM] * 3,
        scratch_shapes=[pltpu.VMEM((n, n), F32)] * 2,
        cost_estimate=CHOL_COST,
        compiler_params=pltpu.CompilerParams(vmem_limit_bytes=40 * MIB),
    )(at, mask, mine, other, W0)


def cut_kernel(x_ref, o_ref):
    strips, _, rows, width = o_ref.shape
    for c in range(width // 128):
        tile = x_ref[pl.ds(c, strips * rows, stride=8), :]
        o_ref[:, 0, :, c * 128 : (c + 1) * 128] = tile.reshape(strips, rows, 128)


def cut_strips(front_rows, first, count, strips):
    return pl.pallas_call(
        cut_kernel,
        grid=(count,),
        out_shape=jax.ShapeDtypeStruct((strips, count, 16, 512), F32),
        in_specs=[pl.BlockSpec((2048, 128), lambda i: (i + first, 0))],
        out_specs=pl.BlockSpec((strips, 1, 16, 512), lambda i: (0, i, 0, 0)),
        cost_estimate=pl.CostEstimate(flops=0, bytes_accessed=count * 2 * MIB, transcendentals=0),
    )(front_rows)


def join_kernel(first, slot_ref, f_ref, c_ref, o_ref):
    count = o_ref.shape[0]
    for i in range(count):
        for j in range(4):
            value = f_ref[j // 2, i, :, (j % 2) * 256 : (j % 2 + 1) * 256]
            for child in range(2):
                slot = slot_ref[((i + first) * 4 + j) * 2 + child]
                piece = c_ref[jnp.maximum(slot, 0)].astype(F32)
                value = value + jnp.where(slot >= 0, piece, F32(0))
            o_ref[i, :, j * 256 : (j + 1) * 256] = value


def join_strips(slots, front_strips, child_strips, first, count):
    return pl.pallas_call(
        functools.partial(join_kernel, first),
        out_shape=jax.ShapeDtypeStruct((count, 16, 1024), F32),
        in_specs=[SMEM, VMEM, VMEM],
        out_specs=VMEM,
        cost_estimate=pl.CostEstimate(flops=0, bytes_accessed=3 * MIB, transcendentals=0),
    )(slots, front_strips, child_strips)


def solve_first_kernel(keep_ref, d_ref, r_ref, w_ref, o_ref):
    width = w_ref.shape[0]
    b = jnp.concatenate(
        [d_ref[:, :, :width].reshape(32, width), r_ref[:, :, :width].reshape(96, width)], axis=0
    )
    x = dot3(b, w_ref[...], NT).reshape(8, 16, width)
    for i in range(8):
        o_ref[i] = jnp.where(keep_ref[i] > 0, x[i], F32(0)).astype(BF16)


def solve_second_kernel(keep_ref, d_ref, r_ref, p_ref, p10_ref, w_ref, o_ref):
    width = w_ref.shape[0]
    half = width // 2
    b = jnp.concatenate(
        [d_ref[:, :, width:].reshape(32, width), r_ref[:, :, width:].reshape(96, width)], axis=0
    )
    u = dot1(p_ref[...].reshape(128, width), p10_ref[...], NT)
    rows = []
    for i in range(8):
        s = slice(16 * i, 16 * i + 16)
        parts = []
        for j in range(2):
            c = slice(j * half, (j + 1) * half)
            parts.append(b[s, c] - jnp.where(keep_ref[8 + 2 * i + j] > 0, u[s, c], F32(0)))
        rows.append(jnp.concatenate(parts, axis=1))
    x = dot3(jnp.concatenate(rows, axis=0), w_ref[...], NT).reshape(8, 16, width)
    for i in range(8):
        o_ref[i] = jnp.where(keep_ref[i] > 0, x[i], F32(0)).astype(BF16)


def solve_strips(kernel, *operands):
    return pl.pallas_call(
        kernel,
        out_shape=jax.ShapeDtypeStruct((8, 16, 512), BF16),
        in_specs=[SMEM] + [VMEM] * (len(operands) - 1),
        out_specs=VMEM,
        cost_estimate=pl.CostEstimate(flops=400_000_000, bytes_accessed=2 * MIB, transcendentals=0),
    )(*operands)


def deal_kernel(y_ref, *refs):
    o_ref = refs[-1]
    for panel in range(2):
        for k in range(4):
            row = lax.rem(y_ref[0] + k, 4) * 2
            for c in range(2):
                for lr in range(4):
                    o_ref[(lr % 2) * 8 + row + c, panel, lr // 2] = refs[panel * 4 + k][c, lr]


def deal(y, first, second):
    return pl.pallas_call(
        deal_kernel,
        out_shape=jax.ShapeDtypeStruct((16, 2, 2, 16, 512), BF16),
        in_specs=[SMEM] + [VMEM] * 8,
        out_specs=VMEM,
        cost_estimate=pl.CostEstimate(flops=0, bytes_accessed=4 * MIB, transcendentals=0),
    )(y, *first, *second)


def finish_kernel(slot_ref, flag_ref, f_ref, *refs):
    child = refs[:8]
    row_refs = refs[8:10]
    col_refs = refs[10:12]
    l_ref, w_ref, o_ref = refs[12:15]
    i = pl.program_id(0)
    rows = jnp.concatenate([ref[:, 0].reshape(256, 512) for ref in row_refs], axis=1)
    for lc in range(2):
        state = flag_ref[32 + i * 2 + lc]

        @pl.when(state > 0)
        def _():
            blocks = []
            for sc in range(2):
                j = lc * 2 + sc
                cols = jnp.concatenate([ref[sc, :, lc].reshape(256, 512) for ref in col_refs], axis=1)
                value = jnp.concatenate(
                    [f_ref[pl.ds(lc * 4 + sc * 2 + c, 256, stride=8), :] for c in range(2)], axis=1
                )
                for ch in range(2):
                    live = slot_ref[(i * 4 + j) * 2 + ch] >= 0
                    value = value + jnp.where(live, child[j * 2 + ch][0].astype(F32), F32(0))
                product = dot1(rows, cols, NT)
                blocks.append(value - jnp.where(flag_ref[i * 4 + j] > 0, product, F32(0)))
            block = jnp.concatenate(blocks, axis=1)

            def put(value):
                for c in range(4):
                    o_ref[pl.ds(lc * 4 + c, 256, stride=8), :] = value[:, c * 128 : (c + 1) * 128]

            @pl.when(state == 1)
            def _():
                put(block)

            if lc == 0:

                @pl.when(state == 2)
                def _():
                    put(dot3(block, w_ref[...], NT))

                @pl.when(state == 3)
                def _():
                    put(l_ref[pl.ds(pl.multiple_of(lax.rem(i, 2) * 256, 256), 256), :])

        @pl.when(state == 0)
        def _():
            for c in range(4):
                o_ref[pl.ds(lc * 4 + c, 256, stride=8), :] = jnp.zeros((256, 128), F32)


def finish(slots, flags, front_rows, arrived, row_panels, col_panels, L, W):
    def child_spec(k):
        return pl.BlockSpec((1, 256, 256), lambda i, s, f: (jnp.maximum(s[i * 8 + k], 0), 0, 0))

    whole = lambda shape: pl.BlockSpec(shape, lambda i, s, f: (0,) * len(shape))
    return pl.pallas_call(
        finish_kernel,
        grid_spec=pltpu.PrefetchScalarGridSpec(
            num_scalar_prefetch=2,
            grid=(8,),
            in_specs=[pl.BlockSpec((2048, 128), lambda i, s, f: (i, 0))]
            + [child_spec(k) for k in range(8)]
            + [pl.BlockSpec((16, 1, 16, 512), lambda i, s, f: (0, i, 0, 0))] * 2
            + [whole((2, 16, 2, 16, 512))] * 2
            + [whole((512, 512))] * 2,
            out_specs=pl.BlockSpec((2048, 128), lambda i, s, f: (i, 0)),
        ),
        out_shape=jax.ShapeDtypeStruct(front_rows.shape, F32),
        cost_estimate=pl.CostEstimate(flops=5_000_000_000, bytes_accessed=28 * MIB, transcendentals=0),
        compiler_params=pltpu.CompilerParams(vmem_limit_bytes=48 * MIB),
    )(slots, flags, front_rows, *([arrived] * 8), *row_panels, *col_panels, L, W)


def slot_of_targets(codes, row_map, rows, cols):
    index = jnp.arange(CNB, dtype=jnp.int32)

    def place(blocks):
        hit = row_map[None] == blocks[:, None, None]
        return jnp.sum(jnp.where(hit, index + 1, 0), axis=-1) - 1

    pi, pj = place(rows), place(cols)
    child = jnp.arange(2, dtype=jnp.int32) * (CNB * CNB)
    wanted = child + pi[:, None, :] * CNB + pj[None, :, :]
    known = (pi[:, None, :] >= 0) & (pj[None, :, :] >= 0)
    wanted = jnp.where(known, wanted, -2).reshape(-1)
    number = jnp.arange(codes.shape[0], dtype=jnp.int32)
    return jnp.sum(jnp.where(wanted[:, None] == codes[None, :], number + 1, 0), axis=-1) - 1


def local(front, child_blocks, row_map, slot_table, struct_mask):
    prow, pcol = lax.axis_size("prow"), lax.axis_size("pcol")
    p, q = lax.axis_index("prow"), lax.axis_index("pcol")
    core = p % 2
    front_rows = front.reshape(16384, 128)
    child = child_blocks[0, 0]

    pair = jnp.arange(2, dtype=jnp.int32)
    row_blocks = jnp.arange(4, dtype=jnp.int32) * prow + p
    col_blocks = jnp.arange(2, dtype=jnp.int32) * pcol + q
    sub_rows = (2 * row_blocks[:, None] + pair).reshape(-1)
    sub_cols = (2 * col_blocks[:, None] + pair).reshape(-1)

    cut_child = child[:2].reshape(6, 16, 16, 256).transpose(1, 0, 2, 3)
    got_child = lax.all_to_all(cut_child, "pcol", 0, 0, tiled=True).reshape(96, 16, 256)
    cut = cut_strips(front_rows, 0, 8, pcol)
    from_first = jnp.where(q == 0, cut[0], F32(0))
    from_second = jnp.where(q == 1, cut[1], F32(0))
    for k in range(1, 16):
        after = (k + 1) % 16
        piece = lax.dynamic_index_in_dim(cut, jnp.where(q == 0, k, after), 0, False)
        piece = lax.ppermute(piece, "pcol", [(0, k), (1, after)])
        from_first = from_first + jnp.where(q == k, piece, F32(0))
        from_second = from_second + jnp.where(q == after, piece, F32(0))
    fronts = jnp.stack([from_first, from_second])

    my_codes = lax.dynamic_index_in_dim(slot_table, p, 0, False)
    strip_slots = slot_of_targets(my_codes[:, :2].reshape(-1), row_map, sub_rows, jnp.arange(4, dtype=jnp.int32))
    slots = slot_of_targets(
        lax.dynamic_index_in_dim(my_codes, q, 1, False).reshape(-1), row_map, sub_rows, sub_cols
    )
    row_mask = struct_mask[sub_rows]
    lower = row_blocks[:, None] >= col_blocks[None, :]
    mask = row_mask[:, sub_cols]
    state = jnp.where(lower, 1, 0)
    owner = (q < 2) & (jnp.arange(2) == 0)
    state = jnp.where(owner[None, :] & lower, jnp.where(row_blocks[:, None] == q, 3, 2), state)
    flags = jnp.concatenate([mask.reshape(-1), jnp.repeat(state, 2, axis=0).reshape(-1)]).astype(jnp.int32)
    keep0 = (sub_rows >= 2).astype(jnp.int32)
    keep1 = jnp.concatenate([(sub_rows >= 4).astype(jnp.int32), row_mask[:, 2:4].reshape(-1)])

    top = join_strips(strip_slots, fronts[:, :2], got_child, 0, 2)
    low = join_strips(strip_slots, fronts[:, 2:], got_child, 2, 6)

    y, x, z = p // 2, q // 4, q % 4
    at = jnp.stack([core, x, z]).astype(jnp.int32)
    swap = [(i, i ^ 1) for i in range(8)]
    along_y = lambda k: [(2 * ((i + k) % 4) + c, 2 * i + c) for i in range(4) for c in range(2)]
    along_x = lambda k: [(4 * ((i + k) % 4) + j, 4 * i + j) for i in range(4) for j in range(4)]
    along_z = lambda k: [(4 * j + (i + k) % 4, 4 * j + i) for i in range(4) for j in range(4)]
    got = lax.ppermute(jnp.where(core == 0, top[1], top[0]), "prow", swap)
    kept = jnp.where(core == 0, top[0], top[1])
    first = jnp.where(core == 0, kept, got)[:, :512]
    rest = jnp.where(core == 0, got, kept)
    both = jnp.concatenate([first, rest], axis=1)
    sent = [lax.ppermute(both, "prow", [(c, 2 * k + c) for c in range(2)]) for k in range(1, 4)]
    both = jnp.where(y == 0, both, sent[0] + sent[1] + sent[2])

    def assemble(strip):
        ring = jnp.stack([strip] + [lax.ppermute(strip, "pcol", along_z(k)) for k in range(1, 4)])
        mine = jnp.stack([ring] + [lax.ppermute(ring, "pcol", along_x(k)) for k in range(1, 4)])
        return mine, lax.ppermute(mine, "prow", swap)

    def gather_columns(strips):
        halves = strips.reshape(4, 2, 16, 512)
        even, odd = halves[:, 0], halves[:, 1]
        got = lax.ppermute(jnp.where(core == 0, odd, even), "prow", swap)
        kept = jnp.where(core == 0, even, odd)
        chip = jnp.where(core == 0, jnp.stack([kept, got]), jnp.stack([got, kept]))
        return [chip] + [lax.ppermute(chip, "prow", along_y(k)) for k in range(1, 4)]

    diag = assemble(both)
    child, diag = lax.optimization_barrier((child, diag))
    arrived = lax.all_to_all(child, "pcol", 0, 0, tiled=True).reshape(48, 256, 256)

    L0, W0 = factor_first(at, *diag)
    P0 = solve_strips(solve_first_kernel, keep0, top, low, W0)
    row0 = lax.all_gather(P0, "pcol")
    P0, diag = lax.optimization_barrier((P0, diag))
    cols0 = gather_columns(P0)
    P10, L1, W1 = factor_second(at, struct_mask[2:4, 2:4].reshape(-1), *diag, W0)
    P1 = solve_strips(solve_second_kernel, keep1, top, low, P0, P10, W1)
    row1 = lax.all_gather(P1, "pcol")
    cols1 = gather_columns(P1)

    dealt = deal(y.reshape(1).astype(jnp.int32), cols0, cols1)
    dealt, arrived = lax.optimization_barrier((dealt, arrived))
    mine = lax.all_to_all(dealt, "pcol", 0, 0, tiled=True)
    other = lax.ppermute(mine, "prow", swap)
    ordered = jnp.stack([jnp.where(core == 0, mine, other), jnp.where(core == 0, other, mine)])

    L = jnp.where(q == 0, L0, L1)
    W = jnp.where(q == 0, W0, W1)
    out = finish(
        slots, flags, front_rows, arrived, (row0, row1), (ordered[:, :, 0], ordered[:, :, 1]), L, W
    )
    return out.reshape(front.shape)


def solution(mesh):
    in_specs = (
        P(None, "prow", None, None, "pcol", None),
        P("prow", "pcol", None, None, None, None),
        P(),
        P(),
        P(),
    )
    out_specs = P(None, "prow", None, None, "pcol", None)
    return jax.shard_map(local, mesh=mesh, in_specs=in_specs, out_specs=out_specs, check_vma=False)
```

```python
import functools

import jax
import jax.numpy as jnp
from jax import lax
from jax.experimental import pallas as pl
from jax.experimental.pallas import tpu as pltpu
from jax.sharding import PartitionSpec as P

F32 = jnp.float32
BF16 = jnp.bfloat16
CNB = 60
NN = (((1,), (0,)), ((), ()))
NT = (((1,), (1,)), ((), ()))
MIB = 2**20
VMEM = pl.BlockSpec(memory_space=pltpu.VMEM)
SMEM = pl.BlockSpec(memory_space=pltpu.SMEM)


def split(x):
    high = x.astype(BF16)
    return high, (x - high.astype(F32)).astype(BF16)


def dot1(a, b, dims):
    return lax.dot_general(a, b, dims, preferred_element_type=F32)


def dot3(a, b, dims):
    ah, al = split(a)
    bh, bl = split(b)
    return dot1(ah, bh, dims) + (dot1(al, bh, dims) + dot1(ah, bl, dims))


def factor_base(S):
    n = S.shape[0]
    wide = 2 * n // 128
    lane = lax.broadcasted_iota(jnp.int32, (n, n), 1)
    sub = lax.broadcasted_iota(jnp.int32, (n, n), 0)
    M = jnp.concatenate([S, jnp.where(lane == sub, F32(1), F32(0))], axis=1)
    row = lax.broadcasted_iota(jnp.int32, (8, 1), 0)
    across = lambda v: jnp.concatenate([v] * wide, axis=1)
    done = []
    for o in range(0, n, 8):
        R = M[0:8]
        cols = [jnp.broadcast_to(R[:, o + j : o + j + 1], (8, 128)) for j in range(8)]
        D = [[jnp.broadcast_to(cols[j][i : i + 1], (8, 128)) for j in range(i + 1)] for i in range(8)]
        Y = [jnp.broadcast_to(R[i : i + 1], (8, 2 * n)) for i in range(8)]
        low = [[None] * 8 for _ in range(8)]
        inv = [None] * 8
        for j in range(8):
            inv[j] = 1.0 / D[j][j]
            for i in range(j + 1, 8):
                low[i][j] = D[i][j] * inv[j]
            for i in range(j + 1, 8):
                for m in range(j + 1, i + 1):
                    D[i][m] = D[i][m] - low[i][j] * D[m][j]
                Y[i] = Y[i] - across(low[i][j]) * Y[j]
        out = None
        for j in range(8):
            scaled = Y[j] * across(lax.rsqrt(D[j][j]))
            out = scaled if out is None else jnp.where(row == j, scaled, out)
        done.append(out)
        if o + 8 == n:
            break
        Z = [None] * 8
        for i in range(7, -1, -1):
            Z[i] = Y[i] * across(inv[i])
            for m in range(i + 1, 8):
                Z[i] = Z[i] - across(low[m][i]) * Z[m]
        step = Z[0]
        for i in range(1, 8):
            step = jnp.where(row == i, Z[i], step)
        parts = [jnp.zeros((o, 2 * n), F32)] if o else []
        parts += [step, jnp.zeros((n - o - 8, 2 * n), F32)]
        M = M[8:] - dot3(M[8:, :n], jnp.concatenate(parts, axis=0), NN)
    done = jnp.concatenate(done, axis=0)
    return jnp.where(lane >= sub, done[:, :n], F32(0)), jnp.where(lane <= sub, done[:, n:], F32(0))


def factor_whole(a_ref, l_ref, w_ref):
    n = a_ref.shape[0]
    b = 128
    w_ref[...] = jnp.zeros((n, n), F32)
    l_ref[...] = jnp.zeros((n, n), F32)
    lane = lax.broadcasted_iota(jnp.int32, (b, b), 1)
    sub = lax.broadcasted_iota(jnp.int32, (b, b), 0)
    for k in range(0, n, b):
        s = slice(k, k + b)
        D = a_ref[s, s]
        U, W = factor_base(jnp.where(sub >= lane, D, D.T))
        l_ref[s, s] = U.T
        w_ref[s, s] = W
        if k:
            T = dot3(l_ref[s, :k], w_ref[:k, :k], NN)
            w_ref[s, :k] = -dot3(W, T, NN)
        if k + b < n:
            L = dot3(a_ref[k + b :, s], W, NT)
            l_ref[k + b :, s] = L
            for j in range(k + b, n, b):
                off = j - k - b
                a_ref[j:, j : j + b] = a_ref[j:, j : j + b] - dot3(L[off:], L[off : off + b], NT)


def factor_first_kernel(at_ref, mine_ref, other_ref, l_ref, w_ref, a_ref):
    for ref, sub in ((mine_ref, at_ref[0]), (other_ref, 1 - at_ref[0])):
        a_ref[pl.ds(pl.multiple_of(sub * 256, 256), 256), :] = ref[...].reshape(256, -1)
    factor_whole(a_ref, l_ref, w_ref)


def factor_second_kernel(at_ref, mask_ref, mine_ref, other_ref, w0_ref, p_ref, l_ref, w_ref, a_ref, b_ref):
    n = a_ref.shape[0]
    for ref, sub in ((mine_ref, at_ref[0]), (other_ref, 1 - at_ref[0])):
        rows = pl.ds(pl.multiple_of(sub * 256, 256), 256)
        b_ref[rows, :] = ref[:, :, :n].reshape(256, n)
        a_ref[rows, :] = ref[:, :, n:].reshape(256, n)
    panel = dot3(b_ref[...], w0_ref[...], NT).astype(BF16)
    p_ref[...] = panel
    h = n // 2
    for i in range(2):
        for j in range(i + 1):
            r, c = slice(i * h, (i + 1) * h), slice(j * h, (j + 1) * h)
            product = dot1(panel[r], panel[c], NT)
            a_ref[r, c] = a_ref[r, c] - jnp.where(mask_ref[i * 2 + j] > 0, product, F32(0))
    factor_whole(a_ref, l_ref, w_ref)


CHOL_COST = pl.CostEstimate(flops=20_000_000_000, bytes_accessed=3 * MIB, transcendentals=1024)


def factor_first(at, mine, other):
    n = mine.shape[-1]
    return pl.pallas_call(
        factor_first_kernel,
        out_shape=[jax.ShapeDtypeStruct((n, n), F32)] * 2,
        in_specs=[SMEM, VMEM, VMEM],
        out_specs=[VMEM] * 2,
        scratch_shapes=[pltpu.VMEM((n, n), F32)],
        cost_estimate=CHOL_COST,
        compiler_params=pltpu.CompilerParams(vmem_limit_bytes=40 * MIB),
    )(at, mine, other)


def factor_second(at, mask, mine, other, W0):
    n = W0.shape[0]
    return pl.pallas_call(
        factor_second_kernel,
        out_shape=[jax.ShapeDtypeStruct((n, n), BF16)] + [jax.ShapeDtypeStruct((n, n), F32)] * 2,
        in_specs=[SMEM, SMEM, VMEM, VMEM, VMEM],
        out_specs=[VMEM] * 3,
        scratch_shapes=[pltpu.VMEM((n, n), F32)] * 2,
        cost_estimate=CHOL_COST,
        compiler_params=pltpu.CompilerParams(vmem_limit_bytes=40 * MIB),
    )(at, mask, mine, other, W0)


def cut_top_kernel(x_ref, c_ref, o_ref):
    for k in range(6):
        o_ref[:, k] = c_ref[k].reshape(16, 16, 256)
    for i in range(2):
        for c in range(4):
            high, low = split(x_ref[pl.ds(i * 2048 + c, 256, stride=8), :])
            at = 6 + i * 4 + c // 2 * 2
            lanes = slice(c % 2 * 128, c % 2 * 128 + 128)
            o_ref[:, at, :, lanes] = high.reshape(16, 16, 128)
            o_ref[:, at + 1, :, lanes] = low.reshape(16, 16, 128)


def cut_top(front_rows, child):
    return pl.pallas_call(
        cut_top_kernel,
        grid=(1,),
        out_shape=jax.ShapeDtypeStruct((16, 14, 16, 256), BF16),
        in_specs=[
            pl.BlockSpec((4096, 128), lambda i: (0, 0)),
            pl.BlockSpec((6, 256, 256), lambda i: (0, 0, 0)),
        ],
        out_specs=pl.BlockSpec((16, 14, 16, 256), lambda i: (0, 0, 0, 0)),
        cost_estimate=pl.CostEstimate(flops=0, bytes_accessed=5 * MIB, transcendentals=0),
        compiler_params=pltpu.CompilerParams(vmem_limit_bytes=40 * MIB),
    )(front_rows, child)


def cut_low_kernel(at_ref, x_ref, o_ref):
    q = at_ref[1]
    o_ref[...] = jnp.zeros(o_ref.shape, F32)
    for owner in range(2):

        @pl.when(q == owner)
        def _():
            for c in range(4):
                tile = x_ref[pl.ds(c, 256, stride=8), :]
                o_ref[:, 0, :, owner * 512 + c * 128 : owner * 512 + c * 128 + 128] = tile.reshape(16, 16, 128)


def cut_low(at, front_rows):
    return pl.pallas_call(
        cut_low_kernel,
        grid=(6,),
        out_shape=jax.ShapeDtypeStruct((16, 6, 16, 1024), F32),
        in_specs=[SMEM, pl.BlockSpec((2048, 128), lambda i: (i + 2, 0))],
        out_specs=pl.BlockSpec((16, 1, 16, 1024), lambda i: (0, i, 0, 0)),
        cost_estimate=pl.CostEstimate(flops=0, bytes_accessed=12 * MIB, transcendentals=0),
    )(at, front_rows)


def add_pieces(value, slot_ref, c_ref, row, j):
    for child in range(2):
        slot = slot_ref[(row * 4 + j) * 2 + child]
        known = jnp.maximum(slot, 0)
        piece = c_ref[known // 6, lax.rem(known, 6)].astype(F32)
        value = value + jnp.where(slot >= 0, piece, F32(0))
    return value


def join_top_kernel(slot_ref, c_ref, o_ref):
    for i in range(2):
        for j in range(4):
            at = 6 + i * 4 + j % 2 * 2
            value = c_ref[j // 2, at].astype(F32) + c_ref[j // 2, at + 1].astype(F32)
            o_ref[i, :, j * 256 : (j + 1) * 256] = add_pieces(value, slot_ref, c_ref, i, j)


def join_low_kernel(slot_ref, c_ref, f_ref, o_ref):
    for i in range(6):
        for j in range(4):
            lanes = slice(j * 256, (j + 1) * 256)
            o_ref[i, :, lanes] = add_pieces(f_ref[i, :, lanes], slot_ref, c_ref, i + 2, j)


def join_strips(kernel, count, slots, *operands):
    return pl.pallas_call(
        kernel,
        out_shape=jax.ShapeDtypeStruct((count, 16, 1024), F32),
        in_specs=[SMEM] + [VMEM] * len(operands),
        out_specs=VMEM,
        cost_estimate=pl.CostEstimate(flops=0, bytes_accessed=3 * MIB, transcendentals=0),
    )(slots, *operands)


def solve_first_kernel(keep_ref, d_ref, r_ref, w_ref, o_ref):
    width = w_ref.shape[0]
    b = jnp.concatenate(
        [d_ref[:, :, :width].reshape(32, width), r_ref[:, :, :width].reshape(96, width)], axis=0
    )
    x = dot3(b, w_ref[...], NT).reshape(8, 16, width)
    for i in range(8):
        o_ref[i] = jnp.where(keep_ref[i] > 0, x[i], F32(0)).astype(BF16)


def solve_second_kernel(keep_ref, d_ref, r_ref, p_ref, p10_ref, w_ref, o_ref):
    width = w_ref.shape[0]
    half = width // 2
    b = jnp.concatenate(
        [d_ref[:, :, width:].reshape(32, width), r_ref[:, :, width:].reshape(96, width)], axis=0
    )
    u = dot1(p_ref[...].reshape(128, width), p10_ref[...], NT)
    rows = []
    for i in range(8):
        s = slice(16 * i, 16 * i + 16)
        parts = []
        for j in range(2):
            c = slice(j * half, (j + 1) * half)
            parts.append(b[s, c] - jnp.where(keep_ref[8 + 2 * i + j] > 0, u[s, c], F32(0)))
        rows.append(jnp.concatenate(parts, axis=1))
    x = dot3(jnp.concatenate(rows, axis=0), w_ref[...], NT).reshape(8, 16, width)
    for i in range(8):
        o_ref[i] = jnp.where(keep_ref[i] > 0, x[i], F32(0)).astype(BF16)


def solve_strips(kernel, *operands):
    return pl.pallas_call(
        kernel,
        out_shape=jax.ShapeDtypeStruct((8, 16, 512), BF16),
        in_specs=[SMEM] + [VMEM] * (len(operands) - 1),
        out_specs=VMEM,
        cost_estimate=pl.CostEstimate(flops=400_000_000, bytes_accessed=2 * MIB, transcendentals=0),
    )(*operands)


def deal_kernel(at_ref, p_ref, *refs):
    o_ref = refs[-1]
    for q in range(16):
        o_ref[q, 0:8] = p_ref[...]
    for panel in range(2):
        for k in range(4):
            row = lax.rem(at_ref[2] + k, 4) * 2
            for c in range(2):
                for lr in range(4):
                    o_ref[(lr % 2) * 8 + row + c, 8 + panel * 2 + lr // 2] = refs[panel * 4 + k][c, lr]


def deal(at, P1, first, second):
    return pl.pallas_call(
        deal_kernel,
        out_shape=jax.ShapeDtypeStruct((16, 12, 16, 512), BF16),
        in_specs=[SMEM] + [VMEM] * 9,
        out_specs=VMEM,
        cost_estimate=pl.CostEstimate(flops=0, bytes_accessed=6 * MIB, transcendentals=0),
    )(at, P1, *first, *second)


def finish_kernel(slot_ref, flag_ref, f_ref, *refs):
    child = refs[:8]
    row0_ref, row1_ref, mine_ref, other_ref, l_ref, w_ref, o_ref, cols_ref = refs[8:]
    i = pl.program_id(0)

    @pl.when(i == 0)
    def _():
        core = flag_ref[48]
        for ref, sub in ((mine_ref, core), (other_ref, 1 - core)):
            for panel in range(2):
                for lc in range(2):
                    strips = ref[:, panel * 2 + lc].reshape(256, 512)
                    cols_ref[lc * 2 + sub, :, panel * 512 : (panel + 1) * 512] = strips

    rows = jnp.concatenate([ref[:, 0].reshape(256, 512) for ref in (row0_ref, row1_ref)], axis=1)
    for lc in range(2):
        state = flag_ref[32 + i * 2 + lc]

        @pl.when(state > 0)
        def _():
            blocks = []
            for sc in range(2):
                j = lc * 2 + sc
                value = jnp.concatenate(
                    [f_ref[pl.ds(lc * 4 + sc * 2 + c, 256, stride=8), :] for c in range(2)], axis=1
                )
                for ch in range(2):
                    live = slot_ref[(i * 4 + j) * 2 + ch] >= 0
                    value = value + jnp.where(live, child[j * 2 + ch][0].astype(F32), F32(0))
                product = dot1(rows, cols_ref[j], NT)
                blocks.append(value - jnp.where(flag_ref[i * 4 + j] > 0, product, F32(0)))
            block = jnp.concatenate(blocks, axis=1)

            def put(value):
                for c in range(4):
                    o_ref[pl.ds(lc * 4 + c, 256, stride=8), :] = value[:, c * 128 : (c + 1) * 128]

            @pl.when(state == 1)
            def _():
                put(block)

            if lc == 0:

                @pl.when(state == 2)
                def _():
                    put(dot3(block, w_ref[...], NT))

                @pl.when(state == 3)
                def _():
                    put(l_ref[pl.ds(pl.multiple_of(lax.rem(i, 2) * 256, 256), 256), :])

        @pl.when(state == 0)
        def _():
            for c in range(4):
                o_ref[pl.ds(lc * 4 + c, 256, stride=8), :] = jnp.zeros((256, 128), F32)


def finish(slots, flags, front_rows, arrived, row0, dealt, other, L, W):
    def child_spec(k):
        return pl.BlockSpec((1, 256, 256), lambda i, s, f: (jnp.maximum(s[i * 8 + k], 0), 0, 0))

    def whole(shape, *at):
        return pl.BlockSpec(shape, lambda i, s, f: at)

    rows = pl.BlockSpec((16, 1, 16, 512), lambda i, s, f: (0, i, 0, 0))
    return pl.pallas_call(
        finish_kernel,
        grid_spec=pltpu.PrefetchScalarGridSpec(
            num_scalar_prefetch=2,
            grid=(8,),
            in_specs=[pl.BlockSpec((2048, 128), lambda i, s, f: (i, 0))]
            + [child_spec(k) for k in range(8)]
            + [rows, rows]
            + [whole((16, 4, 16, 512), 0, 2, 0, 0), whole((16, 4, 16, 512), 0, 0, 0, 0)]
            + [whole((512, 512), 0, 0)] * 2,
            out_specs=pl.BlockSpec((2048, 128), lambda i, s, f: (i, 0)),
            scratch_shapes=[pltpu.VMEM((4, 256, 1024), BF16)],
        ),
        out_shape=jax.ShapeDtypeStruct(front_rows.shape, F32),
        cost_estimate=pl.CostEstimate(flops=5_000_000_000, bytes_accessed=28 * MIB, transcendentals=0),
        compiler_params=pltpu.CompilerParams(vmem_limit_bytes=48 * MIB),
    )(slots, flags, front_rows, *([arrived] * 8), row0, dealt, dealt, other, L, W)


def slot_of_targets(codes, row_map, rows, cols):
    index = jnp.arange(CNB, dtype=jnp.int32)

    def place(blocks):
        hit = row_map[None] == blocks[:, None, None]
        return jnp.sum(jnp.where(hit, index + 1, 0), axis=-1) - 1

    pi, pj = place(rows), place(cols)
    child = jnp.arange(2, dtype=jnp.int32) * (CNB * CNB)
    wanted = child + pi[:, None, :] * CNB + pj[None, :, :]
    known = (pi[:, None, :] >= 0) & (pj[None, :, :] >= 0)
    wanted = jnp.where(known, wanted, -2).reshape(-1)
    number = jnp.arange(codes.shape[0], dtype=jnp.int32)
    return jnp.sum(jnp.where(wanted[:, None] == codes[None, :], number + 1, 0), axis=-1) - 1


def spread(x, axis, count):
    return lax.all_to_all(jnp.broadcast_to(x[None], (count,) + x.shape), axis, 0, 0, tiled=True)


def local(front, child_blocks, row_map, slot_table, struct_mask):
    prow, pcol = lax.axis_size("prow"), lax.axis_size("pcol")
    p, q = lax.axis_index("prow"), lax.axis_index("pcol")
    core, y = p % 2, p // 2
    at = jnp.stack([core, q, y]).astype(jnp.int32)
    swap = [(i, i ^ 1) for i in range(8)]
    front_rows = front.reshape(16384, 128)
    child = child_blocks[0, 0]

    pair = jnp.arange(2, dtype=jnp.int32)
    row_blocks = jnp.arange(4, dtype=jnp.int32) * prow + p
    col_blocks = jnp.arange(2, dtype=jnp.int32) * pcol + q
    sub_rows = (2 * row_blocks[:, None] + pair).reshape(-1)
    sub_cols = (2 * col_blocks[:, None] + pair).reshape(-1)

    got = lax.all_to_all(cut_top(front_rows, child.reshape(48, 256, 256)), "pcol", 0, 0, tiled=True)
    low_front = lax.psum_scatter(
        cut_low(at, front_rows).reshape(96, 16, 1024), "pcol", scatter_dimension=0, tiled=True
    )

    my_codes = lax.dynamic_index_in_dim(slot_table, p, 0, False)
    strip_slots = slot_of_targets(my_codes[:, :2].reshape(-1), row_map, sub_rows, jnp.arange(4, dtype=jnp.int32))
    slots = slot_of_targets(
        lax.dynamic_index_in_dim(my_codes, q, 1, False).reshape(-1), row_map, sub_rows, sub_cols
    )
    row_mask = struct_mask[sub_rows]
    lower = row_blocks[:, None] >= col_blocks[None, :]
    mask = row_mask[:, sub_cols]
    state = jnp.where(lower, 1, 0)
    owner = (q < 2) & (jnp.arange(2) == 0)
    state = jnp.where(owner[None, :] & lower, jnp.where(row_blocks[:, None] == q, 3, 2), state)
    flags = jnp.concatenate([mask.reshape(-1), jnp.repeat(state, 2, axis=0).reshape(-1), core.reshape(1)])
    flags = flags.astype(jnp.int32)
    keep0 = (sub_rows >= 2).astype(jnp.int32)
    keep1 = jnp.concatenate([(sub_rows >= 4).astype(jnp.int32), row_mask[:, 2:4].reshape(-1)])

    top = join_strips(join_top_kernel, 2, strip_slots, got)

    half_top = lax.all_to_all(jnp.tile(top, (prow // 2, 1, 1)), "prow", 0, 0, tiled=True)
    first = spread(half_top[0, :, :512], "pcol", pcol)
    diag0 = (first, lax.ppermute(first, "prow", swap))
    half_rest, diag0 = lax.optimization_barrier((half_top[1], diag0))
    rest = spread(half_rest, "pcol", pcol)
    diag1 = (rest, lax.ppermute(rest, "prow", swap))
    child, diag0, diag1 = lax.optimization_barrier((child, diag0, diag1))
    arrived = lax.all_to_all(child, "pcol", 0, 0, tiled=True).reshape(48, 256, 256)

    def gather_columns(strips):
        halves = strips.reshape(4, 2, 16, 512)
        even, odd = halves[:, 0], halves[:, 1]
        sent = lax.ppermute(jnp.where(core == 0, odd, even), "prow", swap)
        kept = jnp.where(core == 0, even, odd)
        chip = jnp.where(core == 0, jnp.stack([kept, sent]), jnp.stack([sent, kept]))
        along = lambda k: [(2 * ((i + k) % 4) + c, 2 * i + c) for i in range(4) for c in range(2)]
        return [chip] + [lax.ppermute(chip, "prow", along(k)) for k in range(1, 4)]

    L0, W0 = factor_first(at, *diag0)
    low = join_strips(join_low_kernel, 6, strip_slots, got, low_front)
    P0 = solve_strips(solve_first_kernel, keep0, top, low, W0)
    row0 = lax.all_gather(P0, "pcol")
    P0, diag1 = lax.optimization_barrier((P0, diag1))
    cols0 = gather_columns(P0)
    P10, L1, W1 = factor_second(at, struct_mask[2:4, 2:4].reshape(-1), *diag1, W0)
    P1 = solve_strips(solve_second_kernel, keep1, top, low, P0, P10, W1)
    cols1 = gather_columns(P1)

    dealt = deal(at, P1, cols0, cols1)
    dealt, arrived, row0 = lax.optimization_barrier((dealt, arrived, row0))
    dealt = lax.all_to_all(dealt, "pcol", 0, 0, tiled=True)
    other = lax.ppermute(dealt[:, 8:], "prow", swap)

    L = jnp.where(q == 0, L0, L1)
    W = jnp.where(q == 0, W0, W1)
    out = finish(slots, flags, front_rows, arrived, row0, dealt, other, L, W)
    return out.reshape(front.shape)


def solution(mesh):
    in_specs = (
        P(None, "prow", None, None, "pcol", None),
        P("prow", "pcol", None, None, None, None),
        P(),
        P(),
        P(),
    )
    out_specs = P(None, "prow", None, None, "pcol", None)
    return jax.shard_map(local, mesh=mesh, in_specs=in_specs, out_specs=out_specs, check_vma=False)
```

```python
import functools

import jax
import jax.numpy as jnp
from jax import lax
from jax.experimental import pallas as pl
from jax.experimental.pallas import tpu as pltpu
from jax.sharding import PartitionSpec as P

F32 = jnp.float32
BF16 = jnp.bfloat16
CNB = 60
NN = (((1,), (0,)), ((), ()))
NT = (((1,), (1,)), ((), ()))
MIB = 2**20
VMEM = pl.BlockSpec(memory_space=pltpu.VMEM)
SMEM = pl.BlockSpec(memory_space=pltpu.SMEM)


def split(x):
    high = x.astype(BF16)
    return high, (x - high.astype(F32)).astype(BF16)


def dot1(a, b, dims):
    return lax.dot_general(a, b, dims, preferred_element_type=F32)


def dot3(a, b, dims):
    ah, al = split(a)
    bh, bl = split(b)
    return dot1(ah, bh, dims) + (dot1(al, bh, dims) + dot1(ah, bl, dims))


GROUPS = 4


def eliminate(R, n):
    row = lax.broadcasted_iota(jnp.int32, (8, 1), 0)
    across = lambda v: jnp.concatenate([v, v], axis=1)
    over = lambda x, lane: jnp.broadcast_to(x[:, lane : lane + 1], (8, 128))
    done = []
    for g in range(len(R)):
        base = 8 * g
        later = range(g + 1, len(R))
        cols = [over(R[g], base + j) for j in range(8)]
        below = {h: [over(R[h], base + j) for j in range(8)] for h in later}
        D = [[jnp.broadcast_to(cols[j][i : i + 1], (8, 128)) for j in range(i + 1)] for i in range(8)]
        Y = [jnp.broadcast_to(R[g][i : i + 1], (8, 2 * n)) for i in range(8)]
        out = None
        for j in range(8):
            scale = lax.rsqrt(D[j][j])
            inverse = scale * scale
            for i in range(j + 1, 8):
                factor = D[i][j] * inverse
                for m in range(j + 1, i):
                    D[i][m] = D[i][m] - factor * D[m][j]
                D[i][i] = D[i][i] - (D[i][j] * D[i][j]) * inverse
                Y[i] = Y[i] - across(factor) * Y[j]
            for h in later:
                factor = below[h][j] * inverse
                for m in range(j + 1, 8):
                    below[h][m] = below[h][m] - factor * D[m][j]
                R[h] = R[h] - across(factor) * Y[j]
            scaled = Y[j] * across(scale)
            out = scaled if out is None else jnp.where(row == j, scaled, out)
        done.append(out)
    return jnp.concatenate(done, axis=0)


def factor_base(m_ref, o_ref):
    n = m_ref.shape[0]
    step = 8 * GROUPS

    def body(k, _):
        at = k * step
        rows = pl.ds(pl.multiple_of(at, step), step)
        X = m_ref[rows, :]
        A = pltpu.roll(X[:, :n], jnp.where(k == 0, 0, n - at), 1)
        X = jnp.concatenate([A, X[:, n:]], axis=1)
        out = eliminate([X[8 * g : 8 * g + 8] for g in range(GROUPS)], n)
        out = jnp.concatenate([pltpu.roll(out[:, :n], at, 1), out[:, n:]], axis=1)
        o_ref[rows, :] = out
        m_ref[...] = m_ref[...] - dot3(out[:, :n].T, out, NN)
        return 0

    lax.fori_loop(0, n // step, body, 0)


def factor_whole(a_ref, l_ref, w_ref, m_ref, o_ref):
    n = a_ref.shape[0]
    b = 128
    w_ref[...] = jnp.zeros((n, n), F32)
    l_ref[...] = jnp.zeros((n, n), F32)
    lane = lax.broadcasted_iota(jnp.int32, (b, b), 1)
    sub = lax.broadcasted_iota(jnp.int32, (b, b), 0)
    for k in range(0, n, b):
        s = slice(k, k + b)
        D = a_ref[s, s]
        m_ref[:, :b] = jnp.where(sub >= lane, D, D.T)
        m_ref[:, b:] = jnp.where(lane == sub, F32(1), F32(0))
        factor_base(m_ref, o_ref)
        W = jnp.where(lane <= sub, o_ref[:, b:], F32(0))
        l_ref[s, s] = jnp.where(lane >= sub, o_ref[:, :b], F32(0)).T
        w_ref[s, s] = W
        if k:
            T = dot3(l_ref[s, :k], w_ref[:k, :k], NN)
            w_ref[s, :k] = -dot3(W, T, NN)
        if k + b < n:
            L = dot3(a_ref[k + b :, s], W, NT)
            l_ref[k + b :, s] = L
            for j in range(k + b, n, b):
                off = j - k - b
                a_ref[j:, j : j + b] = a_ref[j:, j : j + b] - dot3(L[off:], L[off : off + b], NT)


def factor_first_kernel(at_ref, mine_ref, other_ref, l_ref, w_ref, a_ref, m_ref, o_ref):
    n = a_ref.shape[0]
    for ref, sub in ((mine_ref, at_ref[0]), (other_ref, 1 - at_ref[0])):
        a_ref[pl.ds(pl.multiple_of(sub * 256, 256), 256), :] = ref[:, :, :n].reshape(256, n)
    factor_whole(a_ref, l_ref, w_ref, m_ref, o_ref)


def factor_second_kernel(
    at_ref, mask_ref, mine_ref, other_ref, w0_ref, p_ref, l_ref, w_ref, a_ref, m_ref, o_ref, b_ref
):
    n = a_ref.shape[0]
    for ref, sub in ((mine_ref, at_ref[0]), (other_ref, 1 - at_ref[0])):
        rows = pl.ds(pl.multiple_of(sub * 256, 256), 256)
        b_ref[rows, :] = ref[:, :, n : 2 * n].reshape(256, n)
        a_ref[rows, :] = ref[:, :, 2 * n :].reshape(256, n)
    panel = dot3(b_ref[...], w0_ref[...], NT).astype(BF16)
    p_ref[...] = panel
    h = n // 2
    for i in range(2):
        for j in range(i + 1):
            r, c = slice(i * h, (i + 1) * h), slice(j * h, (j + 1) * h)
            product = dot1(panel[r], panel[c], NT)
            a_ref[r, c] = a_ref[r, c] - jnp.where(mask_ref[i * 2 + j] > 0, product, F32(0))
    factor_whole(a_ref, l_ref, w_ref, m_ref, o_ref)


CHOL_COST = pl.CostEstimate(flops=20_000_000_000, bytes_accessed=3 * MIB, transcendentals=1024)


def factor_first(at, mine, other):
    n = mine.shape[-1] // 3
    return pl.pallas_call(
        factor_first_kernel,
        out_shape=[jax.ShapeDtypeStruct((n, n), F32)] * 2,
        in_specs=[SMEM, VMEM, VMEM],
        out_specs=[VMEM] * 2,
        scratch_shapes=[pltpu.VMEM((n, n), F32)] + [pltpu.VMEM((128, 256), F32)] * 2,
        cost_estimate=CHOL_COST,
        compiler_params=pltpu.CompilerParams(vmem_limit_bytes=40 * MIB),
    )(at, mine, other)


def factor_second(at, mask, mine, other, W0):
    n = W0.shape[0]
    return pl.pallas_call(
        factor_second_kernel,
        out_shape=[jax.ShapeDtypeStruct((n, n), BF16)] + [jax.ShapeDtypeStruct((n, n), F32)] * 2,
        in_specs=[SMEM, SMEM, VMEM, VMEM, VMEM],
        out_specs=[VMEM] * 3,
        scratch_shapes=[pltpu.VMEM((n, n), F32)]
        + [pltpu.VMEM((128, 256), F32)] * 2
        + [pltpu.VMEM((n, n), F32)],
        cost_estimate=CHOL_COST,
        compiler_params=pltpu.CompilerParams(vmem_limit_bytes=40 * MIB),
    )(at, mask, mine, other, W0)


def cut_top_kernel(x_ref, c_ref, o_ref):
    for k in range(6):
        o_ref[:, k] = c_ref[k].reshape(16, 16, 256)
    for i in range(2):
        for c in range(4):
            high, low = split(x_ref[pl.ds(i * 2048 + c, 256, stride=8), :])
            at = 6 + i * 4 + c // 2 * 2
            lanes = slice(c % 2 * 128, c % 2 * 128 + 128)
            o_ref[:, at, :, lanes] = high.reshape(16, 16, 128)
            o_ref[:, at + 1, :, lanes] = low.reshape(16, 16, 128)


def cut_top(front_rows, child):
    return pl.pallas_call(
        cut_top_kernel,
        grid=(1,),
        out_shape=jax.ShapeDtypeStruct((16, 14, 16, 256), BF16),
        in_specs=[
            pl.BlockSpec((4096, 128), lambda i: (0, 0)),
            pl.BlockSpec((6, 256, 256), lambda i: (0, 0, 0)),
        ],
        out_specs=pl.BlockSpec((16, 14, 16, 256), lambda i: (0, 0, 0, 0)),
        cost_estimate=pl.CostEstimate(flops=0, bytes_accessed=5 * MIB, transcendentals=0),
        compiler_params=pltpu.CompilerParams(vmem_limit_bytes=40 * MIB),
    )(front_rows, child)


def cut_low_kernel(at_ref, x_ref, o_ref):
    q = at_ref[1]
    o_ref[...] = jnp.zeros(o_ref.shape, F32)
    for owner in range(2):

        @pl.when(q == owner)
        def _():
            for c in range(4):
                tile = x_ref[pl.ds(c, 256, stride=8), :]
                o_ref[:, 0, :, owner * 512 + c * 128 : owner * 512 + c * 128 + 128] = tile.reshape(16, 16, 128)


def cut_low(at, front_rows):
    return pl.pallas_call(
        cut_low_kernel,
        grid=(6,),
        out_shape=jax.ShapeDtypeStruct((16, 6, 16, 1024), F32),
        in_specs=[SMEM, pl.BlockSpec((2048, 128), lambda i: (i + 2, 0))],
        out_specs=pl.BlockSpec((16, 1, 16, 1024), lambda i: (0, i, 0, 0)),
        cost_estimate=pl.CostEstimate(flops=0, bytes_accessed=12 * MIB, transcendentals=0),
    )(at, front_rows)


def add_pieces(value, slot_ref, c_ref, row, j):
    for child in range(2):
        slot = slot_ref[(row * 4 + j) * 2 + child]
        known = jnp.maximum(slot, 0)
        piece = c_ref[known // 6, lax.rem(known, 6)].astype(F32)
        value = value + jnp.where(slot >= 0, piece, F32(0))
    return value


def join_top_kernel(slot_ref, c_ref, o_ref):
    for i in range(2):
        for j in range(4):
            at = 6 + i * 4 + j % 2 * 2
            value = c_ref[j // 2, at].astype(F32) + c_ref[j // 2, at + 1].astype(F32)
            o_ref[i, :, j * 256 : (j + 1) * 256] = add_pieces(value, slot_ref, c_ref, i, j)


def join_low_kernel(slot_ref, c_ref, f_ref, o_ref):
    for i in range(6):
        for j in range(4):
            lanes = slice(j * 256, (j + 1) * 256)
            o_ref[i, :, lanes] = add_pieces(f_ref[i, :, lanes], slot_ref, c_ref, i + 2, j)


def join_strips(kernel, count, slots, *operands):
    return pl.pallas_call(
        kernel,
        out_shape=jax.ShapeDtypeStruct((count, 16, 1024), F32),
        in_specs=[SMEM] + [VMEM] * len(operands),
        out_specs=VMEM,
        cost_estimate=pl.CostEstimate(flops=0, bytes_accessed=3 * MIB, transcendentals=0),
    )(slots, *operands)


def solve_first_kernel(keep_ref, d_ref, r_ref, w_ref, o_ref):
    width = w_ref.shape[0]
    b = jnp.concatenate(
        [d_ref[:, :, :width].reshape(32, width), r_ref[:, :, :width].reshape(96, width)], axis=0
    )
    x = dot3(b, w_ref[...], NT).reshape(8, 16, width)
    for i in range(8):
        o_ref[i] = jnp.where(keep_ref[i] > 0, x[i], F32(0)).astype(BF16)


def solve_second_kernel(keep_ref, d_ref, r_ref, p_ref, p10_ref, w_ref, o_ref):
    width = w_ref.shape[0]
    half = width // 2
    b = jnp.concatenate(
        [d_ref[:, :, width:].reshape(32, width), r_ref[:, :, width:].reshape(96, width)], axis=0
    )
    u = dot1(p_ref[...].reshape(128, width), p10_ref[...], NT)
    rows = []
    for i in range(8):
        s = slice(16 * i, 16 * i + 16)
        parts = []
        for j in range(2):
            c = slice(j * half, (j + 1) * half)
            parts.append(b[s, c] - jnp.where(keep_ref[8 + 2 * i + j] > 0, u[s, c], F32(0)))
        rows.append(jnp.concatenate(parts, axis=1))
    x = dot3(jnp.concatenate(rows, axis=0), w_ref[...], NT).reshape(8, 16, width)
    for i in range(8):
        o_ref[i] = jnp.where(keep_ref[i] > 0, x[i], F32(0)).astype(BF16)


def solve_strips(kernel, *operands):
    return pl.pallas_call(
        kernel,
        out_shape=jax.ShapeDtypeStruct((8, 16, 512), BF16),
        in_specs=[SMEM] + [VMEM] * (len(operands) - 1),
        out_specs=VMEM,
        cost_estimate=pl.CostEstimate(flops=400_000_000, bytes_accessed=2 * MIB, transcendentals=0),
    )(*operands)


def deal_kernel(at_ref, p0_ref, p1_ref, *refs):
    o_ref = refs[-1]
    for q in range(16):
        o_ref[q, 0:8] = p0_ref[...]
        o_ref[q, 8:16] = p1_ref[...]
    for panel in range(2):
        for k in range(4):
            row = lax.rem(at_ref[2] + k, 4) * 2
            for c in range(2):
                for lr in range(4):
                    o_ref[(lr % 2) * 8 + row + c, 16 + panel * 2 + lr // 2] = refs[panel * 4 + k][c, lr]


def deal(at, P0, P1, first, second):
    return pl.pallas_call(
        deal_kernel,
        out_shape=jax.ShapeDtypeStruct((16, 20, 16, 512), BF16),
        in_specs=[SMEM] + [VMEM] * 10,
        out_specs=VMEM,
        cost_estimate=pl.CostEstimate(flops=0, bytes_accessed=8 * MIB, transcendentals=0),
        compiler_params=pltpu.CompilerParams(vmem_limit_bytes=24 * MIB),
    )(at, P0, P1, *first, *second)


def extend_kernel(slot_ref, f_ref, *refs):
    child, o_ref = refs[:8], refs[8]
    i = pl.program_id(0)
    for j in range(4):
        live = [slot_ref[(i * 4 + j) * 2 + ch] >= 0 for ch in range(2)]
        pieces = [child[j * 2 + ch] for ch in range(2)]
        for c in range(2):
            lanes = slice(c * 128, (c + 1) * 128)
            rows = pl.ds(j * 2 + c, 256, stride=8)
            value = f_ref[rows, :]
            for ch in range(2):
                value = value + jnp.where(live[ch], pieces[ch][0, :, lanes].astype(F32), F32(0))
            o_ref[rows, :] = value


def extend(slots, front_rows, arrived):
    def child_spec(k):
        return pl.BlockSpec((1, 256, 256), lambda i, s: (jnp.maximum(s[i * 8 + k], 0), 0, 0))

    return pl.pallas_call(
        extend_kernel,
        grid_spec=pltpu.PrefetchScalarGridSpec(
            num_scalar_prefetch=1,
            grid=(8,),
            in_specs=[pl.BlockSpec((2048, 128), lambda i, s: (i, 0))] + [child_spec(k) for k in range(8)],
            out_specs=pl.BlockSpec((2048, 128), lambda i, s: (i, 0)),
        ),
        out_shape=jax.ShapeDtypeStruct(front_rows.shape, F32),
        cost_estimate=pl.CostEstimate(flops=0, bytes_accessed=24 * MIB, transcendentals=0),
        compiler_params=pltpu.CompilerParams(vmem_limit_bytes=24 * MIB),
    )(slots, front_rows, *([arrived] * 8))


def finish_kernel(flag_ref, f_ref, row0_ref, row1_ref, mine_ref, other_ref, l_ref, w_ref, o_ref, cols_ref):
    i = pl.program_id(0)

    @pl.when(i == 0)
    def _():
        core = flag_ref[48]
        for ref, sub in ((mine_ref, core), (other_ref, 1 - core)):
            for panel in range(2):
                for lc in range(2):
                    strips = ref[:, panel * 2 + lc].reshape(256, 512)
                    cols_ref[lc * 2 + sub, :, panel * 512 : (panel + 1) * 512] = strips

    rows = jnp.concatenate([ref[:, 0].reshape(256, 512) for ref in (row0_ref, row1_ref)], axis=1)
    for lc in range(2):
        state = flag_ref[32 + i * 2 + lc]

        @pl.when(state > 0)
        def _():
            blocks = []
            for sc in range(2):
                j = lc * 2 + sc
                value = jnp.concatenate(
                    [f_ref[pl.ds(lc * 4 + sc * 2 + c, 256, stride=8), :] for c in range(2)], axis=1
                )
                product = dot1(rows, cols_ref[j], NT)
                blocks.append(value - jnp.where(flag_ref[i * 4 + j] > 0, product, F32(0)))
            block = jnp.concatenate(blocks, axis=1)

            def put(value):
                for c in range(4):
                    o_ref[pl.ds(lc * 4 + c, 256, stride=8), :] = value[:, c * 128 : (c + 1) * 128]

            @pl.when(state == 1)
            def _():
                put(block)

            if lc == 0:

                @pl.when(state == 2)
                def _():
                    put(dot3(block, w_ref[...], NT))

                @pl.when(state == 3)
                def _():
                    put(l_ref[pl.ds(pl.multiple_of(lax.rem(i, 2) * 256, 256), 256), :])

        @pl.when(state == 0)
        def _():
            for c in range(4):
                o_ref[pl.ds(lc * 4 + c, 256, stride=8), :] = jnp.zeros((256, 128), F32)


def finish(flags, extended, dealt, other, L, W):
    def whole(shape, *at):
        return pl.BlockSpec(shape, lambda i, f: at)

    return pl.pallas_call(
        finish_kernel,
        grid_spec=pltpu.PrefetchScalarGridSpec(
            num_scalar_prefetch=1,
            grid=(8,),
            in_specs=[pl.BlockSpec((2048, 128), lambda i, f: (i, 0))]
            + [pl.BlockSpec((16, 1, 16, 512), lambda i, f: (0, i, 0, 0))]
            + [pl.BlockSpec((16, 1, 16, 512), lambda i, f: (0, i + 8, 0, 0))]
            + [whole((16, 4, 16, 512), 0, 4, 0, 0), whole((16, 4, 16, 512), 0, 0, 0, 0)]
            + [whole((512, 512), 0, 0)] * 2,
            out_specs=pl.BlockSpec((2048, 128), lambda i, f: (i, 0)),
            scratch_shapes=[pltpu.VMEM((4, 256, 1024), BF16)],
        ),
        out_shape=jax.ShapeDtypeStruct(extended.shape, F32),
        cost_estimate=pl.CostEstimate(flops=5_000_000_000, bytes_accessed=24 * MIB, transcendentals=0),
        compiler_params=pltpu.CompilerParams(vmem_limit_bytes=48 * MIB),
    )(flags, extended, dealt, dealt, dealt, other, L, W)


def slot_of_targets(codes, row_map, rows, cols):
    index = jnp.arange(CNB, dtype=jnp.int32)

    def place(blocks):
        hit = row_map[None] == blocks[:, None, None]
        return jnp.sum(jnp.where(hit, index + 1, 0), axis=-1) - 1

    pi, pj = place(rows), place(cols)
    child = jnp.arange(2, dtype=jnp.int32) * (CNB * CNB)
    wanted = child + pi[:, None, :] * CNB + pj[None, :, :]
    known = (pi[:, None, :] >= 0) & (pj[None, :, :] >= 0)
    wanted = jnp.where(known, wanted, -2).reshape(-1)
    number = jnp.arange(codes.shape[0], dtype=jnp.int32)
    return jnp.sum(jnp.where(wanted[:, None] == codes[None, :], number + 1, 0), axis=-1) - 1


def spread(x, axis, count):
    return lax.all_to_all(jnp.broadcast_to(x[None], (count,) + x.shape), axis, 0, 0, tiled=True)


def local(front, child_blocks, row_map, slot_table, struct_mask):
    prow, pcol = lax.axis_size("prow"), lax.axis_size("pcol")
    p, q = lax.axis_index("prow"), lax.axis_index("pcol")
    core, y = p % 2, p // 2
    at = jnp.stack([core, q, y]).astype(jnp.int32)
    swap = [(i, i ^ 1) for i in range(8)]
    front_rows = front.reshape(16384, 128)
    child = child_blocks[0, 0]

    pair = jnp.arange(2, dtype=jnp.int32)
    row_blocks = jnp.arange(4, dtype=jnp.int32) * prow + p
    col_blocks = jnp.arange(2, dtype=jnp.int32) * pcol + q
    sub_rows = (2 * row_blocks[:, None] + pair).reshape(-1)
    sub_cols = (2 * col_blocks[:, None] + pair).reshape(-1)

    cut = cut_top(front_rows, child.reshape(48, 256, 256))
    got = lax.all_to_all(cut, "pcol", 0, 0, tiled=True)
    front_rows, _ = lax.optimization_barrier((front_rows, cut))
    low_front = lax.psum_scatter(
        cut_low(at, front_rows).reshape(96, 16, 1024), "pcol", scatter_dimension=0, tiled=True
    )

    my_codes = lax.dynamic_index_in_dim(slot_table, p, 0, False)
    strip_slots = slot_of_targets(my_codes[:, :2].reshape(-1), row_map, sub_rows, jnp.arange(4, dtype=jnp.int32))
    slots = slot_of_targets(
        lax.dynamic_index_in_dim(my_codes, q, 1, False).reshape(-1), row_map, sub_rows, sub_cols
    )
    row_mask = struct_mask[sub_rows]
    lower = row_blocks[:, None] >= col_blocks[None, :]
    mask = row_mask[:, sub_cols]
    state = jnp.where(lower, 1, 0)
    owner = (q < 2) & (jnp.arange(2) == 0)
    state = jnp.where(owner[None, :] & lower, jnp.where(row_blocks[:, None] == q, 3, 2), state)
    flags = jnp.concatenate([mask.reshape(-1), jnp.repeat(state, 2, axis=0).reshape(-1), core.reshape(1)])
    flags = flags.astype(jnp.int32)
    keep0 = (sub_rows >= 2).astype(jnp.int32)
    keep1 = jnp.concatenate([(sub_rows >= 4).astype(jnp.int32), row_mask[:, 2:4].reshape(-1)])

    top = join_strips(join_top_kernel, 2, strip_slots, got)

    half_top = lax.all_to_all(jnp.tile(top, (prow // 2, 1, 1)), "prow", 0, 0, tiled=True)
    first = spread(jnp.concatenate([half_top[0, :, :512], half_top[1]], axis=1), "pcol", pcol)
    diag = (first, lax.ppermute(first, "prow", swap))
    child, diag = lax.optimization_barrier((child, diag))
    arrived = lax.all_to_all(child, "pcol", 0, 0, tiled=True).reshape(48, 256, 256)

    def gather_columns(strips):
        halves = strips.reshape(4, 2, 16, 512)
        even, odd = halves[:, 0], halves[:, 1]
        sent = lax.ppermute(jnp.where(core == 0, odd, even), "prow", swap)
        kept = jnp.where(core == 0, even, odd)
        chip = jnp.where(core == 0, jnp.stack([kept, sent]), jnp.stack([sent, kept]))
        along = lambda k: [(2 * ((i + k) % 4) + c, 2 * i + c) for i in range(4) for c in range(2)]
        return [chip] + [lax.ppermute(chip, "prow", along(k)) for k in range(1, 4)]

    L0, W0 = factor_first(at, *diag)
    low = join_strips(join_low_kernel, 6, strip_slots, got, low_front)
    P0 = solve_strips(solve_first_kernel, keep0, top, low, W0)
    P0, diag = lax.optimization_barrier((P0, diag))
    cols0 = gather_columns(P0)
    P10, L1, W1 = factor_second(at, struct_mask[2:4, 2:4].reshape(-1), *diag, W0)
    W1, cols0 = lax.optimization_barrier((W1, cols0))
    P1 = solve_strips(solve_second_kernel, keep1, top, low, P0, P10, W1)
    cols1 = gather_columns(P1)

    dealt = deal(at, P0, P1, cols0, cols1)
    dealt, arrived = lax.optimization_barrier((dealt, arrived))
    dealt = lax.all_to_all(dealt, "pcol", 0, 0, tiled=True)
    extended = extend(slots, front_rows, arrived)
    dealt, extended = lax.optimization_barrier((dealt, extended))
    other = lax.ppermute(dealt[:, 16:], "prow", swap)

    L = jnp.where(q == 0, L0, L1)
    W = jnp.where(q == 0, W0, W1)
    out = finish(flags, extended, dealt, other, L, W)
    return out.reshape(front.shape)


def solution(mesh):
    in_specs = (
        P(None, "prow", None, None, "pcol", None),
        P("prow", "pcol", None, None, None, None),
        P(),
        P(),
        P(),
    )
    out_specs = P(None, "prow", None, None, "pcol", None)
    return jax.shard_map(local, mesh=mesh, in_specs=in_specs, out_specs=out_specs, check_vma=False)
```

```python
import functools

import jax
import jax.numpy as jnp
from jax import lax
from jax.experimental import pallas as pl
from jax.experimental.pallas import tpu as pltpu
from jax.sharding import PartitionSpec as P

F32 = jnp.float32
BF16 = jnp.bfloat16
CNB = 60
NN = (((1,), (0,)), ((), ()))
NT = (((1,), (1,)), ((), ()))
MIB = 2**20
VMEM = pl.BlockSpec(memory_space=pltpu.VMEM)
SMEM = pl.BlockSpec(memory_space=pltpu.SMEM)


def split(x):
    high = x.astype(BF16)
    return high, (x - high.astype(F32)).astype(BF16)


def dot1(a, b, dims):
    return lax.dot_general(a, b, dims, preferred_element_type=F32)


def dot3(a, b, dims):
    ah, al = split(a)
    bh, bl = split(b)
    return dot1(ah, bh, dims) + (dot1(al, bh, dims) + dot1(ah, bl, dims))


GROUPS = 4


def eliminate(R, n):
    row = lax.broadcasted_iota(jnp.int32, (8, 1), 0)
    across = lambda v: jnp.concatenate([v, v], axis=1)
    over = lambda x, lane: jnp.broadcast_to(x[:, lane : lane + 1], (8, 128))
    done = []
    for g in range(len(R)):
        base = 8 * g
        later = range(g + 1, len(R))
        cols = [over(R[g], base + j) for j in range(8)]
        below = {h: [over(R[h], base + j) for j in range(8)] for h in later}
        D = [[jnp.broadcast_to(cols[j][i : i + 1], (8, 128)) for j in range(i + 1)] for i in range(8)]
        Y = [jnp.broadcast_to(R[g][i : i + 1], (8, 2 * n)) for i in range(8)]
        out = None
        for j in range(8):
            scale = lax.rsqrt(D[j][j])
            inverse = scale * scale
            for i in range(j + 1, 8):
                factor = D[i][j] * inverse
                for m in range(j + 1, i):
                    D[i][m] = D[i][m] - factor * D[m][j]
                D[i][i] = D[i][i] - (D[i][j] * D[i][j]) * inverse
                Y[i] = Y[i] - across(factor) * Y[j]
            for h in later:
                factor = below[h][j] * inverse
                for m in range(j + 1, 8):
                    below[h][m] = below[h][m] - factor * D[m][j]
                R[h] = R[h] - across(factor) * Y[j]
            scaled = Y[j] * across(scale)
            out = scaled if out is None else jnp.where(row == j, scaled, out)
        done.append(out)
    return jnp.concatenate(done, axis=0)


def factor_base(m_ref, o_ref):
    n = m_ref.shape[0]
    step = 8 * GROUPS

    def body(k, _):
        at = k * step
        rows = pl.ds(pl.multiple_of(at, step), step)
        X = m_ref[rows, :]
        A = pltpu.roll(X[:, :n], jnp.where(k == 0, 0, n - at), 1)
        X = jnp.concatenate([A, X[:, n:]], axis=1)
        out = eliminate([X[8 * g : 8 * g + 8] for g in range(GROUPS)], n)
        out = jnp.concatenate([pltpu.roll(out[:, :n], at, 1), out[:, n:]], axis=1)
        o_ref[rows, :] = out
        m_ref[...] = m_ref[...] - dot3(out[:, :n].T, out, NN)
        return 0

    lax.fori_loop(0, n // step, body, 0)


def factor_whole(a_ref, l_ref, w_ref, m_ref, o_ref):
    n = a_ref.shape[0]
    b = 128
    w_ref[...] = jnp.zeros((n, n), F32)
    l_ref[...] = jnp.zeros((n, n), F32)
    lane = lax.broadcasted_iota(jnp.int32, (b, b), 1)
    sub = lax.broadcasted_iota(jnp.int32, (b, b), 0)
    for k in range(0, n, b):
        s = slice(k, k + b)
        D = a_ref[s, s]
        m_ref[:, :b] = jnp.where(sub >= lane, D, D.T)
        m_ref[:, b:] = jnp.where(lane == sub, F32(1), F32(0))
        factor_base(m_ref, o_ref)
        W = jnp.where(lane <= sub, o_ref[:, b:], F32(0))
        l_ref[s, s] = jnp.where(lane >= sub, o_ref[:, :b], F32(0)).T
        w_ref[s, s] = W
        if k:
            T = dot3(l_ref[s, :k], w_ref[:k, :k], NN)
            w_ref[s, :k] = -dot3(W, T, NN)
        if k + b < n:
            L = dot3(a_ref[k + b :, s], W, NT)
            l_ref[k + b :, s] = L
            for j in range(k + b, n, b):
                off = j - k - b
                a_ref[j:, j : j + b] = a_ref[j:, j : j + b] - dot3(L[off:], L[off : off + b], NT)


def factor_first_kernel(at_ref, mine_ref, other_ref, l_ref, w_ref, a_ref, m_ref, o_ref):
    n = a_ref.shape[0]
    for ref, sub in ((mine_ref, at_ref[0]), (other_ref, 1 - at_ref[0])):
        a_ref[pl.ds(pl.multiple_of(sub * 256, 256), 256), :] = ref[:, :, :n].reshape(256, n)
    factor_whole(a_ref, l_ref, w_ref, m_ref, o_ref)


def factor_second_kernel(
    at_ref, mask_ref, mine_ref, other_ref, w0_ref, p_ref, l_ref, w_ref, a_ref, m_ref, o_ref, b_ref
):
    n = a_ref.shape[0]
    for ref, sub in ((mine_ref, at_ref[0]), (other_ref, 1 - at_ref[0])):
        rows = pl.ds(pl.multiple_of(sub * 256, 256), 256)
        b_ref[rows, :] = ref[:, :, n : 2 * n].reshape(256, n)
        a_ref[rows, :] = ref[:, :, 2 * n :].reshape(256, n)
    panel = dot3(b_ref[...], w0_ref[...], NT).astype(BF16)
    p_ref[...] = panel
    h = n // 2
    for i in range(2):
        for j in range(i + 1):
            r, c = slice(i * h, (i + 1) * h), slice(j * h, (j + 1) * h)
            product = dot1(panel[r], panel[c], NT)
            a_ref[r, c] = a_ref[r, c] - jnp.where(mask_ref[i * 2 + j] > 0, product, F32(0))
    factor_whole(a_ref, l_ref, w_ref, m_ref, o_ref)


CHOL_COST = pl.CostEstimate(flops=20_000_000_000, bytes_accessed=3 * MIB, transcendentals=1024)


def factor_first(at, mine, other):
    n = mine.shape[-1] // 3
    return pl.pallas_call(
        factor_first_kernel,
        out_shape=[jax.ShapeDtypeStruct((n, n), F32)] * 2,
        in_specs=[SMEM, VMEM, VMEM],
        out_specs=[VMEM] * 2,
        scratch_shapes=[pltpu.VMEM((n, n), F32)] + [pltpu.VMEM((128, 256), F32)] * 2,
        cost_estimate=CHOL_COST,
        compiler_params=pltpu.CompilerParams(vmem_limit_bytes=40 * MIB),
    )(at, mine, other)


def factor_second(at, mask, mine, other, W0):
    n = W0.shape[0]
    return pl.pallas_call(
        factor_second_kernel,
        out_shape=[jax.ShapeDtypeStruct((n, n), BF16)] + [jax.ShapeDtypeStruct((n, n), F32)] * 2,
        in_specs=[SMEM, SMEM, VMEM, VMEM, VMEM],
        out_specs=[VMEM] * 3,
        scratch_shapes=[pltpu.VMEM((n, n), F32)]
        + [pltpu.VMEM((128, 256), F32)] * 2
        + [pltpu.VMEM((n, n), F32)],
        cost_estimate=CHOL_COST,
        compiler_params=pltpu.CompilerParams(vmem_limit_bytes=40 * MIB),
    )(at, mask, mine, other, W0)


def cut_top_kernel(x_ref, c_ref, o_ref):
    for k in range(6):
        o_ref[:, k] = c_ref[k].reshape(16, 16, 256)
    for i in range(2):
        for c in range(4):
            high, low = split(x_ref[pl.ds(i * 2048 + c, 256, stride=8), :])
            at = 6 + i * 4 + c // 2 * 2
            lanes = slice(c % 2 * 128, c % 2 * 128 + 128)
            o_ref[:, at, :, lanes] = high.reshape(16, 16, 128)
            o_ref[:, at + 1, :, lanes] = low.reshape(16, 16, 128)


def cut_top(front_rows, child):
    return pl.pallas_call(
        cut_top_kernel,
        grid=(1,),
        out_shape=jax.ShapeDtypeStruct((16, 14, 16, 256), BF16),
        in_specs=[
            pl.BlockSpec((4096, 128), lambda i: (0, 0)),
            pl.BlockSpec((6, 256, 256), lambda i: (0, 0, 0)),
        ],
        out_specs=pl.BlockSpec((16, 14, 16, 256), lambda i: (0, 0, 0, 0)),
        cost_estimate=pl.CostEstimate(flops=0, bytes_accessed=5 * MIB, transcendentals=0),
        compiler_params=pltpu.CompilerParams(vmem_limit_bytes=40 * MIB),
    )(front_rows, child)


def cut_low_kernel(at_ref, x_ref, o_ref):
    q = at_ref[1]
    o_ref[...] = jnp.zeros(o_ref.shape, F32)
    for owner in range(2):

        @pl.when(q == owner)
        def _():
            for c in range(4):
                tile = x_ref[pl.ds(c, 256, stride=8), :]
                o_ref[:, 0, :, owner * 512 + c * 128 : owner * 512 + c * 128 + 128] = tile.reshape(16, 16, 128)


def cut_low(at, front_rows):
    return pl.pallas_call(
        cut_low_kernel,
        grid=(6,),
        out_shape=jax.ShapeDtypeStruct((16, 6, 16, 1024), F32),
        in_specs=[SMEM, pl.BlockSpec((2048, 128), lambda i: (i + 2, 0))],
        out_specs=pl.BlockSpec((16, 1, 16, 1024), lambda i: (0, i, 0, 0)),
        cost_estimate=pl.CostEstimate(flops=0, bytes_accessed=12 * MIB, transcendentals=0),
    )(at, front_rows)


def add_pieces(value, slot_ref, c_ref, row, j):
    for child in range(2):
        slot = slot_ref[(row * 4 + j) * 2 + child]
        known = jnp.maximum(slot, 0)
        piece = c_ref[known // 6, lax.rem(known, 6)].astype(F32)
        value = value + jnp.where(slot >= 0, piece, F32(0))
    return value


def join_top_kernel(slot_ref, c_ref, o_ref):
    for i in range(2):
        for j in range(4):
            at = 6 + i * 4 + j % 2 * 2
            value = c_ref[j // 2, at].astype(F32) + c_ref[j // 2, at + 1].astype(F32)
            o_ref[i, :, j * 256 : (j + 1) * 256] = add_pieces(value, slot_ref, c_ref, i, j)


def join_low_kernel(slot_ref, c_ref, f_ref, o_ref):
    for i in range(6):
        for j in range(4):
            lanes = slice(j * 256, (j + 1) * 256)
            o_ref[i, :, lanes] = add_pieces(f_ref[i, :, lanes], slot_ref, c_ref, i + 2, j)


def join_strips(kernel, count, slots, *operands):
    return pl.pallas_call(
        kernel,
        out_shape=jax.ShapeDtypeStruct((count, 16, 1024), F32),
        in_specs=[SMEM] + [VMEM] * len(operands),
        out_specs=VMEM,
        cost_estimate=pl.CostEstimate(flops=0, bytes_accessed=3 * MIB, transcendentals=0),
    )(slots, *operands)


def solve_first_kernel(keep_ref, d_ref, r_ref, w_ref, o_ref):
    width = w_ref.shape[0]
    b = jnp.concatenate(
        [d_ref[:, :, :width].reshape(32, width), r_ref[:, :, :width].reshape(96, width)], axis=0
    )
    x = dot3(b, w_ref[...], NT).reshape(8, 16, width)
    for i in range(8):
        o_ref[i] = jnp.where(keep_ref[i] > 0, x[i], F32(0)).astype(BF16)


def solve_second_kernel(keep_ref, d_ref, r_ref, p_ref, p10_ref, w_ref, o_ref):
    width = w_ref.shape[0]
    half = width // 2
    b = jnp.concatenate(
        [d_ref[:, :, width:].reshape(32, width), r_ref[:, :, width:].reshape(96, width)], axis=0
    )
    u = dot1(p_ref[...].reshape(128, width), p10_ref[...], NT)
    rows = []
    for i in range(8):
        s = slice(16 * i, 16 * i + 16)
        parts = []
        for j in range(2):
            c = slice(j * half, (j + 1) * half)
            parts.append(b[s, c] - jnp.where(keep_ref[8 + 2 * i + j] > 0, u[s, c], F32(0)))
        rows.append(jnp.concatenate(parts, axis=1))
    x = dot3(jnp.concatenate(rows, axis=0), w_ref[...], NT).reshape(8, 16, width)
    for i in range(8):
        o_ref[i] = jnp.where(keep_ref[i] > 0, x[i], F32(0)).astype(BF16)


def solve_strips(kernel, *operands):
    return pl.pallas_call(
        kernel,
        out_shape=jax.ShapeDtypeStruct((8, 16, 512), BF16),
        in_specs=[SMEM] + [VMEM] * (len(operands) - 1),
        out_specs=VMEM,
        cost_estimate=pl.CostEstimate(flops=400_000_000, bytes_accessed=2 * MIB, transcendentals=0),
    )(*operands)


def deal_kernel(at_ref, p0_ref, p1_ref, *refs):
    o_ref = refs[-1]
    for q in range(16):
        o_ref[q, 0:8] = p0_ref[...]
        o_ref[q, 8:16] = p1_ref[...]
    for panel in range(2):
        for k in range(4):
            row = lax.rem(at_ref[2] + k, 4) * 2
            for c in range(2):
                for lr in range(4):
                    o_ref[(lr % 2) * 8 + row + c, 16 + panel * 2 + lr // 2] = refs[panel * 4 + k][c, lr]


def deal(at, P0, P1, first, second):
    return pl.pallas_call(
        deal_kernel,
        out_shape=jax.ShapeDtypeStruct((16, 20, 16, 512), BF16),
        in_specs=[SMEM] + [VMEM] * 10,
        out_specs=VMEM,
        cost_estimate=pl.CostEstimate(flops=0, bytes_accessed=8 * MIB, transcendentals=0),
        compiler_params=pltpu.CompilerParams(vmem_limit_bytes=24 * MIB),
    )(at, P0, P1, *first, *second)


def extend_kernel(slot_ref, f_ref, *refs):
    child, o_ref = refs[:8], refs[8]
    i = pl.program_id(0)
    for j in range(4):
        live = [slot_ref[(i * 4 + j) * 2 + ch] >= 0 for ch in range(2)]
        pieces = [child[j * 2 + ch] for ch in range(2)]
        for c in range(2):
            lanes = slice(c * 128, (c + 1) * 128)
            rows = pl.ds(j * 2 + c, 256, stride=8)
            value = f_ref[rows, :]
            for ch in range(2):
                value = value + jnp.where(live[ch], pieces[ch][0, :, lanes].astype(F32), F32(0))
            o_ref[rows, :] = value


def extend(slots, front_rows, arrived):
    def child_spec(k):
        return pl.BlockSpec((1, 256, 256), lambda i, s: (jnp.maximum(s[i * 8 + k], 0), 0, 0))

    return pl.pallas_call(
        extend_kernel,
        grid_spec=pltpu.PrefetchScalarGridSpec(
            num_scalar_prefetch=1,
            grid=(8,),
            in_specs=[pl.BlockSpec((2048, 128), lambda i, s: (i, 0))] + [child_spec(k) for k in range(8)],
            out_specs=pl.BlockSpec((2048, 128), lambda i, s: (i, 0)),
        ),
        out_shape=jax.ShapeDtypeStruct(front_rows.shape, F32),
        cost_estimate=pl.CostEstimate(flops=0, bytes_accessed=24 * MIB, transcendentals=0),
        compiler_params=pltpu.CompilerParams(vmem_limit_bytes=24 * MIB),
    )(slots, front_rows, *([arrived] * 8))


def finish_kernel(flag_ref, f_ref, row0_ref, row1_ref, mine_ref, other_ref, l_ref, w_ref, o_ref, cols_ref):
    i = pl.program_id(0)

    @pl.when(i == 0)
    def _():
        core = flag_ref[48]
        for ref, sub in ((mine_ref, core), (other_ref, 1 - core)):
            for panel in range(2):
                for lc in range(2):
                    strips = ref[:, panel * 2 + lc].reshape(256, 512)
                    cols_ref[lc * 2 + sub, :, panel * 512 : (panel + 1) * 512] = strips

    rows = jnp.concatenate([ref[:, 0].reshape(256, 512) for ref in (row0_ref, row1_ref)], axis=1)
    for lc in range(2):
        state = flag_ref[32 + i * 2 + lc]

        @pl.when(state > 0)
        def _():
            blocks = []
            for sc in range(2):
                j = lc * 2 + sc
                value = jnp.concatenate(
                    [f_ref[pl.ds(lc * 4 + sc * 2 + c, 256, stride=8), :] for c in range(2)], axis=1
                )
                product = dot1(rows, cols_ref[j], NT)
                blocks.append(value - jnp.where(flag_ref[i * 4 + j] > 0, product, F32(0)))
            block = jnp.concatenate(blocks, axis=1)

            def put(value):
                for c in range(4):
                    o_ref[pl.ds(lc * 4 + c, 256, stride=8), :] = value[:, c * 128 : (c + 1) * 128]

            @pl.when(state == 1)
            def _():
                put(block)

            if lc == 0:

                @pl.when(state == 2)
                def _():
                    put(dot3(block, w_ref[...], NT))

                @pl.when(state == 3)
                def _():
                    put(l_ref[pl.ds(pl.multiple_of(lax.rem(i, 2) * 256, 256), 256), :])

        @pl.when(state == 0)
        def _():
            for c in range(4):
                o_ref[pl.ds(lc * 4 + c, 256, stride=8), :] = jnp.zeros((256, 128), F32)


def finish(flags, extended, dealt, other, L, W):
    def whole(shape, *at):
        return pl.BlockSpec(shape, lambda i, f: at)

    return pl.pallas_call(
        finish_kernel,
        grid_spec=pltpu.PrefetchScalarGridSpec(
            num_scalar_prefetch=1,
            grid=(8,),
            in_specs=[pl.BlockSpec((2048, 128), lambda i, f: (i, 0))]
            + [pl.BlockSpec((16, 1, 16, 512), lambda i, f: (0, i, 0, 0))]
            + [pl.BlockSpec((16, 1, 16, 512), lambda i, f: (0, i + 8, 0, 0))]
            + [whole((16, 4, 16, 512), 0, 4, 0, 0), whole((16, 4, 16, 512), 0, 0, 0, 0)]
            + [whole((512, 512), 0, 0)] * 2,
            out_specs=pl.BlockSpec((2048, 128), lambda i, f: (i, 0)),
            scratch_shapes=[pltpu.VMEM((4, 256, 1024), BF16)],
        ),
        out_shape=jax.ShapeDtypeStruct(extended.shape, F32),
        cost_estimate=pl.CostEstimate(flops=5_000_000_000, bytes_accessed=24 * MIB, transcendentals=0),
        compiler_params=pltpu.CompilerParams(vmem_limit_bytes=48 * MIB),
    )(flags, extended, dealt, dealt, dealt, other, L, W)


def slot_of_targets(codes, row_map, rows, cols):
    index = jnp.arange(CNB, dtype=jnp.int32)

    def place(blocks):
        hit = row_map[None] == blocks[:, None, None]
        return jnp.sum(jnp.where(hit, index + 1, 0), axis=-1) - 1

    pi, pj = place(rows), place(cols)
    child = jnp.arange(2, dtype=jnp.int32) * (CNB * CNB)
    wanted = child + pi[:, None, :] * CNB + pj[None, :, :]
    known = (pi[:, None, :] >= 0) & (pj[None, :, :] >= 0)
    wanted = jnp.where(known, wanted, -2).reshape(-1)
    number = jnp.arange(codes.shape[0], dtype=jnp.int32)
    return jnp.sum(jnp.where(wanted[:, None] == codes[None, :], number + 1, 0), axis=-1) - 1


def spread(x, axis, count):
    return lax.all_to_all(jnp.broadcast_to(x[None], (count,) + x.shape), axis, 0, 0, tiled=True)


def local(front, child_blocks, row_map, slot_table, struct_mask):
    prow, pcol = lax.axis_size("prow"), lax.axis_size("pcol")
    p, q = lax.axis_index("prow"), lax.axis_index("pcol")
    core, y = p % 2, p // 2
    at = jnp.stack([core, q, y]).astype(jnp.int32)
    swap = [(i, i ^ 1) for i in range(8)]
    front_rows = front.reshape(16384, 128)
    child = child_blocks[0, 0]

    pair = jnp.arange(2, dtype=jnp.int32)
    row_blocks = jnp.arange(4, dtype=jnp.int32) * prow + p
    col_blocks = jnp.arange(2, dtype=jnp.int32) * pcol + q
    sub_rows = (2 * row_blocks[:, None] + pair).reshape(-1)
    sub_cols = (2 * col_blocks[:, None] + pair).reshape(-1)

    cut = cut_top(front_rows, child.reshape(48, 256, 256))
    got = lax.all_to_all(cut, "pcol", 0, 0, tiled=True)
    front_rows, _ = lax.optimization_barrier((front_rows, cut))
    low_front = lax.psum_scatter(
        cut_low(at, front_rows).reshape(96, 16, 1024), "pcol", scatter_dimension=0, tiled=True
    )

    my_codes = lax.dynamic_index_in_dim(slot_table, p, 0, False)
    strip_slots = slot_of_targets(my_codes[:, :2].reshape(-1), row_map, sub_rows, jnp.arange(4, dtype=jnp.int32))
    slots = slot_of_targets(
        lax.dynamic_index_in_dim(my_codes, q, 1, False).reshape(-1), row_map, sub_rows, sub_cols
    )
    row_mask = struct_mask[sub_rows]
    lower = row_blocks[:, None] >= col_blocks[None, :]
    mask = row_mask[:, sub_cols]
    state = jnp.where(lower, 1, 0)
    owner = (q < 2) & (jnp.arange(2) == 0)
    state = jnp.where(owner[None, :] & lower, jnp.where(row_blocks[:, None] == q, 3, 2), state)
    flags = jnp.concatenate([mask.reshape(-1), jnp.repeat(state, 2, axis=0).reshape(-1), core.reshape(1)])
    flags = flags.astype(jnp.int32)
    keep0 = (sub_rows >= 2).astype(jnp.int32)
    keep1 = jnp.concatenate([(sub_rows >= 4).astype(jnp.int32), row_mask[:, 2:4].reshape(-1)])

    top = join_strips(join_top_kernel, 2, strip_slots, got)

    half_top = lax.all_to_all(jnp.tile(top, (prow // 2, 1, 1)), "prow", 0, 0, tiled=True)
    first = spread(jnp.concatenate([half_top[0, :, :512], half_top[1]], axis=1), "pcol", pcol)
    diag = (first, lax.ppermute(first, "prow", swap))
    child, diag, low_front = lax.optimization_barrier((child, diag, low_front))
    arrived = lax.all_to_all(child, "pcol", 0, 0, tiled=True).reshape(48, 256, 256)

    def gather_columns(strips):
        halves = strips.reshape(4, 2, 16, 512)
        even, odd = halves[:, 0], halves[:, 1]
        sent = lax.ppermute(jnp.where(core == 0, odd, even), "prow", swap)
        kept = jnp.where(core == 0, even, odd)
        chip = jnp.where(core == 0, jnp.stack([kept, sent]), jnp.stack([sent, kept]))
        along = lambda k: [(2 * ((i + k) % 4) + c, 2 * i + c) for i in range(4) for c in range(2)]
        return [chip] + [lax.ppermute(chip, "prow", along(k)) for k in range(1, 4)]

    L0, W0 = factor_first(at, *diag)
    low = join_strips(join_low_kernel, 6, strip_slots, got, low_front)
    P0 = solve_strips(solve_first_kernel, keep0, top, low, W0)
    P0, diag = lax.optimization_barrier((P0, diag))
    cols0 = gather_columns(P0)
    P10, L1, W1 = factor_second(at, struct_mask[2:4, 2:4].reshape(-1), *diag, W0)
    W1, cols0 = lax.optimization_barrier((W1, cols0))
    P1 = solve_strips(solve_second_kernel, keep1, top, low, P0, P10, W1)
    cols1 = gather_columns(P1)

    dealt = deal(at, P0, P1, cols0, cols1)
    dealt, arrived = lax.optimization_barrier((dealt, arrived))
    dealt = lax.all_to_all(dealt, "pcol", 0, 0, tiled=True)
    extended = extend(slots, front_rows, arrived)
    dealt, extended = lax.optimization_barrier((dealt, extended))
    other = lax.ppermute(dealt[:, 16:], "prow", swap)

    L = jnp.where(q == 0, L0, L1)
    W = jnp.where(q == 0, W0, W1)
    out = finish(flags, extended, dealt, other, L, W)
    return out.reshape(front.shape)


def solution(mesh):
    in_specs = (
        P(None, "prow", None, None, "pcol", None),
        P("prow", "pcol", None, None, None, None),
        P(),
        P(),
        P(),
    )
    out_specs = P(None, "prow", None, None, "pcol", None)
    return jax.shard_map(local, mesh=mesh, in_specs=in_specs, out_specs=out_specs, check_vma=False)
```

```python
import functools

import jax
import jax.numpy as jnp
from jax import lax
from jax.experimental import pallas as pl
from jax.experimental.pallas import tpu as pltpu
from jax.sharding import PartitionSpec as P

F32 = jnp.float32
BF16 = jnp.bfloat16
CNB = 60
NN = (((1,), (0,)), ((), ()))
NT = (((1,), (1,)), ((), ()))
MIB = 2**20
VMEM = pl.BlockSpec(memory_space=pltpu.VMEM)
SMEM = pl.BlockSpec(memory_space=pltpu.SMEM)


def split(x):
    high = x.astype(BF16)
    return high, (x - high.astype(F32)).astype(BF16)


def dot1(a, b, dims):
    return lax.dot_general(a, b, dims, preferred_element_type=F32)


def dot3(a, b, dims):
    ah, al = split(a)
    bh, bl = split(b)
    return dot1(ah, bh, dims) + (dot1(al, bh, dims) + dot1(ah, bl, dims))


GROUPS = 4


def eliminate(R, n):
    row = lax.broadcasted_iota(jnp.int32, (8, 1), 0)
    across = lambda v: jnp.concatenate([v, v], axis=1)
    over = lambda x, lane: jnp.broadcast_to(x[:, lane : lane + 1], (8, 128))
    done = []
    for g in range(len(R)):
        base = 8 * g
        later = range(g + 1, len(R))
        cols = [over(R[g], base + j) for j in range(8)]
        below = {h: [over(R[h], base + j) for j in range(8)] for h in later}
        D = [[jnp.broadcast_to(cols[j][i : i + 1], (8, 128)) for j in range(i + 1)] for i in range(8)]
        Y = [jnp.broadcast_to(R[g][i : i + 1], (8, 2 * n)) for i in range(8)]
        out = None
        for j in range(8):
            scale = lax.rsqrt(D[j][j])
            inverse = scale * scale
            for i in range(j + 1, 8):
                factor = D[i][j] * inverse
                for m in range(j + 1, i):
                    D[i][m] = D[i][m] - factor * D[m][j]
                D[i][i] = D[i][i] - (D[i][j] * D[i][j]) * inverse
                Y[i] = Y[i] - across(factor) * Y[j]
            for h in later:
                factor = below[h][j] * inverse
                for m in range(j + 1, 8):
                    below[h][m] = below[h][m] - factor * D[m][j]
                R[h] = R[h] - across(factor) * Y[j]
            scaled = Y[j] * across(scale)
            out = scaled if out is None else jnp.where(row == j, scaled, out)
        done.append(out)
    return jnp.concatenate(done, axis=0)


def factor_base(m_ref, o_ref):
    n = m_ref.shape[0]
    step = 8 * GROUPS

    def body(k, _):
        at = k * step
        rows = pl.ds(pl.multiple_of(at, step), step)
        X = m_ref[rows, :]
        A = pltpu.roll(X[:, :n], jnp.where(k == 0, 0, n - at), 1)
        X = jnp.concatenate([A, X[:, n:]], axis=1)
        out = eliminate([X[8 * g : 8 * g + 8] for g in range(GROUPS)], n)
        out = jnp.concatenate([pltpu.roll(out[:, :n], at, 1), out[:, n:]], axis=1)
        o_ref[rows, :] = out
        m_ref[...] = m_ref[...] - dot3(out[:, :n].T, out, NN)
        return 0

    lax.fori_loop(0, n // step, body, 0)


def factor_whole(a_ref, l_ref, w_ref, m_ref, o_ref):
    n = a_ref.shape[0]
    b = 128
    w_ref[...] = jnp.zeros((n, n), F32)
    l_ref[...] = jnp.zeros((n, n), F32)
    lane = lax.broadcasted_iota(jnp.int32, (b, b), 1)
    sub = lax.broadcasted_iota(jnp.int32, (b, b), 0)
    for k in range(0, n, b):
        s = slice(k, k + b)
        D = a_ref[s, s]
        m_ref[:, :b] = jnp.where(sub >= lane, D, D.T)
        m_ref[:, b:] = jnp.where(lane == sub, F32(1), F32(0))
        factor_base(m_ref, o_ref)
        W = jnp.where(lane <= sub, o_ref[:, b:], F32(0))
        l_ref[s, s] = jnp.where(lane >= sub, o_ref[:, :b], F32(0)).T
        w_ref[s, s] = W
        if k:
            T = dot3(l_ref[s, :k], w_ref[:k, :k], NN)
            w_ref[s, :k] = -dot3(W, T, NN)
        if k + b < n:
            L = dot3(a_ref[k + b :, s], W, NT)
            l_ref[k + b :, s] = L
            for j in range(k + b, n, b):
                off = j - k - b
                a_ref[j:, j : j + b] = a_ref[j:, j : j + b] - dot3(L[off:], L[off : off + b], NT)


def factor_first_kernel(at_ref, mine_ref, other_ref, l_ref, w_ref, a_ref, m_ref, o_ref):
    n = a_ref.shape[0]
    for ref, sub in ((mine_ref, at_ref[0]), (other_ref, 1 - at_ref[0])):
        a_ref[pl.ds(pl.multiple_of(sub * 256, 256), 256), :] = ref[:, :, :n].reshape(256, n)
    factor_whole(a_ref, l_ref, w_ref, m_ref, o_ref)


def factor_second_kernel(
    at_ref, mask_ref, mine_ref, other_ref, w0_ref, p_ref, l_ref, w_ref, a_ref, m_ref, o_ref, b_ref
):
    n = a_ref.shape[0]
    for ref, sub in ((mine_ref, at_ref[0]), (other_ref, 1 - at_ref[0])):
        rows = pl.ds(pl.multiple_of(sub * 256, 256), 256)
        b_ref[rows, :] = ref[:, :, n : 2 * n].reshape(256, n)
        a_ref[rows, :] = ref[:, :, 2 * n :].reshape(256, n)
    panel = dot3(b_ref[...], w0_ref[...], NT).astype(BF16)
    p_ref[...] = panel
    h = n // 2
    for i in range(2):
        for j in range(i + 1):
            r, c = slice(i * h, (i + 1) * h), slice(j * h, (j + 1) * h)
            product = dot1(panel[r], panel[c], NT)
            a_ref[r, c] = a_ref[r, c] - jnp.where(mask_ref[i * 2 + j] > 0, product, F32(0))
    factor_whole(a_ref, l_ref, w_ref, m_ref, o_ref)


CHOL_COST = pl.CostEstimate(flops=20_000_000_000, bytes_accessed=3 * MIB, transcendentals=1024)


def factor_first(at, mine, other):
    n = mine.shape[-1] // 3
    return pl.pallas_call(
        factor_first_kernel,
        out_shape=[jax.ShapeDtypeStruct((n, n), F32)] * 2,
        in_specs=[SMEM, VMEM, VMEM],
        out_specs=[VMEM] * 2,
        scratch_shapes=[pltpu.VMEM((n, n), F32)] + [pltpu.VMEM((128, 256), F32)] * 2,
        cost_estimate=CHOL_COST,
        compiler_params=pltpu.CompilerParams(vmem_limit_bytes=40 * MIB),
    )(at, mine, other)


def factor_second(at, mask, mine, other, W0):
    n = W0.shape[0]
    return pl.pallas_call(
        factor_second_kernel,
        out_shape=[jax.ShapeDtypeStruct((n, n), BF16)] + [jax.ShapeDtypeStruct((n, n), F32)] * 2,
        in_specs=[SMEM, SMEM, VMEM, VMEM, VMEM],
        out_specs=[VMEM] * 3,
        scratch_shapes=[pltpu.VMEM((n, n), F32)]
        + [pltpu.VMEM((128, 256), F32)] * 2
        + [pltpu.VMEM((n, n), F32)],
        cost_estimate=CHOL_COST,
        compiler_params=pltpu.CompilerParams(vmem_limit_bytes=40 * MIB),
    )(at, mask, mine, other, W0)


def cut_kernel(x_ref, c_ref, o_ref):
    i = pl.program_id(0)

    @pl.when(i < 3)
    def _():
        for k in range(2):
            o_ref[:, k] = c_ref[k].reshape(16, 16, 256)

    for half in range(2):

        @pl.when((i >= 3) & (lax.rem(i, 2) == 1 - half))
        def _():
            for c in range(2):
                high, low = split(x_ref[pl.ds(half * 2 + c, 256, stride=8), :])
                lanes = slice(c * 128, c * 128 + 128)
                o_ref[:, 0, :, lanes] = high.reshape(16, 16, 128)
                o_ref[:, 1, :, lanes] = low.reshape(16, 16, 128)


def cut_strips(front_rows, child):
    return pl.pallas_call(
        cut_kernel,
        grid=(19,),
        out_shape=jax.ShapeDtypeStruct((16, 38, 16, 256), BF16),
        in_specs=[
            pl.BlockSpec((2048, 128), lambda i: (jnp.maximum(i - 3, 0) // 2, 0)),
            pl.BlockSpec((2, 256, 256), lambda i: (jnp.minimum(i, 2), 0, 0)),
        ],
        out_specs=pl.BlockSpec((16, 2, 16, 256), lambda i: (0, i, 0, 0)),
        cost_estimate=pl.CostEstimate(flops=0, bytes_accessed=14 * MIB, transcendentals=0),
    )(front_rows, child)


def add_pieces(value, slot_ref, c_ref, row, j):
    for child in range(2):
        slot = slot_ref[(row * 4 + j) * 2 + child]
        known = jnp.maximum(slot, 0)
        piece = c_ref[known // 6, lax.rem(known, 6)].astype(F32)
        value = value + jnp.where(slot >= 0, piece, F32(0))
    return value


def join_kernel(first, slot_ref, c_ref, f_ref, o_ref):
    for i in range(o_ref.shape[0]):
        for j in range(4):
            at = 6 + (i + first) * 4 + j % 2 * 2
            value = f_ref[j // 2, at].astype(F32) + f_ref[j // 2, at + 1].astype(F32)
            o_ref[i, :, j * 256 : (j + 1) * 256] = add_pieces(value, slot_ref, c_ref, i + first, j)


def join_strips(first, count, slots, got):
    return pl.pallas_call(
        functools.partial(join_kernel, first),
        grid=(1,),
        out_shape=jax.ShapeDtypeStruct((count, 16, 1024), F32),
        in_specs=[
            SMEM,
            pl.BlockSpec((16, 6, 16, 256), lambda i: (0, 0, 0, 0)),
            pl.BlockSpec((2, 38, 16, 256), lambda i: (0, 0, 0, 0)),
        ],
        out_specs=pl.BlockSpec((count, 16, 1024), lambda i: (0, 0, 0)),
        cost_estimate=pl.CostEstimate(flops=0, bytes_accessed=3 * MIB, transcendentals=0),
    )(slots, got, got)


def solve_first_kernel(keep_ref, d_ref, r_ref, w_ref, o_ref):
    width = w_ref.shape[0]
    b = jnp.concatenate(
        [d_ref[:, :, :width].reshape(32, width), r_ref[:, :, :width].reshape(96, width)], axis=0
    )
    x = dot3(b, w_ref[...], NT).reshape(8, 16, width)
    for i in range(8):
        o_ref[i] = jnp.where(keep_ref[i] > 0, x[i], F32(0)).astype(BF16)


def solve_second_kernel(keep_ref, d_ref, r_ref, p_ref, p10_ref, w_ref, o_ref):
    width = w_ref.shape[0]
    half = width // 2
    b = jnp.concatenate(
        [d_ref[:, :, width:].reshape(32, width), r_ref[:, :, width:].reshape(96, width)], axis=0
    )
    u = dot1(p_ref[...].reshape(128, width), p10_ref[...], NT)
    rows = []
    for i in range(8):
        s = slice(16 * i, 16 * i + 16)
        parts = []
        for j in range(2):
            c = slice(j * half, (j + 1) * half)
            parts.append(b[s, c] - jnp.where(keep_ref[8 + 2 * i + j] > 0, u[s, c], F32(0)))
        rows.append(jnp.concatenate(parts, axis=1))
    x = dot3(jnp.concatenate(rows, axis=0), w_ref[...], NT).reshape(8, 16, width)
    for i in range(8):
        o_ref[i] = jnp.where(keep_ref[i] > 0, x[i], F32(0)).astype(BF16)


def solve_strips(kernel, *operands):
    return pl.pallas_call(
        kernel,
        out_shape=jax.ShapeDtypeStruct((8, 16, 512), BF16),
        in_specs=[SMEM] + [VMEM] * (len(operands) - 1),
        out_specs=VMEM,
        cost_estimate=pl.CostEstimate(flops=400_000_000, bytes_accessed=2 * MIB, transcendentals=0),
    )(*operands)


def deal_kernel(at_ref, p0_ref, p1_ref, *refs):
    o_ref = refs[-1]
    for q in range(16):
        o_ref[q, 0:8] = p0_ref[...]
        o_ref[q, 8:16] = p1_ref[...]
    for panel in range(2):
        for k in range(4):
            row = lax.rem(at_ref[2] + k, 4) * 2
            for c in range(2):
                for lr in range(4):
                    o_ref[(lr % 2) * 8 + row + c, 16 + panel * 2 + lr // 2] = refs[panel * 4 + k][c, lr]


def deal(at, P0, P1, first, second):
    return pl.pallas_call(
        deal_kernel,
        out_shape=jax.ShapeDtypeStruct((16, 20, 16, 512), BF16),
        in_specs=[SMEM] + [VMEM] * 10,
        out_specs=VMEM,
        cost_estimate=pl.CostEstimate(flops=0, bytes_accessed=8 * MIB, transcendentals=0),
        compiler_params=pltpu.CompilerParams(vmem_limit_bytes=24 * MIB),
    )(at, P0, P1, *first, *second)


def extend_kernel(slot_ref, f_ref, *refs):
    child, o_ref = refs[:8], refs[8]
    i = pl.program_id(0)
    for j in range(4):
        live = [slot_ref[(i * 4 + j) * 2 + ch] >= 0 for ch in range(2)]
        pieces = [child[j * 2 + ch] for ch in range(2)]
        for c in range(2):
            lanes = slice(c * 128, (c + 1) * 128)
            rows = pl.ds(j * 2 + c, 256, stride=8)
            value = f_ref[rows, :]
            for ch in range(2):
                value = value + jnp.where(live[ch], pieces[ch][0, :, lanes].astype(F32), F32(0))
            o_ref[rows, :] = value


def extend(slots, front_rows, arrived):
    def child_spec(k):
        return pl.BlockSpec((1, 256, 256), lambda i, s: (jnp.maximum(s[i * 8 + k], 0), 0, 0))

    return pl.pallas_call(
        extend_kernel,
        grid_spec=pltpu.PrefetchScalarGridSpec(
            num_scalar_prefetch=1,
            grid=(8,),
            in_specs=[pl.BlockSpec((2048, 128), lambda i, s: (i, 0))] + [child_spec(k) for k in range(8)],
            out_specs=pl.BlockSpec((2048, 128), lambda i, s: (i, 0)),
        ),
        out_shape=jax.ShapeDtypeStruct(front_rows.shape, F32),
        cost_estimate=pl.CostEstimate(flops=0, bytes_accessed=24 * MIB, transcendentals=0),
        compiler_params=pltpu.CompilerParams(vmem_limit_bytes=24 * MIB),
    )(slots, front_rows, *([arrived] * 8))


def finish_kernel(flag_ref, f_ref, row0_ref, row1_ref, mine_ref, other_ref, l_ref, w_ref, o_ref, cols_ref):
    i = pl.program_id(0)

    @pl.when(i == 0)
    def _():
        core = flag_ref[48]
        for ref, sub in ((mine_ref, core), (other_ref, 1 - core)):
            for panel in range(2):
                for lc in range(2):
                    strips = ref[:, panel * 2 + lc].reshape(256, 512)
                    cols_ref[lc * 2 + sub, :, panel * 512 : (panel + 1) * 512] = strips

    rows = jnp.concatenate([ref[:, 0].reshape(256, 512) for ref in (row0_ref, row1_ref)], axis=1)
    for lc in range(2):
        state = flag_ref[32 + i * 2 + lc]

        @pl.when(state > 0)
        def _():
            blocks = []
            for sc in range(2):
                j = lc * 2 + sc
                value = jnp.concatenate(
                    [f_ref[pl.ds(lc * 4 + sc * 2 + c, 256, stride=8), :] for c in range(2)], axis=1
                )
                product = dot1(rows, cols_ref[j], NT)
                blocks.append(value - jnp.where(flag_ref[i * 4 + j] > 0, product, F32(0)))
            block = jnp.concatenate(blocks, axis=1)

            def put(value):
                for c in range(4):
                    o_ref[pl.ds(lc * 4 + c, 256, stride=8), :] = value[:, c * 128 : (c + 1) * 128]

            @pl.when(state == 1)
            def _():
                put(block)

            if lc == 0:

                @pl.when(state == 2)
                def _():
                    put(dot3(block, w_ref[...], NT))

                @pl.when(state == 3)
                def _():
                    put(l_ref[pl.ds(pl.multiple_of(lax.rem(i, 2) * 256, 256), 256), :])

        @pl.when(state == 0)
        def _():
            for c in range(4):
                o_ref[pl.ds(lc * 4 + c, 256, stride=8), :] = jnp.zeros((256, 128), F32)


def finish(flags, extended, dealt, other, L, W):
    def whole(shape, *at):
        return pl.BlockSpec(shape, lambda i, f: at)

    return pl.pallas_call(
        finish_kernel,
        grid_spec=pltpu.PrefetchScalarGridSpec(
            num_scalar_prefetch=1,
            grid=(8,),
            in_specs=[pl.BlockSpec((2048, 128), lambda i, f: (i, 0))]
            + [pl.BlockSpec((16, 1, 16, 512), lambda i, f: (0, i, 0, 0))]
            + [pl.BlockSpec((16, 1, 16, 512), lambda i, f: (0, i + 8, 0, 0))]
            + [whole((16, 4, 16, 512), 0, 4, 0, 0), whole((16, 4, 16, 512), 0, 0, 0, 0)]
            + [whole((512, 512), 0, 0)] * 2,
            out_specs=pl.BlockSpec((2048, 128), lambda i, f: (i, 0)),
            scratch_shapes=[pltpu.VMEM((4, 256, 1024), BF16)],
        ),
        out_shape=jax.ShapeDtypeStruct(extended.shape, F32),
        cost_estimate=pl.CostEstimate(flops=5_000_000_000, bytes_accessed=24 * MIB, transcendentals=0),
        compiler_params=pltpu.CompilerParams(vmem_limit_bytes=48 * MIB),
    )(flags, extended, dealt, dealt, dealt, other, L, W)


def slot_of_targets(codes, row_map, rows, cols):
    index = jnp.arange(CNB, dtype=jnp.int32)

    def place(blocks):
        hit = row_map[None] == blocks[:, None, None]
        return jnp.sum(jnp.where(hit, index + 1, 0), axis=-1) - 1

    pi, pj = place(rows), place(cols)
    child = jnp.arange(2, dtype=jnp.int32) * (CNB * CNB)
    wanted = child + pi[:, None, :] * CNB + pj[None, :, :]
    known = (pi[:, None, :] >= 0) & (pj[None, :, :] >= 0)
    wanted = jnp.where(known, wanted, -2).reshape(-1)
    number = jnp.arange(codes.shape[0], dtype=jnp.int32)
    return jnp.sum(jnp.where(wanted[:, None] == codes[None, :], number + 1, 0), axis=-1) - 1


def spread(x, axis, count):
    return lax.all_to_all(jnp.broadcast_to(x[None], (count,) + x.shape), axis, 0, 0, tiled=True)


def local(front, child_blocks, row_map, slot_table, struct_mask):
    prow, pcol = lax.axis_size("prow"), lax.axis_size("pcol")
    p, q = lax.axis_index("prow"), lax.axis_index("pcol")
    core, y = p % 2, p // 2
    at = jnp.stack([core, q, y]).astype(jnp.int32)
    swap = [(i, i ^ 1) for i in range(8)]
    front_rows = front.reshape(16384, 128)
    child = child_blocks[0, 0]

    pair = jnp.arange(2, dtype=jnp.int32)
    row_blocks = jnp.arange(4, dtype=jnp.int32) * prow + p
    col_blocks = jnp.arange(2, dtype=jnp.int32) * pcol + q
    sub_rows = (2 * row_blocks[:, None] + pair).reshape(-1)
    sub_cols = (2 * col_blocks[:, None] + pair).reshape(-1)

    got = lax.all_to_all(cut_strips(front_rows, child.reshape(48, 256, 256)), "pcol", 0, 0, tiled=True)

    my_codes = lax.dynamic_index_in_dim(slot_table, p, 0, False)
    strip_slots = slot_of_targets(my_codes[:, :2].reshape(-1), row_map, sub_rows, jnp.arange(4, dtype=jnp.int32))
    slots = slot_of_targets(
        lax.dynamic_index_in_dim(my_codes, q, 1, False).reshape(-1), row_map, sub_rows, sub_cols
    )
    row_mask = struct_mask[sub_rows]
    lower = row_blocks[:, None] >= col_blocks[None, :]
    mask = row_mask[:, sub_cols]
    state = jnp.where(lower, 1, 0)
    owner = (q < 2) & (jnp.arange(2) == 0)
    state = jnp.where(owner[None, :] & lower, jnp.where(row_blocks[:, None] == q, 3, 2), state)
    flags = jnp.concatenate([mask.reshape(-1), jnp.repeat(state, 2, axis=0).reshape(-1), core.reshape(1)])
    flags = flags.astype(jnp.int32)
    keep0 = (sub_rows >= 2).astype(jnp.int32)
    keep1 = jnp.concatenate([(sub_rows >= 4).astype(jnp.int32), row_mask[:, 2:4].reshape(-1)])

    top = join_strips(0, 2, strip_slots, got)

    half_top = lax.all_to_all(jnp.tile(top, (prow // 2, 1, 1)), "prow", 0, 0, tiled=True)
    first = spread(jnp.concatenate([half_top[0, :, :512], half_top[1]], axis=1), "pcol", pcol)
    diag = (first, lax.ppermute(first, "prow", swap))
    child, diag = lax.optimization_barrier((child, diag))
    arrived = lax.all_to_all(child, "pcol", 0, 0, tiled=True).reshape(48, 256, 256)

    def gather_columns(strips):
        halves = strips.reshape(4, 2, 16, 512)
        even, odd = halves[:, 0], halves[:, 1]
        sent = lax.ppermute(jnp.where(core == 0, odd, even), "prow", swap)
        kept = jnp.where(core == 0, even, odd)
        chip = jnp.where(core == 0, jnp.stack([kept, sent]), jnp.stack([sent, kept]))
        along = lambda k: [(2 * ((i + k) % 4) + c, 2 * i + c) for i in range(4) for c in range(2)]
        return [chip] + [lax.ppermute(chip, "prow", along(k)) for k in range(1, 4)]

    L0, W0 = factor_first(at, *diag)
    low = join_strips(2, 6, strip_slots, got)
    P0 = solve_strips(solve_first_kernel, keep0, top, low, W0)
    P0, diag = lax.optimization_barrier((P0, diag))
    cols0 = gather_columns(P0)
    P10, L1, W1 = factor_second(at, struct_mask[2:4, 2:4].reshape(-1), *diag, W0)
    W1, cols0 = lax.optimization_barrier((W1, cols0))
    P1 = solve_strips(solve_second_kernel, keep1, top, low, P0, P10, W1)
    cols1 = gather_columns(P1)

    dealt = deal(at, P0, P1, cols0, cols1)
    dealt, arrived = lax.optimization_barrier((dealt, arrived))
    dealt = lax.all_to_all(dealt, "pcol", 0, 0, tiled=True)
    extended = extend(slots, front_rows, arrived)
    L = jnp.where(q == 0, L0, L1)
    W = jnp.where(q == 0, W0, W1)
    dealt, extended, L, W = lax.optimization_barrier((dealt, extended, L, W))
    other = lax.ppermute(dealt[:, 16:], "prow", swap)

    out = finish(flags, extended, dealt, other, L, W)
    return out.reshape(front.shape)


def solution(mesh):
    in_specs = (
        P(None, "prow", None, None, "pcol", None),
        P("prow", "pcol", None, None, None, None),
        P(),
        P(),
        P(),
    )
    out_specs = P(None, "prow", None, None, "pcol", None)
    return jax.shard_map(local, mesh=mesh, in_specs=in_specs, out_specs=out_specs, check_vma=False)
```

```python
import functools

import jax
import jax.numpy as jnp
from jax import lax
from jax.experimental import pallas as pl
from jax.experimental.pallas import tpu as pltpu
from jax.sharding import PartitionSpec as P

F32 = jnp.float32
BF16 = jnp.bfloat16
CNB = 60
NN = (((1,), (0,)), ((), ()))
NT = (((1,), (1,)), ((), ()))
MIB = 2**20
VMEM = pl.BlockSpec(memory_space=pltpu.VMEM)
SMEM = pl.BlockSpec(memory_space=pltpu.SMEM)


def split(x):
    high = x.astype(BF16)
    return high, (x - high.astype(F32)).astype(BF16)


def dot1(a, b, dims):
    return lax.dot_general(a, b, dims, preferred_element_type=F32)


def dot3(a, b, dims):
    ah, al = split(a)
    bh, bl = split(b)
    return dot1(ah, bh, dims) + (dot1(al, bh, dims) + dot1(ah, bl, dims))


GROUPS = 4


def eliminate(R, n):
    row = lax.broadcasted_iota(jnp.int32, (8, 1), 0)
    across = lambda v: jnp.concatenate([v, v], axis=1)
    over = lambda x, lane: jnp.broadcast_to(x[:, lane : lane + 1], (8, 128))
    done = []
    for g in range(len(R)):
        base = 8 * g
        later = range(g + 1, len(R))
        cols = [over(R[g], base + j) for j in range(8)]
        below = {h: [over(R[h], base + j) for j in range(8)] for h in later}
        D = [[jnp.broadcast_to(cols[j][i : i + 1], (8, 128)) for j in range(i + 1)] for i in range(8)]
        Y = [jnp.broadcast_to(R[g][i : i + 1], (8, 2 * n)) for i in range(8)]
        out = None
        for j in range(8):
            scale = lax.rsqrt(D[j][j])
            inverse = scale * scale
            for i in range(j + 1, 8):
                factor = D[i][j] * inverse
                for m in range(j + 1, i):
                    D[i][m] = D[i][m] - factor * D[m][j]
                D[i][i] = D[i][i] - (D[i][j] * D[i][j]) * inverse
                Y[i] = Y[i] - across(factor) * Y[j]
            for h in later:
                factor = below[h][j] * inverse
                for m in range(j + 1, 8):
                    below[h][m] = below[h][m] - factor * D[m][j]
                R[h] = R[h] - across(factor) * Y[j]
            scaled = Y[j] * across(scale)
            out = scaled if out is None else jnp.where(row == j, scaled, out)
        done.append(out)
    return jnp.concatenate(done, axis=0)


def factor_base(m_ref, o_ref):
    n = m_ref.shape[0]
    step = 8 * GROUPS

    def body(k, _):
        at = k * step
        rows = pl.ds(pl.multiple_of(at, step), step)
        X = m_ref[rows, :]
        A = pltpu.roll(X[:, :n], jnp.where(k == 0, 0, n - at), 1)
        X = jnp.concatenate([A, X[:, n:]], axis=1)
        out = eliminate([X[8 * g : 8 * g + 8] for g in range(GROUPS)], n)
        out = jnp.concatenate([pltpu.roll(out[:, :n], at, 1), out[:, n:]], axis=1)
        o_ref[rows, :] = out
        m_ref[...] = m_ref[...] - dot3(out[:, :n].T, out, NN)
        return 0

    lax.fori_loop(0, n // step, body, 0)


def factor_whole(a_ref, l_ref, w_ref, m_ref, o_ref):
    n = a_ref.shape[0]
    b = 128
    w_ref[...] = jnp.zeros((n, n), F32)
    l_ref[...] = jnp.zeros((n, n), F32)
    lane = lax.broadcasted_iota(jnp.int32, (b, b), 1)
    sub = lax.broadcasted_iota(jnp.int32, (b, b), 0)
    for k in range(0, n, b):
        s = slice(k, k + b)
        D = a_ref[s, s]
        m_ref[:, :b] = jnp.where(sub >= lane, D, D.T)
        m_ref[:, b:] = jnp.where(lane == sub, F32(1), F32(0))
        factor_base(m_ref, o_ref)
        W = jnp.where(lane <= sub, o_ref[:, b:], F32(0))
        l_ref[s, s] = jnp.where(lane >= sub, o_ref[:, :b], F32(0)).T
        w_ref[s, s] = W
        if k:
            T = dot3(l_ref[s, :k], w_ref[:k, :k], NN)
            w_ref[s, :k] = -dot3(W, T, NN)
        if k + b < n:
            L = dot3(a_ref[k + b :, s], W, NT)
            l_ref[k + b :, s] = L
            for j in range(k + b, n, b):
                off = j - k - b
                a_ref[j:, j : j + b] = a_ref[j:, j : j + b] - dot3(L[off:], L[off : off + b], NT)


def factor_first_kernel(at_ref, mine_ref, other_ref, l_ref, w_ref, a_ref, m_ref, o_ref):
    n = a_ref.shape[0]
    for ref, sub in ((mine_ref, at_ref[0]), (other_ref, 1 - at_ref[0])):
        a_ref[pl.ds(pl.multiple_of(sub * 256, 256), 256), :] = ref[:, :, :n].reshape(256, n)
    factor_whole(a_ref, l_ref, w_ref, m_ref, o_ref)


def factor_second_kernel(
    at_ref, mask_ref, mine_ref, other_ref, w0_ref, p_ref, l_ref, w_ref, a_ref, m_ref, o_ref, b_ref
):
    n = a_ref.shape[0]
    for ref, sub in ((mine_ref, at_ref[0]), (other_ref, 1 - at_ref[0])):
        rows = pl.ds(pl.multiple_of(sub * 256, 256), 256)
        b_ref[rows, :] = ref[:, :, n : 2 * n].reshape(256, n)
        a_ref[rows, :] = ref[:, :, 2 * n :].reshape(256, n)
    panel = dot3(b_ref[...], w0_ref[...], NT).astype(BF16)
    p_ref[...] = panel
    h = n // 2
    for i in range(2):
        for j in range(i + 1):
            r, c = slice(i * h, (i + 1) * h), slice(j * h, (j + 1) * h)
            product = dot1(panel[r], panel[c], NT)
            a_ref[r, c] = a_ref[r, c] - jnp.where(mask_ref[i * 2 + j] > 0, product, F32(0))
    factor_whole(a_ref, l_ref, w_ref, m_ref, o_ref)


CHOL_COST = pl.CostEstimate(flops=20_000_000_000, bytes_accessed=3 * MIB, transcendentals=1024)


def factor_first(at, mine, other):
    n = mine.shape[-1] // 3
    return pl.pallas_call(
        factor_first_kernel,
        out_shape=[jax.ShapeDtypeStruct((n, n), F32)] * 2,
        in_specs=[SMEM, VMEM, VMEM],
        out_specs=[VMEM] * 2,
        scratch_shapes=[pltpu.VMEM((n, n), F32)] + [pltpu.VMEM((128, 256), F32)] * 2,
        cost_estimate=CHOL_COST,
        compiler_params=pltpu.CompilerParams(vmem_limit_bytes=40 * MIB),
    )(at, mine, other)


def factor_second(at, mask, mine, other, W0):
    n = W0.shape[0]
    return pl.pallas_call(
        factor_second_kernel,
        out_shape=[jax.ShapeDtypeStruct((n, n), BF16)] + [jax.ShapeDtypeStruct((n, n), F32)] * 2,
        in_specs=[SMEM, SMEM, VMEM, VMEM, VMEM],
        out_specs=[VMEM] * 3,
        scratch_shapes=[pltpu.VMEM((n, n), F32)]
        + [pltpu.VMEM((128, 256), F32)] * 2
        + [pltpu.VMEM((n, n), F32)],
        cost_estimate=CHOL_COST,
        compiler_params=pltpu.CompilerParams(vmem_limit_bytes=40 * MIB),
    )(at, mask, mine, other, W0)


def cut_top_kernel(x_ref, c_ref, o_ref):
    for k in range(6):
        o_ref[:, k] = c_ref[k].reshape(16, 16, 256)
    for i in range(2):
        for c in range(4):
            high, low = split(x_ref[pl.ds(i * 2048 + c, 256, stride=8), :])
            at = 6 + i * 4 + c // 2 * 2
            lanes = slice(c % 2 * 128, c % 2 * 128 + 128)
            o_ref[:, at, :, lanes] = high.reshape(16, 16, 128)
            o_ref[:, at + 1, :, lanes] = low.reshape(16, 16, 128)


def cut_top(front_rows, child):
    return pl.pallas_call(
        cut_top_kernel,
        grid=(1,),
        out_shape=jax.ShapeDtypeStruct((16, 14, 16, 256), BF16),
        in_specs=[
            pl.BlockSpec((4096, 128), lambda i: (0, 0)),
            pl.BlockSpec((6, 256, 256), lambda i: (0, 0, 0)),
        ],
        out_specs=pl.BlockSpec((16, 14, 16, 256), lambda i: (0, 0, 0, 0)),
        cost_estimate=pl.CostEstimate(flops=0, bytes_accessed=5 * MIB, transcendentals=0),
        compiler_params=pltpu.CompilerParams(vmem_limit_bytes=40 * MIB),
    )(front_rows, child)


def cut_low_kernel(at_ref, x_ref, o_ref):
    q = at_ref[1]
    o_ref[...] = jnp.zeros(o_ref.shape, F32)
    for owner in range(2):

        @pl.when(q == owner)
        def _():
            for c in range(4):
                tile = x_ref[pl.ds(c, 256, stride=8), :]
                o_ref[:, 0, :, owner * 512 + c * 128 : owner * 512 + c * 128 + 128] = tile.reshape(16, 16, 128)


def cut_low(at, front_rows):
    return pl.pallas_call(
        cut_low_kernel,
        grid=(6,),
        out_shape=jax.ShapeDtypeStruct((16, 6, 16, 1024), F32),
        in_specs=[SMEM, pl.BlockSpec((2048, 128), lambda i: (i + 2, 0))],
        out_specs=pl.BlockSpec((16, 1, 16, 1024), lambda i: (0, i, 0, 0)),
        cost_estimate=pl.CostEstimate(flops=0, bytes_accessed=12 * MIB, transcendentals=0),
    )(at, front_rows)


def add_pieces(value, slot_ref, c_ref, row, j):
    for child in range(2):
        slot = slot_ref[(row * 4 + j) * 2 + child]
        known = jnp.maximum(slot, 0)
        piece = c_ref[known // 6, lax.rem(known, 6)].astype(F32)
        value = value + jnp.where(slot >= 0, piece, F32(0))
    return value


def join_top_kernel(slot_ref, c_ref, o_ref):
    for i in range(2):
        for j in range(4):
            at = 6 + i * 4 + j % 2 * 2
            value = c_ref[j // 2, at].astype(F32) + c_ref[j // 2, at + 1].astype(F32)
            o_ref[i, :, j * 256 : (j + 1) * 256] = add_pieces(value, slot_ref, c_ref, i, j)


def join_low_kernel(slot_ref, c_ref, f_ref, o_ref):
    for i in range(6):
        for j in range(4):
            lanes = slice(j * 256, (j + 1) * 256)
            o_ref[i, :, lanes] = add_pieces(f_ref[i, :, lanes], slot_ref, c_ref, i + 2, j)


def join_strips(kernel, count, slots, *operands):
    return pl.pallas_call(
        kernel,
        out_shape=jax.ShapeDtypeStruct((count, 16, 1024), F32),
        in_specs=[SMEM] + [VMEM] * len(operands),
        out_specs=VMEM,
        cost_estimate=pl.CostEstimate(flops=0, bytes_accessed=3 * MIB, transcendentals=0),
    )(slots, *operands)


def solve_first_kernel(keep_ref, d_ref, r_ref, w_ref, o_ref):
    width = w_ref.shape[0]
    b = jnp.concatenate(
        [d_ref[:, :, :width].reshape(32, width), r_ref[:, :, :width].reshape(96, width)], axis=0
    )
    x = dot3(b, w_ref[...], NT).reshape(8, 16, width)
    for i in range(8):
        o_ref[i] = jnp.where(keep_ref[i] > 0, x[i], F32(0)).astype(BF16)


def solve_second_kernel(keep_ref, d_ref, r_ref, p_ref, p10_ref, w_ref, o_ref):
    width = w_ref.shape[0]
    half = width // 2
    b = jnp.concatenate(
        [d_ref[:, :, width:].reshape(32, width), r_ref[:, :, width:].reshape(96, width)], axis=0
    )
    u = dot1(p_ref[...].reshape(128, width), p10_ref[...], NT)
    rows = []
    for i in range(8):
        s = slice(16 * i, 16 * i + 16)
        parts = []
        for j in range(2):
            c = slice(j * half, (j + 1) * half)
            parts.append(b[s, c] - jnp.where(keep_ref[8 + 2 * i + j] > 0, u[s, c], F32(0)))
        rows.append(jnp.concatenate(parts, axis=1))
    x = dot3(jnp.concatenate(rows, axis=0), w_ref[...], NT).reshape(8, 16, width)
    for i in range(8):
        o_ref[i] = jnp.where(keep_ref[i] > 0, x[i], F32(0)).astype(BF16)


def solve_strips(kernel, *operands):
    return pl.pallas_call(
        kernel,
        out_shape=jax.ShapeDtypeStruct((8, 16, 512), BF16),
        in_specs=[SMEM] + [VMEM] * (len(operands) - 1),
        out_specs=VMEM,
        cost_estimate=pl.CostEstimate(flops=400_000_000, bytes_accessed=2 * MIB, transcendentals=0),
    )(*operands)


def deal_kernel(at_ref, p0_ref, p1_ref, *refs):
    o_ref = refs[-1]
    for q in range(16):
        o_ref[q, 0:8] = p0_ref[...]
        o_ref[q, 8:16] = p1_ref[...]
    for panel in range(2):
        for k in range(4):
            row = lax.rem(at_ref[2] + k, 4) * 2
            for c in range(2):
                for lr in range(4):
                    o_ref[(lr % 2) * 8 + row + c, 16 + panel * 2 + lr // 2] = refs[panel * 4 + k][c, lr]


def deal(at, P0, P1, first, second):
    return pl.pallas_call(
        deal_kernel,
        out_shape=jax.ShapeDtypeStruct((16, 20, 16, 512), BF16),
        in_specs=[SMEM] + [VMEM] * 10,
        out_specs=VMEM,
        cost_estimate=pl.CostEstimate(flops=0, bytes_accessed=8 * MIB, transcendentals=0),
        compiler_params=pltpu.CompilerParams(vmem_limit_bytes=24 * MIB),
    )(at, P0, P1, *first, *second)


def extend_kernel(slot_ref, f_ref, *refs):
    child, o_ref = refs[:8], refs[8]
    i = pl.program_id(0)
    for j in range(4):
        live = [slot_ref[(i * 4 + j) * 2 + ch] >= 0 for ch in range(2)]
        pieces = [child[j * 2 + ch] for ch in range(2)]
        for c in range(2):
            lanes = slice(c * 128, (c + 1) * 128)
            rows = pl.ds(j * 2 + c, 256, stride=8)
            value = f_ref[rows, :]
            for ch in range(2):
                value = value + jnp.where(live[ch], pieces[ch][0, :, lanes].astype(F32), F32(0))
            o_ref[rows, :] = value


def extend(slots, front_rows, arrived):
    def child_spec(k):
        return pl.BlockSpec((1, 256, 256), lambda i, s: (jnp.maximum(s[i * 8 + k], 0), 0, 0))

    return pl.pallas_call(
        extend_kernel,
        grid_spec=pltpu.PrefetchScalarGridSpec(
            num_scalar_prefetch=1,
            grid=(8,),
            in_specs=[pl.BlockSpec((2048, 128), lambda i, s: (i, 0))] + [child_spec(k) for k in range(8)],
            out_specs=pl.BlockSpec((2048, 128), lambda i, s: (i, 0)),
        ),
        out_shape=jax.ShapeDtypeStruct(front_rows.shape, F32),
        cost_estimate=pl.CostEstimate(flops=0, bytes_accessed=24 * MIB, transcendentals=0),
        compiler_params=pltpu.CompilerParams(vmem_limit_bytes=24 * MIB),
    )(slots, front_rows, *([arrived] * 8))


def finish_kernel(flag_ref, f_ref, row0_ref, row1_ref, mine_ref, other_ref, l_ref, wh_ref, wl_ref, o_ref, cols_ref):
    i = pl.program_id(0)

    @pl.when(i == 0)
    def _():
        core = flag_ref[48]
        for ref, sub in ((mine_ref, core), (other_ref, 1 - core)):
            for panel in range(2):
                for lc in range(2):
                    strips = ref[:, panel * 2 + lc].reshape(256, 512)
                    cols_ref[lc * 2 + sub, :, panel * 512 : (panel + 1) * 512] = strips

    rows = jnp.concatenate([ref[:, 0].reshape(256, 512) for ref in (row0_ref, row1_ref)], axis=1)
    for lc in range(2):
        state = flag_ref[32 + i * 2 + lc]

        @pl.when(state > 0)
        def _():
            blocks = []
            for sc in range(2):
                j = lc * 2 + sc
                value = jnp.concatenate(
                    [f_ref[pl.ds(lc * 4 + sc * 2 + c, 256, stride=8), :] for c in range(2)], axis=1
                )
                product = dot1(rows, cols_ref[j], NT)
                blocks.append(value - jnp.where(flag_ref[i * 4 + j] > 0, product, F32(0)))
            block = jnp.concatenate(blocks, axis=1)

            def put(value):
                for c in range(4):
                    o_ref[pl.ds(lc * 4 + c, 256, stride=8), :] = value[:, c * 128 : (c + 1) * 128]

            @pl.when(state == 1)
            def _():
                put(block)

            if lc == 0:

                @pl.when(state == 2)
                def _():
                    high, low = split(block)
                    wh = wh_ref[...]
                    put(dot1(high, wh, NT) + (dot1(low, wh, NT) + dot1(high, wl_ref[...], NT)))

                @pl.when(state == 3)
                def _():
                    put(l_ref[pl.ds(pl.multiple_of(lax.rem(i, 2) * 256, 256), 256), :])

        @pl.when(state == 0)
        def _():
            for c in range(4):
                o_ref[pl.ds(lc * 4 + c, 256, stride=8), :] = jnp.zeros((256, 128), F32)


def finish(flags, extended, dealt, other, L, W):
    def whole(shape, *at):
        return pl.BlockSpec(shape, lambda i, f: at)

    return pl.pallas_call(
        finish_kernel,
        grid_spec=pltpu.PrefetchScalarGridSpec(
            num_scalar_prefetch=1,
            grid=(8,),
            in_specs=[pl.BlockSpec((2048, 128), lambda i, f: (i, 0))]
            + [pl.BlockSpec((16, 1, 16, 512), lambda i, f: (0, i, 0, 0))]
            + [pl.BlockSpec((16, 1, 16, 512), lambda i, f: (0, i + 8, 0, 0))]
            + [whole((16, 4, 16, 512), 0, 4, 0, 0), whole((16, 4, 16, 512), 0, 0, 0, 0)]
            + [whole((512, 512), 0, 0)] * 3,
            out_specs=pl.BlockSpec((2048, 128), lambda i, f: (i, 0)),
            scratch_shapes=[pltpu.VMEM((4, 256, 1024), BF16)],
        ),
        out_shape=jax.ShapeDtypeStruct(extended.shape, F32),
        cost_estimate=pl.CostEstimate(flops=5_000_000_000, bytes_accessed=24 * MIB, transcendentals=0),
        compiler_params=pltpu.CompilerParams(vmem_limit_bytes=48 * MIB),
    )(flags, extended, dealt, dealt, dealt, other, L, *W)


def slot_of_targets(codes, row_map, rows, cols):
    index = jnp.arange(CNB, dtype=jnp.int32)

    def place(blocks):
        hit = row_map[None] == blocks[:, None, None]
        return jnp.sum(jnp.where(hit, index + 1, 0), axis=-1) - 1

    pi, pj = place(rows), place(cols)
    child = jnp.arange(2, dtype=jnp.int32) * (CNB * CNB)
    wanted = child + pi[:, None, :] * CNB + pj[None, :, :]
    known = (pi[:, None, :] >= 0) & (pj[None, :, :] >= 0)
    wanted = jnp.where(known, wanted, -2).reshape(-1)
    number = jnp.arange(codes.shape[0], dtype=jnp.int32)
    return jnp.sum(jnp.where(wanted[:, None] == codes[None, :], number + 1, 0), axis=-1) - 1


def spread(x, axis, count):
    return lax.all_to_all(jnp.broadcast_to(x[None], (count,) + x.shape), axis, 0, 0, tiled=True)


def local(front, child_blocks, row_map, slot_table, struct_mask):
    prow, pcol = lax.axis_size("prow"), lax.axis_size("pcol")
    p, q = lax.axis_index("prow"), lax.axis_index("pcol")
    core, y = p % 2, p // 2
    at = jnp.stack([core, q, y]).astype(jnp.int32)
    swap = [(i, i ^ 1) for i in range(8)]
    front_rows = front.reshape(16384, 128)
    child = child_blocks[0, 0]

    pair = jnp.arange(2, dtype=jnp.int32)
    row_blocks = jnp.arange(4, dtype=jnp.int32) * prow + p
    col_blocks = jnp.arange(2, dtype=jnp.int32) * pcol + q
    sub_rows = (2 * row_blocks[:, None] + pair).reshape(-1)
    sub_cols = (2 * col_blocks[:, None] + pair).reshape(-1)

    low_cut = cut_low(at, front_rows)
    low_front = lax.psum_scatter(
        low_cut.reshape(96, 16, 1024), "pcol", scatter_dimension=0, tiled=True
    )
    front_top, _ = lax.optimization_barrier((front_rows, low_cut))
    got = lax.all_to_all(cut_top(front_top, child.reshape(48, 256, 256)), "pcol", 0, 0, tiled=True)

    my_codes = lax.dynamic_index_in_dim(slot_table, p, 0, False)
    strip_slots = slot_of_targets(my_codes[:, :2].reshape(-1), row_map, sub_rows, jnp.arange(4, dtype=jnp.int32))
    slots = slot_of_targets(
        lax.dynamic_index_in_dim(my_codes, q, 1, False).reshape(-1), row_map, sub_rows, sub_cols
    )
    row_mask = struct_mask[sub_rows]
    lower = row_blocks[:, None] >= col_blocks[None, :]
    mask = row_mask[:, sub_cols]
    state = jnp.where(lower, 1, 0)
    owner = (q < 2) & (jnp.arange(2) == 0)
    state = jnp.where(owner[None, :] & lower, jnp.where(row_blocks[:, None] == q, 3, 2), state)
    flags = jnp.concatenate([mask.reshape(-1), jnp.repeat(state, 2, axis=0).reshape(-1), core.reshape(1)])
    flags = flags.astype(jnp.int32)
    keep0 = (sub_rows >= 2).astype(jnp.int32)
    keep1 = jnp.concatenate([(sub_rows >= 4).astype(jnp.int32), row_mask[:, 2:4].reshape(-1)])

    top = join_strips(join_top_kernel, 2, strip_slots, got)

    half_top = lax.all_to_all(jnp.tile(top, (prow // 2, 1, 1)), "prow", 0, 0, tiled=True)
    first = spread(jnp.concatenate([half_top[0, :, :512], half_top[1]], axis=1), "pcol", pcol)
    diag = (first, lax.ppermute(first, "prow", swap))
    child, diag, low_front = lax.optimization_barrier((child, diag, low_front))
    arrived = lax.all_to_all(child, "pcol", 0, 0, tiled=True).reshape(48, 256, 256)

    def gather_columns(strips):
        halves = strips.reshape(4, 2, 16, 512)
        even, odd = halves[:, 0], halves[:, 1]
        sent = lax.ppermute(jnp.where(core == 0, odd, even), "prow", swap)
        kept = jnp.where(core == 0, even, odd)
        chip = jnp.where(core == 0, jnp.stack([kept, sent]), jnp.stack([sent, kept]))
        along = lambda k: [(2 * ((i + k) % 4) + c, 2 * i + c) for i in range(4) for c in range(2)]
        return [chip] + [lax.ppermute(chip, "prow", along(k)) for k in range(1, 4)]

    L0, W0 = factor_first(at, *diag)
    low = join_strips(join_low_kernel, 6, strip_slots, got, low_front)
    P0 = solve_strips(solve_first_kernel, keep0, top, low, W0)
    P0, diag = lax.optimization_barrier((P0, diag))
    cols0 = gather_columns(P0)
    P10, L1, W1 = factor_second(at, struct_mask[2:4, 2:4].reshape(-1), *diag, W0)
    W1, cols0 = lax.optimization_barrier((W1, cols0))
    P1 = solve_strips(solve_second_kernel, keep1, top, low, P0, P10, W1)
    cols1 = gather_columns(P1)

    dealt = deal(at, P0, P1, cols0, cols1)
    dealt, arrived = lax.optimization_barrier((dealt, arrived))
    dealt = lax.all_to_all(dealt, "pcol", 0, 0, tiled=True)
    extended = extend(slots, front_rows, arrived)
    L = jnp.where(q == 0, L0, L1)
    W = split(jnp.where(q == 0, W0, W1))
    dealt, extended, L, W = lax.optimization_barrier((dealt, extended, L, W))
    other = lax.ppermute(dealt[:, 16:], "prow", swap)
    out = finish(flags, extended, dealt, other, L, W)
    return out.reshape(front.shape)


def solution(mesh):
    in_specs = (
        P(None, "prow", None, None, "pcol", None),
        P("prow", "pcol", None, None, None, None),
        P(),
        P(),
        P(),
    )
    out_specs = P(None, "prow", None, None, "pcol", None)
    return jax.shard_map(local, mesh=mesh, in_specs=in_specs, out_specs=out_specs, check_vma=False)
```

```python
import functools

import jax
import jax.numpy as jnp
from jax import lax
from jax.experimental import pallas as pl
from jax.experimental.pallas import tpu as pltpu
from jax.sharding import PartitionSpec as P

F32 = jnp.float32
BF16 = jnp.bfloat16
CNB = 60
NN = (((1,), (0,)), ((), ()))
NT = (((1,), (1,)), ((), ()))
MIB = 2**20
VMEM = pl.BlockSpec(memory_space=pltpu.VMEM)
SMEM = pl.BlockSpec(memory_space=pltpu.SMEM)


def split(x):
    high = x.astype(BF16)
    return high, (x - high.astype(F32)).astype(BF16)


def dot1(a, b, dims):
    return lax.dot_general(a, b, dims, preferred_element_type=F32)


def dot3(a, b, dims):
    ah, al = split(a)
    bh, bl = split(b)
    return dot1(ah, bh, dims) + (dot1(al, bh, dims) + dot1(ah, bl, dims))


GROUPS = 4


def eliminate(R, n):
    row = lax.broadcasted_iota(jnp.int32, (8, 1), 0)
    across = lambda v: jnp.concatenate([v, v], axis=1)
    over = lambda x, lane: jnp.broadcast_to(x[:, lane : lane + 1], (8, 128))
    done = []
    for g in range(len(R)):
        base = 8 * g
        later = range(g + 1, len(R))
        cols = [over(R[g], base + j) for j in range(8)]
        below = {h: [over(R[h], base + j) for j in range(8)] for h in later}
        D = [[jnp.broadcast_to(cols[j][i : i + 1], (8, 128)) for j in range(i + 1)] for i in range(8)]
        Y = [jnp.broadcast_to(R[g][i : i + 1], (8, 2 * n)) for i in range(8)]
        out = None
        for j in range(8):
            scale = lax.rsqrt(D[j][j])
            inverse = scale * scale
            for i in range(j + 1, 8):
                factor = D[i][j] * inverse
                for m in range(j + 1, i):
                    D[i][m] = D[i][m] - factor * D[m][j]
                D[i][i] = D[i][i] - (D[i][j] * D[i][j]) * inverse
                Y[i] = Y[i] - across(factor) * Y[j]
            for h in later:
                factor = below[h][j] * inverse
                for m in range(j + 1, 8):
                    below[h][m] = below[h][m] - factor * D[m][j]
                R[h] = R[h] - across(factor) * Y[j]
            scaled = Y[j] * across(scale)
            out = scaled if out is None else jnp.where(row == j, scaled, out)
        done.append(out)
    return jnp.concatenate(done, axis=0)


def factor_base(m_ref, o_ref):
    n = m_ref.shape[0]
    step = 8 * GROUPS

    def body(k, _):
        at = k * step
        rows = pl.ds(pl.multiple_of(at, step), step)
        X = m_ref[rows, :]
        A = pltpu.roll(X[:, :n], jnp.where(k == 0, 0, n - at), 1)
        X = jnp.concatenate([A, X[:, n:]], axis=1)
        out = eliminate([X[8 * g : 8 * g + 8] for g in range(GROUPS)], n)
        out = jnp.concatenate([pltpu.roll(out[:, :n], at, 1), out[:, n:]], axis=1)
        o_ref[rows, :] = out
        m_ref[...] = m_ref[...] - dot3(out[:, :n].T, out, NN)
        return 0

    lax.fori_loop(0, n // step, body, 0)


def factor_whole(a_ref, l_ref, w_ref, m_ref, o_ref):
    n = a_ref.shape[0]
    b = 128
    w_ref[...] = jnp.zeros((n, n), F32)
    l_ref[...] = jnp.zeros((n, n), F32)
    lane = lax.broadcasted_iota(jnp.int32, (b, b), 1)
    sub = lax.broadcasted_iota(jnp.int32, (b, b), 0)
    for k in range(0, n, b):
        s = slice(k, k + b)
        D = a_ref[s, s]
        m_ref[:, :b] = jnp.where(sub >= lane, D, D.T)
        m_ref[:, b:] = jnp.where(lane == sub, F32(1), F32(0))
        factor_base(m_ref, o_ref)
        W = jnp.where(lane <= sub, o_ref[:, b:], F32(0))
        l_ref[s, s] = jnp.where(lane >= sub, o_ref[:, :b], F32(0)).T
        w_ref[s, s] = W
        if k:
            T = dot3(l_ref[s, :k], w_ref[:k, :k], NN)
            w_ref[s, :k] = -dot3(W, T, NN)
        if k + b < n:
            L = dot3(a_ref[k + b :, s], W, NT)
            l_ref[k + b :, s] = L
            for j in range(k + b, n, b):
                off = j - k - b
                a_ref[j:, j : j + b] = a_ref[j:, j : j + b] - dot3(L[off:], L[off : off + b], NT)


def factor_first_kernel(at_ref, mine_ref, other_ref, l_ref, w_ref, a_ref, m_ref, o_ref):
    n = a_ref.shape[0]
    for ref, sub in ((mine_ref, at_ref[0]), (other_ref, 1 - at_ref[0])):
        a_ref[pl.ds(pl.multiple_of(sub * 256, 256), 256), :] = ref[:, :, :n].reshape(256, n)
    factor_whole(a_ref, l_ref, w_ref, m_ref, o_ref)


def factor_second_kernel(
    at_ref, mask_ref, mine_ref, other_ref, w0_ref, p_ref, l_ref, w_ref, a_ref, m_ref, o_ref, b_ref
):
    n = a_ref.shape[0]
    for ref, sub in ((mine_ref, at_ref[0]), (other_ref, 1 - at_ref[0])):
        rows = pl.ds(pl.multiple_of(sub * 256, 256), 256)
        b_ref[rows, :] = ref[:, :, n : 2 * n].reshape(256, n)
        a_ref[rows, :] = ref[:, :, 2 * n :].reshape(256, n)
    panel = dot3(b_ref[...], w0_ref[...], NT).astype(BF16)
    p_ref[...] = panel
    h = n // 2
    for i in range(2):
        for j in range(i + 1):
            r, c = slice(i * h, (i + 1) * h), slice(j * h, (j + 1) * h)
            product = dot1(panel[r], panel[c], NT)
            a_ref[r, c] = a_ref[r, c] - jnp.where(mask_ref[i * 2 + j] > 0, product, F32(0))
    factor_whole(a_ref, l_ref, w_ref, m_ref, o_ref)


CHOL_COST = pl.CostEstimate(flops=20_000_000_000, bytes_accessed=3 * MIB, transcendentals=1024)


def factor_first(at, mine, other):
    n = mine.shape[-1] // 3
    return pl.pallas_call(
        factor_first_kernel,
        out_shape=[jax.ShapeDtypeStruct((n, n), F32)] * 2,
        in_specs=[SMEM, VMEM, VMEM],
        out_specs=[VMEM] * 2,
        scratch_shapes=[pltpu.VMEM((n, n), F32)] + [pltpu.VMEM((128, 256), F32)] * 2,
        cost_estimate=CHOL_COST,
        compiler_params=pltpu.CompilerParams(vmem_limit_bytes=40 * MIB),
    )(at, mine, other)


def factor_second(at, mask, mine, other, W0):
    n = W0.shape[0]
    return pl.pallas_call(
        factor_second_kernel,
        out_shape=[jax.ShapeDtypeStruct((n, n), BF16)] + [jax.ShapeDtypeStruct((n, n), F32)] * 2,
        in_specs=[SMEM, SMEM, VMEM, VMEM, VMEM],
        out_specs=[VMEM] * 3,
        scratch_shapes=[pltpu.VMEM((n, n), F32)]
        + [pltpu.VMEM((128, 256), F32)] * 2
        + [pltpu.VMEM((n, n), F32)],
        cost_estimate=CHOL_COST,
        compiler_params=pltpu.CompilerParams(vmem_limit_bytes=40 * MIB),
    )(at, mask, mine, other, W0)


def cut_top_kernel(x_ref, c_ref, o_ref):
    for k in range(6):
        o_ref[:, k] = c_ref[k].reshape(16, 16, 256)
    for i in range(2):
        for c in range(4):
            high, low = split(x_ref[pl.ds(i * 2048 + c, 256, stride=8), :])
            at = 6 + i * 4 + c // 2 * 2
            lanes = slice(c % 2 * 128, c % 2 * 128 + 128)
            o_ref[:, at, :, lanes] = high.reshape(16, 16, 128)
            o_ref[:, at + 1, :, lanes] = low.reshape(16, 16, 128)


def cut_top(front_rows, child):
    return pl.pallas_call(
        cut_top_kernel,
        grid=(1,),
        out_shape=jax.ShapeDtypeStruct((16, 14, 16, 256), BF16),
        in_specs=[
            pl.BlockSpec((4096, 128), lambda i: (0, 0)),
            pl.BlockSpec((6, 256, 256), lambda i: (0, 0, 0)),
        ],
        out_specs=pl.BlockSpec((16, 14, 16, 256), lambda i: (0, 0, 0, 0)),
        cost_estimate=pl.CostEstimate(flops=0, bytes_accessed=5 * MIB, transcendentals=0),
        compiler_params=pltpu.CompilerParams(vmem_limit_bytes=40 * MIB),
    )(front_rows, child)


def cut_low_kernel(at_ref, x_ref, o_ref):
    q = at_ref[1]
    o_ref[...] = jnp.zeros(o_ref.shape, F32)
    for owner in range(2):

        @pl.when(q == owner)
        def _():
            for c in range(4):
                tile = x_ref[pl.ds(c, 256, stride=8), :]
                o_ref[:, 0, :, owner * 512 + c * 128 : owner * 512 + c * 128 + 128] = tile.reshape(16, 16, 128)


def cut_low(at, front_rows):
    return pl.pallas_call(
        cut_low_kernel,
        grid=(6,),
        out_shape=jax.ShapeDtypeStruct((16, 6, 16, 1024), F32),
        in_specs=[SMEM, pl.BlockSpec((2048, 128), lambda i: (i + 2, 0))],
        out_specs=pl.BlockSpec((16, 1, 16, 1024), lambda i: (0, i, 0, 0)),
        cost_estimate=pl.CostEstimate(flops=0, bytes_accessed=12 * MIB, transcendentals=0),
    )(at, front_rows)


def add_pieces(value, slot_ref, c_ref, row, j):
    for child in range(2):
        slot = slot_ref[(row * 4 + j) * 2 + child]
        known = jnp.maximum(slot, 0)
        piece = c_ref[known // 6, lax.rem(known, 6)].astype(F32)
        value = value + jnp.where(slot >= 0, piece, F32(0))
    return value


def join_top_kernel(slot_ref, c_ref, o_ref):
    for i in range(2):
        for j in range(4):
            at = 6 + i * 4 + j % 2 * 2
            value = c_ref[j // 2, at].astype(F32) + c_ref[j // 2, at + 1].astype(F32)
            o_ref[i, :, j * 256 : (j + 1) * 256] = add_pieces(value, slot_ref, c_ref, i, j)


def join_low_kernel(slot_ref, c_ref, f_ref, o_ref):
    for i in range(6):
        for j in range(4):
            lanes = slice(j * 256, (j + 1) * 256)
            o_ref[i, :, lanes] = add_pieces(f_ref[i, :, lanes], slot_ref, c_ref, i + 2, j)


def join_strips(kernel, count, slots, *operands):
    return pl.pallas_call(
        kernel,
        out_shape=jax.ShapeDtypeStruct((count, 16, 1024), F32),
        in_specs=[SMEM] + [VMEM] * len(operands),
        out_specs=VMEM,
        cost_estimate=pl.CostEstimate(flops=0, bytes_accessed=3 * MIB, transcendentals=0),
    )(slots, *operands)


def solve_first_kernel(keep_ref, d_ref, r_ref, w_ref, o_ref):
    width = w_ref.shape[0]
    b = jnp.concatenate(
        [d_ref[:, :, :width].reshape(32, width), r_ref[:, :, :width].reshape(96, width)], axis=0
    )
    x = dot3(b, w_ref[...], NT).reshape(8, 16, width)
    for i in range(8):
        o_ref[i] = jnp.where(keep_ref[i] > 0, x[i], F32(0)).astype(BF16)


def solve_second_kernel(keep_ref, d_ref, r_ref, p_ref, p10_ref, w_ref, o_ref):
    width = w_ref.shape[0]
    half = width // 2
    b = jnp.concatenate(
        [d_ref[:, :, width:].reshape(32, width), r_ref[:, :, width:].reshape(96, width)], axis=0
    )
    u = dot1(p_ref[...].reshape(128, width), p10_ref[...], NT)
    rows = []
    for i in range(8):
        s = slice(16 * i, 16 * i + 16)
        parts = []
        for j in range(2):
            c = slice(j * half, (j + 1) * half)
            parts.append(b[s, c] - jnp.where(keep_ref[8 + 2 * i + j] > 0, u[s, c], F32(0)))
        rows.append(jnp.concatenate(parts, axis=1))
    x = dot3(jnp.concatenate(rows, axis=0), w_ref[...], NT).reshape(8, 16, width)
    for i in range(8):
        o_ref[i] = jnp.where(keep_ref[i] > 0, x[i], F32(0)).astype(BF16)


def solve_strips(kernel, *operands):
    return pl.pallas_call(
        kernel,
        out_shape=jax.ShapeDtypeStruct((8, 16, 512), BF16),
        in_specs=[SMEM] + [VMEM] * (len(operands) - 1),
        out_specs=VMEM,
        cost_estimate=pl.CostEstimate(flops=400_000_000, bytes_accessed=2 * MIB, transcendentals=0),
    )(*operands)


def deal_kernel(at_ref, p0_ref, p1_ref, *refs):
    o_ref = refs[-1]
    for q in range(16):
        o_ref[q, 0:8] = p0_ref[...]
        o_ref[q, 8:16] = p1_ref[...]
    for panel in range(2):
        for k in range(4):
            row = lax.rem(at_ref[2] + k, 4) * 2
            for c in range(2):
                for lr in range(4):
                    o_ref[(lr % 2) * 8 + row + c, 16 + panel * 2 + lr // 2] = refs[panel * 4 + k][c, lr]


def deal(at, P0, P1, first, second):
    return pl.pallas_call(
        deal_kernel,
        out_shape=jax.ShapeDtypeStruct((16, 20, 16, 512), BF16),
        in_specs=[SMEM] + [VMEM] * 10,
        out_specs=VMEM,
        cost_estimate=pl.CostEstimate(flops=0, bytes_accessed=8 * MIB, transcendentals=0),
        compiler_params=pltpu.CompilerParams(vmem_limit_bytes=24 * MIB),
    )(at, P0, P1, *first, *second)


def extend_kernel(slot_ref, f_ref, *refs):
    child, o_ref = refs[:8], refs[8]
    i = pl.program_id(0)
    for j in range(4):
        live = [slot_ref[(i * 4 + j) * 2 + ch] >= 0 for ch in range(2)]
        pieces = [child[j * 2 + ch] for ch in range(2)]
        for c in range(2):
            lanes = slice(c * 128, (c + 1) * 128)
            rows = pl.ds(j * 2 + c, 256, stride=8)
            value = f_ref[rows, :]
            for ch in range(2):
                value = value + jnp.where(live[ch], pieces[ch][0, :, lanes].astype(F32), F32(0))
            o_ref[rows, :] = value


def extend(slots, front_rows, arrived):
    def child_spec(k):
        return pl.BlockSpec((1, 256, 256), lambda i, s: (jnp.maximum(s[i * 8 + k], 0), 0, 0))

    return pl.pallas_call(
        extend_kernel,
        grid_spec=pltpu.PrefetchScalarGridSpec(
            num_scalar_prefetch=1,
            grid=(8,),
            in_specs=[pl.BlockSpec((2048, 128), lambda i, s: (i, 0))] + [child_spec(k) for k in range(8)],
            out_specs=pl.BlockSpec((2048, 128), lambda i, s: (i, 0)),
        ),
        out_shape=jax.ShapeDtypeStruct(front_rows.shape, F32),
        cost_estimate=pl.CostEstimate(flops=0, bytes_accessed=24 * MIB, transcendentals=0),
        compiler_params=pltpu.CompilerParams(vmem_limit_bytes=24 * MIB),
    )(slots, front_rows, *([arrived] * 8))


def finish_kernel(flag_ref, f_ref, row0_ref, row1_ref, mine_ref, other_ref, l_ref, w_ref, o_ref, cols_ref, wh_ref, wl_ref):
    i = pl.program_id(0)

    @pl.when(i == 0)
    def _():
        core = flag_ref[48]
        for ref, sub in ((mine_ref, core), (other_ref, 1 - core)):
            for panel in range(2):
                for lc in range(2):
                    strips = ref[:, panel * 2 + lc].reshape(256, 512)
                    cols_ref[lc * 2 + sub, :, panel * 512 : (panel + 1) * 512] = strips

    @pl.when((i == 0) & (flag_ref[49] > 0))
    def _():
        wh_ref[...], wl_ref[...] = split(w_ref[...])

    rows = jnp.concatenate([ref[:, 0].reshape(256, 512) for ref in (row0_ref, row1_ref)], axis=1)
    for lc in range(2):
        state = flag_ref[32 + i * 2 + lc]

        @pl.when(state > 0)
        def _():
            blocks = []
            for sc in range(2):
                j = lc * 2 + sc
                value = jnp.concatenate(
                    [f_ref[pl.ds(lc * 4 + sc * 2 + c, 256, stride=8), :] for c in range(2)], axis=1
                )
                product = dot1(rows, cols_ref[j], NT)
                blocks.append(value - jnp.where(flag_ref[i * 4 + j] > 0, product, F32(0)))
            block = jnp.concatenate(blocks, axis=1)

            def put(value):
                for c in range(4):
                    o_ref[pl.ds(lc * 4 + c, 256, stride=8), :] = value[:, c * 128 : (c + 1) * 128]

            @pl.when(state == 1)
            def _():
                put(block)

            if lc == 0:

                @pl.when(state == 2)
                def _():
                    high, low = split(block)
                    wh = wh_ref[...]
                    put(dot1(high, wh, NT) + (dot1(low, wh, NT) + dot1(high, wl_ref[...], NT)))

                @pl.when(state == 3)
                def _():
                    put(l_ref[pl.ds(pl.multiple_of(lax.rem(i, 2) * 256, 256), 256), :])

        @pl.when(state == 0)
        def _():
            for c in range(4):
                o_ref[pl.ds(lc * 4 + c, 256, stride=8), :] = jnp.zeros((256, 128), F32)


def finish(flags, extended, dealt, other, L, W):
    def whole(shape, *at):
        return pl.BlockSpec(shape, lambda i, f: at)

    return pl.pallas_call(
        finish_kernel,
        grid_spec=pltpu.PrefetchScalarGridSpec(
            num_scalar_prefetch=1,
            grid=(8,),
            in_specs=[pl.BlockSpec((2048, 128), lambda i, f: (i, 0))]
            + [pl.BlockSpec((16, 1, 16, 512), lambda i, f: (0, i, 0, 0))]
            + [pl.BlockSpec((16, 1, 16, 512), lambda i, f: (0, i + 8, 0, 0))]
            + [whole((16, 4, 16, 512), 0, 4, 0, 0), whole((16, 4, 16, 512), 0, 0, 0, 0)]
            + [whole((512, 512), 0, 0)] * 2,
            out_specs=pl.BlockSpec((2048, 128), lambda i, f: (i, 0)),
            scratch_shapes=[pltpu.VMEM((4, 256, 1024), BF16)] + [pltpu.VMEM((512, 512), BF16)] * 2,
        ),
        out_shape=jax.ShapeDtypeStruct(extended.shape, F32),
        cost_estimate=pl.CostEstimate(flops=5_000_000_000, bytes_accessed=24 * MIB, transcendentals=0),
        compiler_params=pltpu.CompilerParams(vmem_limit_bytes=48 * MIB),
    )(flags, extended, dealt, dealt, dealt, other, L, W)


def slot_of_targets(codes, row_map, rows, cols):
    index = jnp.arange(CNB, dtype=jnp.int32)

    def place(blocks):
        hit = row_map[None] == blocks[:, None, None]
        return jnp.sum(jnp.where(hit, index + 1, 0), axis=-1) - 1

    pi, pj = place(rows), place(cols)
    child = jnp.arange(2, dtype=jnp.int32) * (CNB * CNB)
    wanted = child + pi[:, None, :] * CNB + pj[None, :, :]
    known = (pi[:, None, :] >= 0) & (pj[None, :, :] >= 0)
    wanted = jnp.where(known, wanted, -2).reshape(-1)
    number = jnp.arange(codes.shape[0], dtype=jnp.int32)
    return jnp.sum(jnp.where(wanted[:, None] == codes[None, :], number + 1, 0), axis=-1) - 1


def spread(x, axis, count):
    return lax.all_to_all(jnp.broadcast_to(x[None], (count,) + x.shape), axis, 0, 0, tiled=True)


def local(front, child_blocks, row_map, slot_table, struct_mask):
    prow, pcol = lax.axis_size("prow"), lax.axis_size("pcol")
    p, q = lax.axis_index("prow"), lax.axis_index("pcol")
    core, y = p % 2, p // 2
    at = jnp.stack([core, q, y]).astype(jnp.int32)
    swap = [(i, i ^ 1) for i in range(8)]
    front_rows = front.reshape(16384, 128)
    child = child_blocks[0, 0]

    pair = jnp.arange(2, dtype=jnp.int32)
    row_blocks = jnp.arange(4, dtype=jnp.int32) * prow + p
    col_blocks = jnp.arange(2, dtype=jnp.int32) * pcol + q
    sub_rows = (2 * row_blocks[:, None] + pair).reshape(-1)
    sub_cols = (2 * col_blocks[:, None] + pair).reshape(-1)

    low_cut = cut_low(at, front_rows)
    low_front = lax.psum_scatter(
        low_cut.reshape(96, 16, 1024), "pcol", scatter_dimension=0, tiled=True
    )
    front_top, _ = lax.optimization_barrier((front_rows, low_cut))
    got = lax.all_to_all(cut_top(front_top, child.reshape(48, 256, 256)), "pcol", 0, 0, tiled=True)

    my_codes = lax.dynamic_index_in_dim(slot_table, p, 0, False)
    strip_slots = slot_of_targets(my_codes[:, :2].reshape(-1), row_map, sub_rows, jnp.arange(4, dtype=jnp.int32))
    slots = slot_of_targets(
        lax.dynamic_index_in_dim(my_codes, q, 1, False).reshape(-1), row_map, sub_rows, sub_cols
    )
    row_mask = struct_mask[sub_rows]
    lower = row_blocks[:, None] >= col_blocks[None, :]
    mask = row_mask[:, sub_cols]
    state = jnp.where(lower, 1, 0)
    owner = (q < 2) & (jnp.arange(2) == 0)
    state = jnp.where(owner[None, :] & lower, jnp.where(row_blocks[:, None] == q, 3, 2), state)
    flags = jnp.concatenate([mask.reshape(-1), jnp.repeat(state, 2, axis=0).reshape(-1), jnp.stack([core, 2 - q])])
    flags = flags.astype(jnp.int32)
    keep0 = (sub_rows >= 2).astype(jnp.int32)
    keep1 = jnp.concatenate([(sub_rows >= 4).astype(jnp.int32), row_mask[:, 2:4].reshape(-1)])

    top = join_strips(join_top_kernel, 2, strip_slots, got)

    half_top = lax.all_to_all(jnp.tile(top, (prow // 2, 1, 1)), "prow", 0, 0, tiled=True)
    first = spread(jnp.concatenate([half_top[0, :, :512], half_top[1]], axis=1), "pcol", pcol)
    diag = (first, lax.ppermute(first, "prow", swap))
    child, diag = lax.optimization_barrier((child, diag))
    arrived = lax.all_to_all(child, "pcol", 0, 0, tiled=True).reshape(48, 256, 256)

    def gather_columns(strips):
        halves = strips.reshape(4, 2, 16, 512)
        even, odd = halves[:, 0], halves[:, 1]
        sent = lax.ppermute(jnp.where(core == 0, odd, even), "prow", swap)
        kept = jnp.where(core == 0, even, odd)
        chip = jnp.where(core == 0, jnp.stack([kept, sent]), jnp.stack([sent, kept]))
        along = lambda k: [(2 * ((i + k) % 4) + c, 2 * i + c) for i in range(4) for c in range(2)]
        return [chip] + [lax.ppermute(chip, "prow", along(k)) for k in range(1, 4)]

    L0, W0 = factor_first(at, *diag)
    P10, L1, W1 = factor_second(at, struct_mask[2:4, 2:4].reshape(-1), *diag, W0)
    W1, low_front = lax.optimization_barrier((W1, low_front))
    low = join_strips(join_low_kernel, 6, strip_slots, got, low_front)
    P0 = solve_strips(solve_first_kernel, keep0, top, low, W0)
    cols0 = gather_columns(P0)
    P1 = solve_strips(solve_second_kernel, keep1, top, low, P0, P10, W1)
    cols1 = gather_columns(P1)

    dealt = deal(at, P0, P1, cols0, cols1)
    dealt, arrived = lax.optimization_barrier((dealt, arrived))
    dealt = lax.all_to_all(dealt, "pcol", 0, 0, tiled=True)
    extended = extend(slots, front_rows, arrived)
    L = jnp.where(q == 0, L0, L1)
    W = jnp.where(q == 0, W0, W1)
    dealt, extended, L, W = lax.optimization_barrier((dealt, extended, L, W))
    other = lax.ppermute(dealt[:, 16:], "prow", swap)
    out = finish(flags, extended, dealt, other, L, W)
    return out.reshape(front.shape)


def solution(mesh):
    in_specs = (
        P(None, "prow", None, None, "pcol", None),
        P("prow", "pcol", None, None, None, None),
        P(),
        P(),
        P(),
    )
    out_specs = P(None, "prow", None, None, "pcol", None)
    return jax.shard_map(local, mesh=mesh, in_specs=in_specs, out_specs=out_specs, check_vma=False)
```

```python
import functools

import jax
import jax.numpy as jnp
from jax import lax
from jax.experimental import pallas as pl
from jax.experimental.pallas import tpu as pltpu
from jax.sharding import PartitionSpec as P

F32 = jnp.float32
BF16 = jnp.bfloat16
CNB = 60
NN = (((1,), (0,)), ((), ()))
NT = (((1,), (1,)), ((), ()))
MIB = 2**20
VMEM = pl.BlockSpec(memory_space=pltpu.VMEM)
SMEM = pl.BlockSpec(memory_space=pltpu.SMEM)


def split(x):
    high = x.astype(BF16)
    return high, (x - high.astype(F32)).astype(BF16)


def dot1(a, b, dims):
    return lax.dot_general(a, b, dims, preferred_element_type=F32)


def dot3(a, b, dims):
    ah, al = split(a)
    bh, bl = split(b)
    return dot1(ah, bh, dims) + (dot1(al, bh, dims) + dot1(ah, bl, dims))


GROUPS = 4


def eliminate(R, n):
    row = lax.broadcasted_iota(jnp.int32, (8, 1), 0)
    across = lambda v: jnp.concatenate([v, v], axis=1)
    over = lambda x, lane: jnp.broadcast_to(x[:, lane : lane + 1], (8, 128))
    done = []
    for g in range(len(R)):
        base = 8 * g
        later = range(g + 1, len(R))
        cols = [over(R[g], base + j) for j in range(8)]
        below = {h: [over(R[h], base + j) for j in range(8)] for h in later}
        D = [[jnp.broadcast_to(cols[j][i : i + 1], (8, 128)) for j in range(i + 1)] for i in range(8)]
        Y = [jnp.broadcast_to(R[g][i : i + 1], (8, 2 * n)) for i in range(8)]
        out = None
        for j in range(8):
            scale = lax.rsqrt(D[j][j])
            inverse = scale * scale
            for i in range(j + 1, 8):
                factor = D[i][j] * inverse
                for m in range(j + 1, i):
                    D[i][m] = D[i][m] - factor * D[m][j]
                D[i][i] = D[i][i] - (D[i][j] * D[i][j]) * inverse
                Y[i] = Y[i] - across(factor) * Y[j]
            for h in later:
                factor = below[h][j] * inverse
                for m in range(j + 1, 8):
                    below[h][m] = below[h][m] - factor * D[m][j]
                R[h] = R[h] - across(factor) * Y[j]
            scaled = Y[j] * across(scale)
            out = scaled if out is None else jnp.where(row == j, scaled, out)
        done.append(out)
    return jnp.concatenate(done, axis=0)


def factor_base(m_ref, o_ref):
    n = m_ref.shape[0]
    step = 8 * GROUPS

    def body(k, _):
        at = k * step
        rows = pl.ds(pl.multiple_of(at, step), step)
        X = m_ref[rows, :]
        A = pltpu.roll(X[:, :n], jnp.where(k == 0, 0, n - at), 1)
        X = jnp.concatenate([A, X[:, n:]], axis=1)
        out = eliminate([X[8 * g : 8 * g + 8] for g in range(GROUPS)], n)
        out = jnp.concatenate([pltpu.roll(out[:, :n], at, 1), out[:, n:]], axis=1)
        o_ref[rows, :] = out
        m_ref[...] = m_ref[...] - dot3(out[:, :n].T, out, NN)
        return 0

    lax.fori_loop(0, n // step, body, 0)


def factor_whole(a_ref, l_ref, w_ref, m_ref, o_ref):
    n = a_ref.shape[0]
    b = 128
    w_ref[...] = jnp.zeros((n, n), F32)
    l_ref[...] = jnp.zeros((n, n), F32)
    lane = lax.broadcasted_iota(jnp.int32, (b, b), 1)
    sub = lax.broadcasted_iota(jnp.int32, (b, b), 0)
    for k in range(0, n, b):
        s = slice(k, k + b)
        D = a_ref[s, s]
        m_ref[:, :b] = jnp.where(sub >= lane, D, D.T)
        m_ref[:, b:] = jnp.where(lane == sub, F32(1), F32(0))
        factor_base(m_ref, o_ref)
        W = jnp.where(lane <= sub, o_ref[:, b:], F32(0))
        l_ref[s, s] = jnp.where(lane >= sub, o_ref[:, :b], F32(0)).T
        w_ref[s, s] = W
        if k:
            T = dot3(l_ref[s, :k], w_ref[:k, :k], NN)
            w_ref[s, :k] = -dot3(W, T, NN)
        if k + b < n:
            L = dot3(a_ref[k + b :, s], W, NT)
            l_ref[k + b :, s] = L
            for j in range(k + b, n, b):
                off = j - k - b
                a_ref[j:, j : j + b] = a_ref[j:, j : j + b] - dot3(L[off:], L[off : off + b], NT)


def factor_first_kernel(at_ref, mine_ref, other_ref, l_ref, w_ref, a_ref, m_ref, o_ref):
    n = a_ref.shape[0]
    for ref, sub in ((mine_ref, at_ref[0]), (other_ref, 1 - at_ref[0])):
        a_ref[pl.ds(pl.multiple_of(sub * 256, 256), 256), :] = ref[:, :, :n].reshape(256, n)
    factor_whole(a_ref, l_ref, w_ref, m_ref, o_ref)


def factor_second_kernel(
    at_ref, mask_ref, mine_ref, other_ref, w0_ref, p_ref, l_ref, w_ref, a_ref, m_ref, o_ref, b_ref
):
    n = a_ref.shape[0]
    for ref, sub in ((mine_ref, at_ref[0]), (other_ref, 1 - at_ref[0])):
        rows = pl.ds(pl.multiple_of(sub * 256, 256), 256)
        b_ref[rows, :] = ref[:, :, n : 2 * n].reshape(256, n)
        a_ref[rows, :] = ref[:, :, 2 * n :].reshape(256, n)
    panel = dot3(b_ref[...], w0_ref[...], NT).astype(BF16)
    p_ref[...] = panel
    h = n // 2
    for i in range(2):
        for j in range(i + 1):
            r, c = slice(i * h, (i + 1) * h), slice(j * h, (j + 1) * h)
            product = dot1(panel[r], panel[c], NT)
            a_ref[r, c] = a_ref[r, c] - jnp.where(mask_ref[i * 2 + j] > 0, product, F32(0))
    factor_whole(a_ref, l_ref, w_ref, m_ref, o_ref)


CHOL_COST = pl.CostEstimate(flops=20_000_000_000, bytes_accessed=3 * MIB, transcendentals=1024)


def factor_first(at, mine, other):
    n = mine.shape[-1] // 3
    return pl.pallas_call(
        factor_first_kernel,
        out_shape=[jax.ShapeDtypeStruct((n, n), F32)] * 2,
        in_specs=[SMEM, VMEM, VMEM],
        out_specs=[VMEM] * 2,
        scratch_shapes=[pltpu.VMEM((n, n), F32)] + [pltpu.VMEM((128, 256), F32)] * 2,
        cost_estimate=CHOL_COST,
        compiler_params=pltpu.CompilerParams(vmem_limit_bytes=40 * MIB),
    )(at, mine, other)


def factor_second(at, mask, mine, other, W0):
    n = W0.shape[0]
    return pl.pallas_call(
        factor_second_kernel,
        out_shape=[jax.ShapeDtypeStruct((n, n), BF16)] + [jax.ShapeDtypeStruct((n, n), F32)] * 2,
        in_specs=[SMEM, SMEM, VMEM, VMEM, VMEM],
        out_specs=[VMEM] * 3,
        scratch_shapes=[pltpu.VMEM((n, n), F32)]
        + [pltpu.VMEM((128, 256), F32)] * 2
        + [pltpu.VMEM((n, n), F32)],
        cost_estimate=CHOL_COST,
        compiler_params=pltpu.CompilerParams(vmem_limit_bytes=40 * MIB),
    )(at, mask, mine, other, W0)


def cut_top_kernel(x_ref, c_ref, o_ref):
    for k in range(6):
        o_ref[:, k] = c_ref[k].reshape(16, 16, 256)
    for i in range(2):
        for c in range(4):
            high, low = split(x_ref[pl.ds(i * 2048 + c, 256, stride=8), :])
            at = 6 + i * 4 + c // 2 * 2
            lanes = slice(c % 2 * 128, c % 2 * 128 + 128)
            o_ref[:, at, :, lanes] = high.reshape(16, 16, 128)
            o_ref[:, at + 1, :, lanes] = low.reshape(16, 16, 128)


def cut_top(front_rows, child):
    return pl.pallas_call(
        cut_top_kernel,
        grid=(1,),
        out_shape=jax.ShapeDtypeStruct((16, 14, 16, 256), BF16),
        in_specs=[
            pl.BlockSpec((4096, 128), lambda i: (0, 0)),
            pl.BlockSpec((6, 256, 256), lambda i: (0, 0, 0)),
        ],
        out_specs=pl.BlockSpec((16, 14, 16, 256), lambda i: (0, 0, 0, 0)),
        cost_estimate=pl.CostEstimate(flops=0, bytes_accessed=5 * MIB, transcendentals=0),
        compiler_params=pltpu.CompilerParams(vmem_limit_bytes=40 * MIB),
    )(front_rows, child)


def cut_low_kernel(at_ref, x_ref, o_ref):
    q = at_ref[1]
    o_ref[...] = jnp.zeros(o_ref.shape, F32)
    for owner in range(2):

        @pl.when(q == owner)
        def _():
            for c in range(4):
                tile = x_ref[pl.ds(c, 256, stride=8), :]
                o_ref[:, 0, :, owner * 512 + c * 128 : owner * 512 + c * 128 + 128] = tile.reshape(16, 16, 128)


def cut_low(at, front_rows):
    return pl.pallas_call(
        cut_low_kernel,
        grid=(6,),
        out_shape=jax.ShapeDtypeStruct((16, 6, 16, 1024), F32),
        in_specs=[SMEM, pl.BlockSpec((2048, 128), lambda i: (i + 2, 0))],
        out_specs=pl.BlockSpec((16, 1, 16, 1024), lambda i: (0, i, 0, 0)),
        cost_estimate=pl.CostEstimate(flops=0, bytes_accessed=12 * MIB, transcendentals=0),
    )(at, front_rows)


def add_pieces(value, slot_ref, c_ref, row, j):
    for child in range(2):
        slot = slot_ref[(row * 4 + j) * 2 + child]
        known = jnp.maximum(slot, 0)
        piece = c_ref[known // 6, lax.rem(known, 6)].astype(F32)
        value = value + jnp.where(slot >= 0, piece, F32(0))
    return value


def join_top_kernel(slot_ref, c_ref, o_ref):
    for i in range(2):
        for j in range(4):
            at = 6 + i * 4 + j % 2 * 2
            value = c_ref[j // 2, at].astype(F32) + c_ref[j // 2, at + 1].astype(F32)
            o_ref[i, :, j * 256 : (j + 1) * 256] = add_pieces(value, slot_ref, c_ref, i, j)


def join_low_kernel(slot_ref, c_ref, f_ref, o_ref):
    for i in range(6):
        for j in range(4):
            lanes = slice(j * 256, (j + 1) * 256)
            o_ref[i, :, lanes] = add_pieces(f_ref[i, :, lanes], slot_ref, c_ref, i + 2, j)


def join_strips(kernel, count, slots, *operands):
    return pl.pallas_call(
        kernel,
        out_shape=jax.ShapeDtypeStruct((count, 16, 1024), F32),
        in_specs=[SMEM] + [VMEM] * len(operands),
        out_specs=VMEM,
        cost_estimate=pl.CostEstimate(flops=0, bytes_accessed=3 * MIB, transcendentals=0),
    )(slots, *operands)


def solve_first_kernel(keep_ref, d_ref, r_ref, w_ref, o_ref):
    width = w_ref.shape[0]
    b = jnp.concatenate(
        [d_ref[:, :, :width].reshape(32, width), r_ref[:, :, :width].reshape(96, width)], axis=0
    )
    x = dot3(b, w_ref[...], NT).reshape(8, 16, width)
    for i in range(8):
        o_ref[i] = jnp.where(keep_ref[i] > 0, x[i], F32(0)).astype(BF16)


def solve_second_kernel(keep_ref, d_ref, r_ref, p_ref, p10_ref, w_ref, o_ref):
    width = w_ref.shape[0]
    half = width // 2
    b = jnp.concatenate(
        [d_ref[:, :, width:].reshape(32, width), r_ref[:, :, width:].reshape(96, width)], axis=0
    )
    u = dot1(p_ref[...].reshape(128, width), p10_ref[...], NT)
    rows = []
    for i in range(8):
        s = slice(16 * i, 16 * i + 16)
        parts = []
        for j in range(2):
            c = slice(j * half, (j + 1) * half)
            parts.append(b[s, c] - jnp.where(keep_ref[8 + 2 * i + j] > 0, u[s, c], F32(0)))
        rows.append(jnp.concatenate(parts, axis=1))
    x = dot3(jnp.concatenate(rows, axis=0), w_ref[...], NT).reshape(8, 16, width)
    for i in range(8):
        o_ref[i] = jnp.where(keep_ref[i] > 0, x[i], F32(0)).astype(BF16)


def solve_strips(kernel, *operands):
    return pl.pallas_call(
        kernel,
        out_shape=jax.ShapeDtypeStruct((8, 16, 512), BF16),
        in_specs=[SMEM] + [VMEM] * (len(operands) - 1),
        out_specs=VMEM,
        cost_estimate=pl.CostEstimate(flops=400_000_000, bytes_accessed=2 * MIB, transcendentals=0),
    )(*operands)


def deal_kernel(at_ref, p0_ref, p1_ref, *refs):
    o_ref = refs[-1]
    for q in range(16):
        o_ref[q, 0:8] = p0_ref[...]
        o_ref[q, 8:16] = p1_ref[...]
    for panel in range(2):
        for k in range(4):
            row = lax.rem(at_ref[2] + k, 4) * 2
            for c in range(2):
                for lr in range(4):
                    o_ref[(lr % 2) * 8 + row + c, 16 + panel * 2 + lr // 2] = refs[panel * 4 + k][c, lr]


def deal(at, P0, P1, first, second):
    return pl.pallas_call(
        deal_kernel,
        out_shape=jax.ShapeDtypeStruct((16, 20, 16, 512), BF16),
        in_specs=[SMEM] + [VMEM] * 10,
        out_specs=VMEM,
        cost_estimate=pl.CostEstimate(flops=0, bytes_accessed=8 * MIB, transcendentals=0),
        compiler_params=pltpu.CompilerParams(vmem_limit_bytes=24 * MIB),
    )(at, P0, P1, *first, *second)


def extend_kernel(slot_ref, f_ref, *refs):
    child, o_ref = refs[:8], refs[8]
    i = pl.program_id(0)
    for j in range(4):
        live = [slot_ref[(i * 4 + j) * 2 + ch] >= 0 for ch in range(2)]
        pieces = [child[j * 2 + ch] for ch in range(2)]
        for c in range(2):
            lanes = slice(c * 128, (c + 1) * 128)
            rows = pl.ds(j * 2 + c, 256, stride=8)
            value = f_ref[rows, :]
            for ch in range(2):
                value = value + jnp.where(live[ch], pieces[ch][0, :, lanes].astype(F32), F32(0))
            o_ref[rows, :] = value


def extend(slots, front_rows, arrived):
    def child_spec(k):
        return pl.BlockSpec((1, 256, 256), lambda i, s: (jnp.maximum(s[i * 8 + k], 0), 0, 0))

    return pl.pallas_call(
        extend_kernel,
        grid_spec=pltpu.PrefetchScalarGridSpec(
            num_scalar_prefetch=1,
            grid=(8,),
            in_specs=[pl.BlockSpec((2048, 128), lambda i, s: (i, 0))] + [child_spec(k) for k in range(8)],
            out_specs=pl.BlockSpec((2048, 128), lambda i, s: (i, 0)),
        ),
        out_shape=jax.ShapeDtypeStruct(front_rows.shape, F32),
        cost_estimate=pl.CostEstimate(flops=0, bytes_accessed=24 * MIB, transcendentals=0),
        compiler_params=pltpu.CompilerParams(vmem_limit_bytes=24 * MIB),
    )(slots, front_rows, *([arrived] * 8))


def finish_kernel(flag_ref, f_ref, row0_ref, row1_ref, mine_ref, other_ref, l_ref, w_ref, o_ref, cols_ref, wh_ref, wl_ref):
    i = pl.program_id(0)

    @pl.when(i == 0)
    def _():
        core = flag_ref[48]
        for ref, sub in ((mine_ref, core), (other_ref, 1 - core)):
            for panel in range(2):
                for lc in range(2):
                    strips = ref[:, panel * 2 + lc].reshape(256, 512)
                    cols_ref[lc * 2 + sub, :, panel * 512 : (panel + 1) * 512] = strips

    @pl.when((i == 0) & (flag_ref[49] > 0))
    def _():
        wh_ref[...], wl_ref[...] = split(w_ref[...])

    rows = jnp.concatenate([ref[:, 0].reshape(256, 512) for ref in (row0_ref, row1_ref)], axis=1)
    for lc in range(2):
        state = flag_ref[32 + i * 2 + lc]

        @pl.when(state > 0)
        def _():
            blocks = []
            for sc in range(2):
                j = lc * 2 + sc
                value = jnp.concatenate(
                    [f_ref[pl.ds(lc * 4 + sc * 2 + c, 256, stride=8), :] for c in range(2)], axis=1
                )
                product = dot1(rows, cols_ref[j], NT)
                blocks.append(value - jnp.where(flag_ref[i * 4 + j] > 0, product, F32(0)))
            block = jnp.concatenate(blocks, axis=1)

            def put(value):
                for c in range(4):
                    o_ref[pl.ds(lc * 4 + c, 256, stride=8), :] = value[:, c * 128 : (c + 1) * 128]

            @pl.when(state == 1)
            def _():
                put(block)

            if lc == 0:

                @pl.when(state == 2)
                def _():
                    high, low = split(block)
                    wh = wh_ref[...]
                    put(dot1(high, wh, NT) + (dot1(low, wh, NT) + dot1(high, wl_ref[...], NT)))

                @pl.when(state == 3)
                def _():
                    put(l_ref[pl.ds(pl.multiple_of(lax.rem(i, 2) * 256, 256), 256), :])

        @pl.when(state == 0)
        def _():
            for c in range(4):
                o_ref[pl.ds(lc * 4 + c, 256, stride=8), :] = jnp.zeros((256, 128), F32)


def finish(flags, extended, dealt, other, L, W):
    def whole(shape, *at):
        return pl.BlockSpec(shape, lambda i, f: at)

    return pl.pallas_call(
        finish_kernel,
        grid_spec=pltpu.PrefetchScalarGridSpec(
            num_scalar_prefetch=1,
            grid=(8,),
            in_specs=[pl.BlockSpec((2048, 128), lambda i, f: (i, 0))]
            + [pl.BlockSpec((16, 1, 16, 512), lambda i, f: (0, i, 0, 0))]
            + [pl.BlockSpec((16, 1, 16, 512), lambda i, f: (0, i + 8, 0, 0))]
            + [whole((16, 4, 16, 512), 0, 4, 0, 0), whole((16, 4, 16, 512), 0, 0, 0, 0)]
            + [whole((512, 512), 0, 0)] * 2,
            out_specs=pl.BlockSpec((2048, 128), lambda i, f: (i, 0)),
            scratch_shapes=[pltpu.VMEM((4, 256, 1024), BF16)] + [pltpu.VMEM((512, 512), BF16)] * 2,
        ),
        out_shape=jax.ShapeDtypeStruct(extended.shape, F32),
        cost_estimate=pl.CostEstimate(flops=5_000_000_000, bytes_accessed=24 * MIB, transcendentals=0),
        compiler_params=pltpu.CompilerParams(vmem_limit_bytes=48 * MIB),
    )(flags, extended, dealt, dealt, dealt, other, L, W)


def slot_of_targets(codes, row_map, rows, cols):
    index = jnp.arange(CNB, dtype=jnp.int32)

    def place(blocks):
        hit = row_map[None] == blocks[:, None, None]
        return jnp.sum(jnp.where(hit, index + 1, 0), axis=-1) - 1

    pi, pj = place(rows), place(cols)
    child = jnp.arange(2, dtype=jnp.int32) * (CNB * CNB)
    wanted = child + pi[:, None, :] * CNB + pj[None, :, :]
    known = (pi[:, None, :] >= 0) & (pj[None, :, :] >= 0)
    wanted = jnp.where(known, wanted, -2).reshape(-1)
    number = jnp.arange(codes.shape[0], dtype=jnp.int32)
    return jnp.sum(jnp.where(wanted[:, None] == codes[None, :], number + 1, 0), axis=-1) - 1


def spread(x, axis, count):
    return lax.all_to_all(jnp.broadcast_to(x[None], (count,) + x.shape), axis, 0, 0, tiled=True)


def local(front, child_blocks, row_map, slot_table, struct_mask):
    prow, pcol = lax.axis_size("prow"), lax.axis_size("pcol")
    p, q = lax.axis_index("prow"), lax.axis_index("pcol")
    core, y = p % 2, p // 2
    at = jnp.stack([core, q, y]).astype(jnp.int32)
    swap = [(i, i ^ 1) for i in range(8)]
    front_rows = front.reshape(16384, 128)
    child = child_blocks[0, 0]

    pair = jnp.arange(2, dtype=jnp.int32)
    row_blocks = jnp.arange(4, dtype=jnp.int32) * prow + p
    col_blocks = jnp.arange(2, dtype=jnp.int32) * pcol + q
    sub_rows = (2 * row_blocks[:, None] + pair).reshape(-1)
    sub_cols = (2 * col_blocks[:, None] + pair).reshape(-1)

    low_cut = cut_low(at, front_rows)
    low_front = lax.psum_scatter(
        low_cut.reshape(96, 16, 1024), "pcol", scatter_dimension=0, tiled=True
    )
    front_top, _ = lax.optimization_barrier((front_rows, low_cut))
    got = lax.all_to_all(cut_top(front_top, child.reshape(48, 256, 256)), "pcol", 0, 0, tiled=True)

    my_codes = lax.dynamic_index_in_dim(slot_table, p, 0, False)
    strip_slots = slot_of_targets(my_codes[:, :2].reshape(-1), row_map, sub_rows, jnp.arange(4, dtype=jnp.int32))
    slots = slot_of_targets(
        lax.dynamic_index_in_dim(my_codes, q, 1, False).reshape(-1), row_map, sub_rows, sub_cols
    )
    row_mask = struct_mask[sub_rows]
    lower = row_blocks[:, None] >= col_blocks[None, :]
    mask = row_mask[:, sub_cols]
    state = jnp.where(lower, 1, 0)
    owner = (q < 2) & (jnp.arange(2) == 0)
    state = jnp.where(owner[None, :] & lower, jnp.where(row_blocks[:, None] == q, 3, 2), state)
    flags = jnp.concatenate([mask.reshape(-1), jnp.repeat(state, 2, axis=0).reshape(-1), jnp.stack([core, 2 - q])])
    flags = flags.astype(jnp.int32)
    keep0 = (sub_rows >= 2).astype(jnp.int32)
    keep1 = jnp.concatenate([(sub_rows >= 4).astype(jnp.int32), row_mask[:, 2:4].reshape(-1)])

    top = join_strips(join_top_kernel, 2, strip_slots, got)

    half_top = lax.all_to_all(jnp.tile(top, (prow // 2, 1, 1)), "prow", 0, 0, tiled=True)
    first = spread(jnp.concatenate([half_top[0, :, :512], half_top[1]], axis=1), "pcol", pcol)
    diag = (first, lax.ppermute(first, "prow", swap))
    child, diag, low_front = lax.optimization_barrier((child, diag, low_front))
    arrived = lax.all_to_all(child, "pcol", 0, 0, tiled=True).reshape(48, 256, 256)

    def gather_columns(strips):
        halves = strips.reshape(4, 2, 16, 512)
        even, odd = halves[:, 0], halves[:, 1]
        sent = lax.ppermute(jnp.where(core == 0, odd, even), "prow", swap)
        kept = jnp.where(core == 0, even, odd)
        chip = jnp.where(core == 0, jnp.stack([kept, sent]), jnp.stack([sent, kept]))
        along = lambda k: [(2 * ((i + k) % 4) + c, 2 * i + c) for i in range(4) for c in range(2)]
        return [chip] + [lax.ppermute(chip, "prow", along(k)) for k in range(1, 4)]

    L0, W0 = factor_first(at, *diag)
    low = join_strips(join_low_kernel, 6, strip_slots, got, low_front)
    P0 = solve_strips(solve_first_kernel, keep0, top, low, W0)
    P0, diag = lax.optimization_barrier((P0, diag))
    cols0 = gather_columns(P0)
    P10, L1, W1 = factor_second(at, struct_mask[2:4, 2:4].reshape(-1), *diag, W0)
    W1, cols0 = lax.optimization_barrier((W1, cols0))
    P1 = solve_strips(solve_second_kernel, keep1, top, low, P0, P10, W1)
    cols1 = gather_columns(P1)

    dealt = deal(at, P0, P1, cols0, cols1)
    dealt, arrived = lax.optimization_barrier((dealt, arrived))
    dealt = lax.all_to_all(dealt, "pcol", 0, 0, tiled=True)
    extended = extend(slots, front_rows, arrived)
    L = jnp.where(q == 0, L0, L1)
    W = jnp.where(q == 0, W0, W1)
    dealt, extended, L, W = lax.optimization_barrier((dealt, extended, L, W))
    other = lax.ppermute(dealt[:, 16:], "prow", swap)
    out = finish(flags, extended, dealt, other, L, W)
    return out.reshape(front.shape)


def solution(mesh):
    in_specs = (
        P(None, "prow", None, None, "pcol", None),
        P("prow", "pcol", None, None, None, None),
        P(),
        P(),
        P(),
    )
    out_specs = P(None, "prow", None, None, "pcol", None)
    return jax.shard_map(local, mesh=mesh, in_specs=in_specs, out_specs=out_specs, check_vma=False)
```

```python
import functools

import jax
import jax.numpy as jnp
from jax import lax
from jax.experimental import pallas as pl
from jax.experimental.pallas import tpu as pltpu
from jax.sharding import PartitionSpec as P

F32 = jnp.float32
BF16 = jnp.bfloat16
CNB = 60
NN = (((1,), (0,)), ((), ()))
NT = (((1,), (1,)), ((), ()))
MIB = 2**20
VMEM = pl.BlockSpec(memory_space=pltpu.VMEM)
SMEM = pl.BlockSpec(memory_space=pltpu.SMEM)


def split(x):
    high = x.astype(BF16)
    return high, (x - high.astype(F32)).astype(BF16)


def dot1(a, b, dims):
    return lax.dot_general(a, b, dims, preferred_element_type=F32)


def dot3(a, b, dims):
    ah, al = split(a)
    bh, bl = split(b)
    return dot1(ah, bh, dims) + (dot1(al, bh, dims) + dot1(ah, bl, dims))


GROUPS = 4


def eliminate(R, n):
    row = lax.broadcasted_iota(jnp.int32, (8, 1), 0)
    across = lambda v: jnp.concatenate([v, v], axis=1)
    over = lambda x, lane: jnp.broadcast_to(x[:, lane : lane + 1], (8, 128))
    done = []
    for g in range(len(R)):
        base = 8 * g
        later = range(g + 1, len(R))
        cols = [over(R[g], base + j) for j in range(8)]
        below = {h: [over(R[h], base + j) for j in range(8)] for h in later}
        D = [[jnp.broadcast_to(cols[j][i : i + 1], (8, 128)) for j in range(i + 1)] for i in range(8)]
        Y = [jnp.broadcast_to(R[g][i : i + 1], (8, 2 * n)) for i in range(8)]
        out = None
        for j in range(8):
            scale = lax.rsqrt(D[j][j])
            inverse = scale * scale
            for i in range(j + 1, 8):
                factor = D[i][j] * inverse
                for m in range(j + 1, i):
                    D[i][m] = D[i][m] - factor * D[m][j]
                D[i][i] = D[i][i] - (D[i][j] * D[i][j]) * inverse
                Y[i] = Y[i] - across(factor) * Y[j]
            for h in later:
                factor = below[h][j] * inverse
                for m in range(j + 1, 8):
                    below[h][m] = below[h][m] - factor * D[m][j]
                R[h] = R[h] - across(factor) * Y[j]
            scaled = Y[j] * across(scale)
            out = scaled if out is None else jnp.where(row == j, scaled, out)
        done.append(out)
    return jnp.concatenate(done, axis=0)


def factor_base(m_ref, o_ref):
    n = m_ref.shape[0]
    step = 8 * GROUPS

    def body(k, _):
        at = k * step
        rows = pl.ds(pl.multiple_of(at, step), step)
        X = m_ref[rows, :]
        A = pltpu.roll(X[:, :n], jnp.where(k == 0, 0, n - at), 1)
        X = jnp.concatenate([A, X[:, n:]], axis=1)
        out = eliminate([X[8 * g : 8 * g + 8] for g in range(GROUPS)], n)
        out = jnp.concatenate([pltpu.roll(out[:, :n], at, 1), out[:, n:]], axis=1)
        o_ref[rows, :] = out
        m_ref[...] = m_ref[...] - dot3(out[:, :n].T, out, NN)
        return 0

    lax.fori_loop(0, n // step, body, 0)


def factor_whole(a_ref, l_ref, w_ref, m_ref, o_ref):
    n = a_ref.shape[0]
    b = 128
    w_ref[...] = jnp.zeros((n, n), F32)
    l_ref[...] = jnp.zeros((n, n), F32)
    lane = lax.broadcasted_iota(jnp.int32, (b, b), 1)
    sub = lax.broadcasted_iota(jnp.int32, (b, b), 0)
    for k in range(0, n, b):
        s = slice(k, k + b)
        D = a_ref[s, s]
        m_ref[:, :b] = jnp.where(sub >= lane, D, D.T)
        m_ref[:, b:] = jnp.where(lane == sub, F32(1), F32(0))
        factor_base(m_ref, o_ref)
        W = jnp.where(lane <= sub, o_ref[:, b:], F32(0))
        l_ref[s, s] = jnp.where(lane >= sub, o_ref[:, :b], F32(0)).T
        w_ref[s, s] = W
        if k:
            T = dot3(l_ref[s, :k], w_ref[:k, :k], NN)
            w_ref[s, :k] = -dot3(W, T, NN)
        if k + b < n:
            L = dot3(a_ref[k + b :, s], W, NT)
            l_ref[k + b :, s] = L
            for j in range(k + b, n, b):
                off = j - k - b
                a_ref[j:, j : j + b] = a_ref[j:, j : j + b] - dot3(L[off:], L[off : off + b], NT)


def factor_first_kernel(at_ref, mine_ref, other_ref, l_ref, w_ref, a_ref, m_ref, o_ref):
    n = a_ref.shape[0]
    for ref, sub in ((mine_ref, at_ref[0]), (other_ref, 1 - at_ref[0])):
        a_ref[pl.ds(pl.multiple_of(sub * 256, 256), 256), :] = ref[:, :, :n].reshape(256, n)
    factor_whole(a_ref, l_ref, w_ref, m_ref, o_ref)


def factor_second_kernel(
    at_ref, mask_ref, mine_ref, other_ref, w0_ref, p_ref, l_ref, w_ref, a_ref, m_ref, o_ref, b_ref
):
    n = a_ref.shape[0]
    for ref, sub in ((mine_ref, at_ref[0]), (other_ref, 1 - at_ref[0])):
        rows = pl.ds(pl.multiple_of(sub * 256, 256), 256)
        b_ref[rows, :] = ref[:, :, n : 2 * n].reshape(256, n)
        a_ref[rows, :] = ref[:, :, 2 * n :].reshape(256, n)
    panel = dot3(b_ref[...], w0_ref[...], NT).astype(BF16)
    p_ref[...] = panel
    h = n // 2
    for i in range(2):
        for j in range(i + 1):
            r, c = slice(i * h, (i + 1) * h), slice(j * h, (j + 1) * h)
            product = dot1(panel[r], panel[c], NT)
            a_ref[r, c] = a_ref[r, c] - jnp.where(mask_ref[i * 2 + j] > 0, product, F32(0))
    factor_whole(a_ref, l_ref, w_ref, m_ref, o_ref)


CHOL_COST = pl.CostEstimate(flops=20_000_000_000, bytes_accessed=3 * MIB, transcendentals=1024)


def factor_first(at, mine, other):
    n = mine.shape[-1] // 3
    return pl.pallas_call(
        factor_first_kernel,
        out_shape=[jax.ShapeDtypeStruct((n, n), F32)] * 2,
        in_specs=[SMEM, VMEM, VMEM],
        out_specs=[VMEM] * 2,
        scratch_shapes=[pltpu.VMEM((n, n), F32)] + [pltpu.VMEM((128, 256), F32)] * 2,
        cost_estimate=CHOL_COST,
        compiler_params=pltpu.CompilerParams(vmem_limit_bytes=40 * MIB),
    )(at, mine, other)


def factor_second(at, mask, mine, other, W0):
    n = W0.shape[0]
    return pl.pallas_call(
        factor_second_kernel,
        out_shape=[jax.ShapeDtypeStruct((n, n), BF16)] + [jax.ShapeDtypeStruct((n, n), F32)] * 2,
        in_specs=[SMEM, SMEM, VMEM, VMEM, VMEM],
        out_specs=[VMEM] * 3,
        scratch_shapes=[pltpu.VMEM((n, n), F32)]
        + [pltpu.VMEM((128, 256), F32)] * 2
        + [pltpu.VMEM((n, n), F32)],
        cost_estimate=CHOL_COST,
        compiler_params=pltpu.CompilerParams(vmem_limit_bytes=40 * MIB),
    )(at, mask, mine, other, W0)


def cut_top_kernel(x_ref, c_ref, o_ref):
    for k in range(6):
        o_ref[:, k] = c_ref[k].reshape(16, 16, 256)
    for i in range(3):
        for c in range(4):
            high, low = split(x_ref[pl.ds(i * 2048 + c, 256, stride=8), :])
            at = 6 + i * 4 + c // 2 * 2
            lanes = slice(c % 2 * 128, c % 2 * 128 + 128)
            o_ref[:, at, :, lanes] = high.reshape(16, 16, 128)
            o_ref[:, at + 1, :, lanes] = low.reshape(16, 16, 128)


def cut_top(front_rows, child):
    return pl.pallas_call(
        cut_top_kernel,
        grid=(1,),
        out_shape=jax.ShapeDtypeStruct((16, 18, 16, 256), BF16),
        in_specs=[
            pl.BlockSpec((6144, 128), lambda i: (0, 0)),
            pl.BlockSpec((6, 256, 256), lambda i: (0, 0, 0)),
        ],
        out_specs=pl.BlockSpec((16, 18, 16, 256), lambda i: (0, 0, 0, 0)),
        cost_estimate=pl.CostEstimate(flops=0, bytes_accessed=5 * MIB, transcendentals=0),
        compiler_params=pltpu.CompilerParams(vmem_limit_bytes=40 * MIB),
    )(front_rows, child)


def cut_low_kernel(at_ref, x_ref, o_ref):
    q = at_ref[1]
    o_ref[...] = jnp.zeros(o_ref.shape, F32)
    for owner in range(2):

        @pl.when(q == owner)
        def _():
            for c in range(4):
                tile = x_ref[pl.ds(c, 256, stride=8), :]
                o_ref[:, 0, :, owner * 512 + c * 128 : owner * 512 + c * 128 + 128] = tile.reshape(16, 16, 128)


def cut_low(at, front_rows):
    return pl.pallas_call(
        cut_low_kernel,
        grid=(5,),
        out_shape=jax.ShapeDtypeStruct((16, 5, 16, 1024), F32),
        in_specs=[SMEM, pl.BlockSpec((2048, 128), lambda i: (i + 3, 0))],
        out_specs=pl.BlockSpec((16, 1, 16, 1024), lambda i: (0, i, 0, 0)),
        cost_estimate=pl.CostEstimate(flops=0, bytes_accessed=12 * MIB, transcendentals=0),
    )(at, front_rows)


def add_pieces(value, slot_ref, c_ref, row, j):
    for child in range(2):
        slot = slot_ref[(row * 4 + j) * 2 + child]
        known = jnp.maximum(slot, 0)
        piece = c_ref[known // 6, lax.rem(known, 6)].astype(F32)
        value = value + jnp.where(slot >= 0, piece, F32(0))
    return value


def whole_piece(c_ref, row, j):
    at = 6 + row * 4 + j % 2 * 2
    return c_ref[j // 2, at].astype(F32) + c_ref[j // 2, at + 1].astype(F32)


def join_top_kernel(slot_ref, c_ref, o_ref):
    for i in range(2):
        for j in range(4):
            value = whole_piece(c_ref, i, j)
            o_ref[i, :, j * 256 : (j + 1) * 256] = add_pieces(value, slot_ref, c_ref, i, j)


def join_low_kernel(slot_ref, c_ref, f_ref, o_ref):
    for i in range(6):
        for j in range(4):
            lanes = slice(j * 256, (j + 1) * 256)
            value = f_ref[i - 1, :, lanes] if i else whole_piece(c_ref, 2, j)
            o_ref[i, :, lanes] = add_pieces(value, slot_ref, c_ref, i + 2, j)


def join_strips(kernel, count, slots, *operands):
    return pl.pallas_call(
        kernel,
        out_shape=jax.ShapeDtypeStruct((count, 16, 1024), F32),
        in_specs=[SMEM] + [VMEM] * len(operands),
        out_specs=VMEM,
        cost_estimate=pl.CostEstimate(flops=0, bytes_accessed=3 * MIB, transcendentals=0),
    )(slots, *operands)


def solve_first_kernel(keep_ref, d_ref, r_ref, w_ref, o_ref):
    width = w_ref.shape[0]
    b = jnp.concatenate(
        [d_ref[:, :, :width].reshape(32, width), r_ref[:, :, :width].reshape(96, width)], axis=0
    )
    x = dot3(b, w_ref[...], NT).reshape(8, 16, width)
    for i in range(8):
        o_ref[i] = jnp.where(keep_ref[i] > 0, x[i], F32(0)).astype(BF16)


def solve_second_kernel(keep_ref, d_ref, r_ref, p_ref, p10_ref, w_ref, o_ref):
    width = w_ref.shape[0]
    half = width // 2
    b = jnp.concatenate(
        [d_ref[:, :, width:].reshape(32, width), r_ref[:, :, width:].reshape(96, width)], axis=0
    )
    u = dot1(p_ref[...].reshape(128, width), p10_ref[...], NT)
    rows = []
    for i in range(8):
        s = slice(16 * i, 16 * i + 16)
        parts = []
        for j in range(2):
            c = slice(j * half, (j + 1) * half)
            parts.append(b[s, c] - jnp.where(keep_ref[8 + 2 * i + j] > 0, u[s, c], F32(0)))
        rows.append(jnp.concatenate(parts, axis=1))
    x = dot3(jnp.concatenate(rows, axis=0), w_ref[...], NT).reshape(8, 16, width)
    for i in range(8):
        o_ref[i] = jnp.where(keep_ref[i] > 0, x[i], F32(0)).astype(BF16)


def solve_strips(kernel, *operands):
    return pl.pallas_call(
        kernel,
        out_shape=jax.ShapeDtypeStruct((8, 16, 512), BF16),
        in_specs=[SMEM] + [VMEM] * (len(operands) - 1),
        out_specs=VMEM,
        cost_estimate=pl.CostEstimate(flops=400_000_000, bytes_accessed=2 * MIB, transcendentals=0),
    )(*operands)


def deal_kernel(at_ref, p0_ref, p1_ref, *refs):
    o_ref = refs[-1]
    for q in range(16):
        o_ref[q, 0:8] = p0_ref[...]
        o_ref[q, 8:16] = p1_ref[...]
    for panel in range(2):
        for k in range(4):
            row = lax.rem(at_ref[2] + k, 4) * 2
            for c in range(2):
                for lr in range(4):
                    o_ref[(lr % 2) * 8 + row + c, 16 + panel * 2 + lr // 2] = refs[panel * 4 + k][c, lr]


def deal(at, P0, P1, first, second):
    return pl.pallas_call(
        deal_kernel,
        out_shape=jax.ShapeDtypeStruct((16, 20, 16, 512), BF16),
        in_specs=[SMEM] + [VMEM] * 10,
        out_specs=VMEM,
        cost_estimate=pl.CostEstimate(flops=0, bytes_accessed=8 * MIB, transcendentals=0),
        compiler_params=pltpu.CompilerParams(vmem_limit_bytes=24 * MIB),
    )(at, P0, P1, *first, *second)


def extend_kernel(slot_ref, f_ref, *refs):
    child, o_ref = refs[:8], refs[8]
    i = pl.program_id(0)
    for j in range(4):
        live = [slot_ref[(i * 4 + j) * 2 + ch] >= 0 for ch in range(2)]
        pieces = [child[j * 2 + ch] for ch in range(2)]
        for c in range(2):
            lanes = slice(c * 128, (c + 1) * 128)
            rows = pl.ds(j * 2 + c, 256, stride=8)
            value = f_ref[rows, :]
            for ch in range(2):
                value = value + jnp.where(live[ch], pieces[ch][0, :, lanes].astype(F32), F32(0))
            o_ref[rows, :] = value


def extend(slots, front_rows, arrived):
    def child_spec(k):
        return pl.BlockSpec((1, 256, 256), lambda i, s: (jnp.maximum(s[i * 8 + k], 0), 0, 0))

    return pl.pallas_call(
        extend_kernel,
        grid_spec=pltpu.PrefetchScalarGridSpec(
            num_scalar_prefetch=1,
            grid=(8,),
            in_specs=[pl.BlockSpec((2048, 128), lambda i, s: (i, 0))] + [child_spec(k) for k in range(8)],
            out_specs=pl.BlockSpec((2048, 128), lambda i, s: (i, 0)),
        ),
        out_shape=jax.ShapeDtypeStruct(front_rows.shape, F32),
        cost_estimate=pl.CostEstimate(flops=0, bytes_accessed=24 * MIB, transcendentals=0),
        compiler_params=pltpu.CompilerParams(vmem_limit_bytes=24 * MIB),
    )(slots, front_rows, *([arrived] * 8))


def finish_kernel(flag_ref, f_ref, row0_ref, row1_ref, mine_ref, other_ref, l_ref, w_ref, o_ref, cols_ref, wh_ref, wl_ref):
    i = pl.program_id(0)

    @pl.when(i == 0)
    def _():
        core = flag_ref[48]
        for ref, sub in ((mine_ref, core), (other_ref, 1 - core)):
            for panel in range(2):
                for lc in range(2):
                    strips = ref[:, panel * 2 + lc].reshape(256, 512)
                    cols_ref[lc * 2 + sub, :, panel * 512 : (panel + 1) * 512] = strips

    @pl.when((i == 0) & (flag_ref[49] > 0))
    def _():
        wh_ref[...], wl_ref[...] = split(w_ref[...])

    rows = jnp.concatenate([ref[:, 0].reshape(256, 512) for ref in (row0_ref, row1_ref)], axis=1)
    for lc in range(2):
        state = flag_ref[32 + i * 2 + lc]

        @pl.when(state > 0)
        def _():
            blocks = []
            for sc in range(2):
                j = lc * 2 + sc
                value = jnp.concatenate(
                    [f_ref[pl.ds(lc * 4 + sc * 2 + c, 256, stride=8), :] for c in range(2)], axis=1
                )
                product = dot1(rows, cols_ref[j], NT)
                blocks.append(value - jnp.where(flag_ref[i * 4 + j] > 0, product, F32(0)))
            block = jnp.concatenate(blocks, axis=1)

            def put(value):
                for c in range(4):
                    o_ref[pl.ds(lc * 4 + c, 256, stride=8), :] = value[:, c * 128 : (c + 1) * 128]

            @pl.when(state == 1)
            def _():
                put(block)

            if lc == 0:

                @pl.when(state == 2)
                def _():
                    high, low = split(block)
                    wh = wh_ref[...]
                    put(dot1(high, wh, NT) + (dot1(low, wh, NT) + dot1(high, wl_ref[...], NT)))

                @pl.when(state == 3)
                def _():
                    put(l_ref[pl.ds(pl.multiple_of(lax.rem(i, 2) * 256, 256), 256), :])

        @pl.when(state == 0)
        def _():
            for c in range(4):
                o_ref[pl.ds(lc * 4 + c, 256, stride=8), :] = jnp.zeros((256, 128), F32)


def finish(flags, extended, dealt, other, L, W):
    def whole(shape, *at):
        return pl.BlockSpec(shape, lambda i, f: at)

    return pl.pallas_call(
        finish_kernel,
        grid_spec=pltpu.PrefetchScalarGridSpec(
            num_scalar_prefetch=1,
            grid=(8,),
            in_specs=[pl.BlockSpec((2048, 128), lambda i, f: (i, 0))]
            + [pl.BlockSpec((16, 1, 16, 512), lambda i, f: (0, i, 0, 0))]
            + [pl.BlockSpec((16, 1, 16, 512), lambda i, f: (0, i + 8, 0, 0))]
            + [whole((16, 4, 16, 512), 0, 4, 0, 0), whole((16, 4, 16, 512), 0, 0, 0, 0)]
            + [whole((512, 512), 0, 0)] * 2,
            out_specs=pl.BlockSpec((2048, 128), lambda i, f: (i, 0)),
            scratch_shapes=[pltpu.VMEM((4, 256, 1024), BF16)] + [pltpu.VMEM((512, 512), BF16)] * 2,
        ),
        out_shape=jax.ShapeDtypeStruct(extended.shape, F32),
        cost_estimate=pl.CostEstimate(flops=5_000_000_000, bytes_accessed=24 * MIB, transcendentals=0),
        compiler_params=pltpu.CompilerParams(vmem_limit_bytes=48 * MIB),
    )(flags, extended, dealt, dealt, dealt, other, L, W)


def slot_of_targets(codes, row_map, rows, cols):
    index = jnp.arange(CNB, dtype=jnp.int32)

    def place(blocks):
        hit = row_map[None] == blocks[:, None, None]
        return jnp.sum(jnp.where(hit, index + 1, 0), axis=-1) - 1

    pi, pj = place(rows), place(cols)
    child = jnp.arange(2, dtype=jnp.int32) * (CNB * CNB)
    wanted = child + pi[:, None, :] * CNB + pj[None, :, :]
    known = (pi[:, None, :] >= 0) & (pj[None, :, :] >= 0)
    wanted = jnp.where(known, wanted, -2).reshape(-1)
    number = jnp.arange(codes.shape[0], dtype=jnp.int32)
    return jnp.sum(jnp.where(wanted[:, None] == codes[None, :], number + 1, 0), axis=-1) - 1


def spread(x, axis, count):
    return lax.all_to_all(jnp.broadcast_to(x[None], (count,) + x.shape), axis, 0, 0, tiled=True)


def local(front, child_blocks, row_map, slot_table, struct_mask):
    prow, pcol = lax.axis_size("prow"), lax.axis_size("pcol")
    p, q = lax.axis_index("prow"), lax.axis_index("pcol")
    core, y = p % 2, p // 2
    at = jnp.stack([core, q, y]).astype(jnp.int32)
    swap = [(i, i ^ 1) for i in range(8)]
    front_rows = front.reshape(16384, 128)
    child = child_blocks[0, 0]

    pair = jnp.arange(2, dtype=jnp.int32)
    row_blocks = jnp.arange(4, dtype=jnp.int32) * prow + p
    col_blocks = jnp.arange(2, dtype=jnp.int32) * pcol + q
    sub_rows = (2 * row_blocks[:, None] + pair).reshape(-1)
    sub_cols = (2 * col_blocks[:, None] + pair).reshape(-1)

    low_cut = cut_low(at, front_rows)
    low_front = lax.psum_scatter(
        low_cut.reshape(80, 16, 1024), "pcol", scatter_dimension=0, tiled=True
    )
    front_top, _ = lax.optimization_barrier((front_rows, low_cut))
    got = lax.all_to_all(cut_top(front_top, child.reshape(48, 256, 256)), "pcol", 0, 0, tiled=True)

    my_codes = lax.dynamic_index_in_dim(slot_table, p, 0, False)
    strip_slots = slot_of_targets(my_codes[:, :2].reshape(-1), row_map, sub_rows, jnp.arange(4, dtype=jnp.int32))
    slots = slot_of_targets(
        lax.dynamic_index_in_dim(my_codes, q, 1, False).reshape(-1), row_map, sub_rows, sub_cols
    )
    row_mask = struct_mask[sub_rows]
    lower = row_blocks[:, None] >= col_blocks[None, :]
    mask = row_mask[:, sub_cols]
    state = jnp.where(lower, 1, 0)
    owner = (q < 2) & (jnp.arange(2) == 0)
    state = jnp.where(owner[None, :] & lower, jnp.where(row_blocks[:, None] == q, 3, 2), state)
    flags = jnp.concatenate([mask.reshape(-1), jnp.repeat(state, 2, axis=0).reshape(-1), jnp.stack([core, 2 - q])])
    flags = flags.astype(jnp.int32)
    keep0 = (sub_rows >= 2).astype(jnp.int32)
    keep1 = jnp.concatenate([(sub_rows >= 4).astype(jnp.int32), row_mask[:, 2:4].reshape(-1)])

    top = join_strips(join_top_kernel, 2, strip_slots, got)

    half_top = lax.all_to_all(jnp.tile(top, (prow // 2, 1, 1)), "prow", 0, 0, tiled=True)
    first = spread(jnp.concatenate([half_top[0, :, :512], half_top[1]], axis=1), "pcol", pcol)
    diag = (first, lax.ppermute(first, "prow", swap))
    child, diag, low_front = lax.optimization_barrier((child, diag, low_front))
    arrived = lax.all_to_all(child, "pcol", 0, 0, tiled=True).reshape(48, 256, 256)

    def gather_columns(strips):
        halves = strips.reshape(4, 2, 16, 512)
        even, odd = halves[:, 0], halves[:, 1]
        sent = lax.ppermute(jnp.where(core == 0, odd, even), "prow", swap)
        kept = jnp.where(core == 0, even, odd)
        chip = jnp.where(core == 0, jnp.stack([kept, sent]), jnp.stack([sent, kept]))
        along = lambda k: [(2 * ((i + k) % 4) + c, 2 * i + c) for i in range(4) for c in range(2)]
        return [chip] + [lax.ppermute(chip, "prow", along(k)) for k in range(1, 4)]

    L0, W0 = factor_first(at, *diag)
    low = join_strips(join_low_kernel, 6, strip_slots, got, low_front)
    P0 = solve_strips(solve_first_kernel, keep0, top, low, W0)
    P0, diag = lax.optimization_barrier((P0, diag))
    cols0 = gather_columns(P0)
    P10, L1, W1 = factor_second(at, struct_mask[2:4, 2:4].reshape(-1), *diag, W0)
    W1, cols0 = lax.optimization_barrier((W1, cols0))
    P1 = solve_strips(solve_second_kernel, keep1, top, low, P0, P10, W1)
    cols1 = gather_columns(P1)

    dealt = deal(at, P0, P1, cols0, cols1)
    dealt, arrived = lax.optimization_barrier((dealt, arrived))
    dealt = lax.all_to_all(dealt, "pcol", 0, 0, tiled=True)
    extended = extend(slots, front_rows, arrived)
    L = jnp.where(q == 0, L0, L1)
    W = jnp.where(q == 0, W0, W1)
    dealt, extended, L, W = lax.optimization_barrier((dealt, extended, L, W))
    other = lax.ppermute(dealt[:, 16:], "prow", swap)
    out = finish(flags, extended, dealt, other, L, W)
    return out.reshape(front.shape)


def solution(mesh):
    in_specs = (
        P(None, "prow", None, None, "pcol", None),
        P("prow", "pcol", None, None, None, None),
        P(),
        P(),
        P(),
    )
    out_specs = P(None, "prow", None, None, "pcol", None)
    return jax.shard_map(local, mesh=mesh, in_specs=in_specs, out_specs=out_specs, check_vma=False)
```

```python
import functools

import jax
import jax.numpy as jnp
from jax import lax
from jax.experimental import pallas as pl
from jax.experimental.pallas import tpu as pltpu
from jax.sharding import PartitionSpec as P

F32 = jnp.float32
BF16 = jnp.bfloat16
CNB = 60
NN = (((1,), (0,)), ((), ()))
NT = (((1,), (1,)), ((), ()))
MIB = 2**20
VMEM = pl.BlockSpec(memory_space=pltpu.VMEM)
SMEM = pl.BlockSpec(memory_space=pltpu.SMEM)


def split(x):
    high = x.astype(BF16)
    return high, (x - high.astype(F32)).astype(BF16)


def dot1(a, b, dims):
    return lax.dot_general(a, b, dims, preferred_element_type=F32)


def dot3(a, b, dims):
    ah, al = split(a)
    bh, bl = split(b)
    return dot1(ah, bh, dims) + (dot1(al, bh, dims) + dot1(ah, bl, dims))


GROUPS = 4


def eliminate(R, n):
    row = lax.broadcasted_iota(jnp.int32, (8, 1), 0)
    across = lambda v: jnp.concatenate([v, v], axis=1)
    over = lambda x, lane: jnp.broadcast_to(x[:, lane : lane + 1], (8, 128))
    done = []
    for g in range(len(R)):
        base = 8 * g
        later = range(g + 1, len(R))
        cols = [over(R[g], base + j) for j in range(8)]
        below = {h: [over(R[h], base + j) for j in range(8)] for h in later}
        D = [[jnp.broadcast_to(cols[j][i : i + 1], (8, 128)) for j in range(i + 1)] for i in range(8)]
        Y = [jnp.broadcast_to(R[g][i : i + 1], (8, 2 * n)) for i in range(8)]
        out = None
        for j in range(8):
            scale = lax.rsqrt(D[j][j])
            inverse = scale * scale
            for i in range(j + 1, 8):
                factor = D[i][j] * inverse
                for m in range(j + 1, i):
                    D[i][m] = D[i][m] - factor * D[m][j]
                D[i][i] = D[i][i] - (D[i][j] * D[i][j]) * inverse
                Y[i] = Y[i] - across(factor) * Y[j]
            for h in later:
                factor = below[h][j] * inverse
                for m in range(j + 1, 8):
                    below[h][m] = below[h][m] - factor * D[m][j]
                R[h] = R[h] - across(factor) * Y[j]
            scaled = Y[j] * across(scale)
            out = scaled if out is None else jnp.where(row == j, scaled, out)
        done.append(out)
    return jnp.concatenate(done, axis=0)


def factor_base(m_ref, o_ref):
    n = m_ref.shape[0]
    step = 8 * GROUPS

    def body(k, _):
        at = k * step
        rows = pl.ds(pl.multiple_of(at, step), step)
        X = m_ref[rows, :]
        A = pltpu.roll(X[:, :n], jnp.where(k == 0, 0, n - at), 1)
        X = jnp.concatenate([A, X[:, n:]], axis=1)
        out = eliminate([X[8 * g : 8 * g + 8] for g in range(GROUPS)], n)
        out = jnp.concatenate([pltpu.roll(out[:, :n], at, 1), out[:, n:]], axis=1)
        o_ref[rows, :] = out
        m_ref[...] = m_ref[...] - dot3(out[:, :n].T, out, NN)
        return 0

    lax.fori_loop(0, n // step, body, 0)


def factor_whole(a_ref, l_ref, w_ref, m_ref, o_ref):
    n = a_ref.shape[0]
    b = 128
    w_ref[...] = jnp.zeros((n, n), F32)
    l_ref[...] = jnp.zeros((n, n), F32)
    lane = lax.broadcasted_iota(jnp.int32, (b, b), 1)
    sub = lax.broadcasted_iota(jnp.int32, (b, b), 0)
    for k in range(0, n, b):
        s = slice(k, k + b)
        D = a_ref[s, s]
        m_ref[:, :b] = jnp.where(sub >= lane, D, D.T)
        m_ref[:, b:] = jnp.where(lane == sub, F32(1), F32(0))
        factor_base(m_ref, o_ref)
        W = jnp.where(lane <= sub, o_ref[:, b:], F32(0))
        l_ref[s, s] = jnp.where(lane >= sub, o_ref[:, :b], F32(0)).T
        w_ref[s, s] = W
        if k:
            T = dot3(l_ref[s, :k], w_ref[:k, :k], NN)
            w_ref[s, :k] = -dot3(W, T, NN)
        if k + b < n:
            L = dot3(a_ref[k + b :, s], W, NT)
            l_ref[k + b :, s] = L
            for j in range(k + b, n, b):
                off = j - k - b
                a_ref[j:, j : j + b] = a_ref[j:, j : j + b] - dot3(L[off:], L[off : off + b], NT)


def factor_first_kernel(at_ref, mine_ref, other_ref, l_ref, w_ref, a_ref, m_ref, o_ref):
    n = a_ref.shape[0]
    for ref, sub in ((mine_ref, at_ref[0]), (other_ref, 1 - at_ref[0])):
        a_ref[pl.ds(pl.multiple_of(sub * 256, 256), 256), :] = ref[:, :, :n].reshape(256, n)
    factor_whole(a_ref, l_ref, w_ref, m_ref, o_ref)


def factor_second_kernel(
    at_ref, mask_ref, mine_ref, other_ref, w0_ref, p_ref, l_ref, w_ref, a_ref, m_ref, o_ref, b_ref
):
    n = a_ref.shape[0]
    for ref, sub in ((mine_ref, at_ref[0]), (other_ref, 1 - at_ref[0])):
        rows = pl.ds(pl.multiple_of(sub * 256, 256), 256)
        b_ref[rows, :] = ref[:, :, n : 2 * n].reshape(256, n)
        a_ref[rows, :] = ref[:, :, 2 * n :].reshape(256, n)
    panel = dot3(b_ref[...], w0_ref[...], NT).astype(BF16)
    p_ref[...] = panel
    h = n // 2
    for i in range(2):
        for j in range(i + 1):
            r, c = slice(i * h, (i + 1) * h), slice(j * h, (j + 1) * h)
            product = dot1(panel[r], panel[c], NT)
            a_ref[r, c] = a_ref[r, c] - jnp.where(mask_ref[i * 2 + j] > 0, product, F32(0))
    factor_whole(a_ref, l_ref, w_ref, m_ref, o_ref)


CHOL_COST = pl.CostEstimate(flops=20_000_000_000, bytes_accessed=3 * MIB, transcendentals=1024)


def factor_first(at, mine, other):
    n = mine.shape[-1] // 3
    return pl.pallas_call(
        factor_first_kernel,
        out_shape=[jax.ShapeDtypeStruct((n, n), F32)] * 2,
        in_specs=[SMEM, VMEM, VMEM],
        out_specs=[VMEM] * 2,
        scratch_shapes=[pltpu.VMEM((n, n), F32)] + [pltpu.VMEM((128, 256), F32)] * 2,
        cost_estimate=CHOL_COST,
        compiler_params=pltpu.CompilerParams(vmem_limit_bytes=40 * MIB),
    )(at, mine, other)


def factor_second(at, mask, mine, other, W0):
    n = W0.shape[0]
    return pl.pallas_call(
        factor_second_kernel,
        out_shape=[jax.ShapeDtypeStruct((n, n), BF16)] + [jax.ShapeDtypeStruct((n, n), F32)] * 2,
        in_specs=[SMEM, SMEM, VMEM, VMEM, VMEM],
        out_specs=[VMEM] * 3,
        scratch_shapes=[pltpu.VMEM((n, n), F32)]
        + [pltpu.VMEM((128, 256), F32)] * 2
        + [pltpu.VMEM((n, n), F32)],
        cost_estimate=CHOL_COST,
        compiler_params=pltpu.CompilerParams(vmem_limit_bytes=40 * MIB),
    )(at, mask, mine, other, W0)


def cut_top_kernel(x_ref, c_ref, o_ref):
    for k in range(6):
        o_ref[:, k] = c_ref[k].reshape(16, 16, 256)
    for i in range(3):
        for c in range(4):
            high, low = split(x_ref[pl.ds(i * 2048 + c, 256, stride=8), :])
            at = 6 + i * 4 + c // 2 * 2
            lanes = slice(c % 2 * 128, c % 2 * 128 + 128)
            o_ref[:, at, :, lanes] = high.reshape(16, 16, 128)
            o_ref[:, at + 1, :, lanes] = low.reshape(16, 16, 128)


def cut_top(front_rows, child):
    return pl.pallas_call(
        cut_top_kernel,
        grid=(1,),
        out_shape=jax.ShapeDtypeStruct((16, 18, 16, 256), BF16),
        in_specs=[
            pl.BlockSpec((6144, 128), lambda i: (0, 0)),
            pl.BlockSpec((6, 256, 256), lambda i: (0, 0, 0)),
        ],
        out_specs=pl.BlockSpec((16, 18, 16, 256), lambda i: (0, 0, 0, 0)),
        cost_estimate=pl.CostEstimate(flops=0, bytes_accessed=5 * MIB, transcendentals=0),
        compiler_params=pltpu.CompilerParams(vmem_limit_bytes=40 * MIB),
    )(front_rows, child)


def cut_low_kernel(at_ref, x_ref, o_ref):
    q = at_ref[1]
    o_ref[...] = jnp.zeros(o_ref.shape, F32)
    for owner in range(2):

        @pl.when(q == owner)
        def _():
            for c in range(4):
                tile = x_ref[pl.ds(c, 256, stride=8), :]
                o_ref[:, 0, :, owner * 512 + c * 128 : owner * 512 + c * 128 + 128] = tile.reshape(16, 16, 128)


def cut_low(at, front_rows):
    return pl.pallas_call(
        cut_low_kernel,
        grid=(5,),
        out_shape=jax.ShapeDtypeStruct((16, 5, 16, 1024), F32),
        in_specs=[SMEM, pl.BlockSpec((2048, 128), lambda i: (i + 3, 0))],
        out_specs=pl.BlockSpec((16, 1, 16, 1024), lambda i: (0, i, 0, 0)),
        cost_estimate=pl.CostEstimate(flops=0, bytes_accessed=12 * MIB, transcendentals=0),
    )(at, front_rows)


def add_pieces(value, slot_ref, c_ref, row, j):
    for child in range(2):
        slot = slot_ref[(row * 4 + j) * 2 + child]
        known = jnp.maximum(slot, 0)
        piece = c_ref[known // 6, lax.rem(known, 6)].astype(F32)
        value = value + jnp.where(slot >= 0, piece, F32(0))
    return value


def whole_piece(c_ref, row, j):
    at = 6 + row * 4 + j % 2 * 2
    return c_ref[j // 2, at].astype(F32) + c_ref[j // 2, at + 1].astype(F32)


def join_top_kernel(slot_ref, c_ref, o_ref):
    for i in range(2):
        for j in range(4):
            value = whole_piece(c_ref, i, j)
            o_ref[i, :, j * 256 : (j + 1) * 256] = add_pieces(value, slot_ref, c_ref, i, j)


def join_low_kernel(slot_ref, c_ref, f_ref, o_ref):
    for i in range(6):
        for j in range(4):
            lanes = slice(j * 256, (j + 1) * 256)
            value = f_ref[i - 1, :, lanes] if i else whole_piece(c_ref, 2, j)
            o_ref[i, :, lanes] = add_pieces(value, slot_ref, c_ref, i + 2, j)


def join_strips(kernel, count, slots, *operands):
    return pl.pallas_call(
        kernel,
        out_shape=jax.ShapeDtypeStruct((count, 16, 1024), F32),
        in_specs=[SMEM] + [VMEM] * len(operands),
        out_specs=VMEM,
        cost_estimate=pl.CostEstimate(flops=0, bytes_accessed=3 * MIB, transcendentals=0),
    )(slots, *operands)


def solve_first_kernel(keep_ref, d_ref, r_ref, w_ref, o_ref):
    width = w_ref.shape[0]
    b = jnp.concatenate(
        [d_ref[:, :, :width].reshape(32, width), r_ref[:, :, :width].reshape(96, width)], axis=0
    )
    x = dot3(b, w_ref[...], NT).reshape(8, 16, width)
    for i in range(8):
        o_ref[i] = jnp.where(keep_ref[i] > 0, x[i], F32(0)).astype(BF16)


def solve_second_kernel(keep_ref, d_ref, r_ref, p_ref, p10_ref, w_ref, o_ref):
    width = w_ref.shape[0]
    half = width // 2
    b = jnp.concatenate(
        [d_ref[:, :, width:].reshape(32, width), r_ref[:, :, width:].reshape(96, width)], axis=0
    )
    u = dot1(p_ref[...].reshape(128, width), p10_ref[...], NT)
    rows = []
    for i in range(8):
        s = slice(16 * i, 16 * i + 16)
        parts = []
        for j in range(2):
            c = slice(j * half, (j + 1) * half)
            parts.append(b[s, c] - jnp.where(keep_ref[8 + 2 * i + j] > 0, u[s, c], F32(0)))
        rows.append(jnp.concatenate(parts, axis=1))
    x = dot3(jnp.concatenate(rows, axis=0), w_ref[...], NT).reshape(8, 16, width)
    for i in range(8):
        o_ref[i] = jnp.where(keep_ref[i] > 0, x[i], F32(0)).astype(BF16)


def solve_strips(kernel, *operands):
    return pl.pallas_call(
        kernel,
        out_shape=jax.ShapeDtypeStruct((8, 16, 512), BF16),
        in_specs=[SMEM] + [VMEM] * (len(operands) - 1),
        out_specs=VMEM,
        cost_estimate=pl.CostEstimate(flops=400_000_000, bytes_accessed=2 * MIB, transcendentals=0),
    )(*operands)


def deal_kernel(at_ref, p0_ref, p1_ref, *refs):
    o_ref = refs[-1]
    for q in range(16):
        o_ref[q, 0:8] = p0_ref[...]
        o_ref[q, 8:16] = p1_ref[...]
    for panel in range(2):
        for k in range(4):
            row = lax.rem(at_ref[2] + k, 4) * 2
            for c in range(2):
                for lr in range(4):
                    o_ref[(lr % 2) * 8 + row + c, 16 + panel * 2 + lr // 2] = refs[panel * 4 + k][c, lr]


def deal(at, P0, P1, first, second):
    return pl.pallas_call(
        deal_kernel,
        out_shape=jax.ShapeDtypeStruct((16, 20, 16, 512), BF16),
        in_specs=[SMEM] + [VMEM] * 10,
        out_specs=VMEM,
        cost_estimate=pl.CostEstimate(flops=0, bytes_accessed=8 * MIB, transcendentals=0),
        compiler_params=pltpu.CompilerParams(vmem_limit_bytes=24 * MIB),
    )(at, P0, P1, *first, *second)


def extend_kernel(slot_ref, f_ref, *refs):
    child, (w_ref, o_ref, wh_ref, wl_ref) = refs[:8], refs[8:]
    i = pl.program_id(0)

    @pl.when(i == 0)
    def _():
        wh_ref[...], wl_ref[...] = split(w_ref[...])

    for j in range(4):
        live = [slot_ref[(i * 4 + j) * 2 + ch] >= 0 for ch in range(2)]
        pieces = [child[j * 2 + ch] for ch in range(2)]
        for c in range(2):
            lanes = slice(c * 128, (c + 1) * 128)
            rows = pl.ds(j * 2 + c, 256, stride=8)
            value = f_ref[rows, :]
            for ch in range(2):
                value = value + jnp.where(live[ch], pieces[ch][0, :, lanes].astype(F32), F32(0))
            o_ref[rows, :] = value


def extend(slots, front_rows, arrived, W):
    def child_spec(k):
        return pl.BlockSpec((1, 256, 256), lambda i, s: (jnp.maximum(s[i * 8 + k], 0), 0, 0))

    whole = pl.BlockSpec((512, 512), lambda i, s: (0, 0))

    return pl.pallas_call(
        extend_kernel,
        grid_spec=pltpu.PrefetchScalarGridSpec(
            num_scalar_prefetch=1,
            grid=(8,),
            in_specs=[pl.BlockSpec((2048, 128), lambda i, s: (i, 0))] + [child_spec(k) for k in range(8)]
            + [whole],
            out_specs=[pl.BlockSpec((2048, 128), lambda i, s: (i, 0)), whole, whole],
        ),
        out_shape=[jax.ShapeDtypeStruct(front_rows.shape, F32)]
        + [jax.ShapeDtypeStruct((512, 512), BF16)] * 2,
        cost_estimate=pl.CostEstimate(flops=0, bytes_accessed=24 * MIB, transcendentals=0),
        compiler_params=pltpu.CompilerParams(vmem_limit_bytes=24 * MIB),
    )(slots, front_rows, *([arrived] * 8), W)


def finish_kernel(flag_ref, f_ref, row0_ref, row1_ref, mine_ref, other_ref, l_ref, wh_ref, wl_ref, o_ref, cols_ref):
    i = pl.program_id(0)

    @pl.when(i == 0)
    def _():
        core = flag_ref[48]
        for ref, sub in ((mine_ref, core), (other_ref, 1 - core)):
            for panel in range(2):
                for lc in range(2):
                    strips = ref[:, panel * 2 + lc].reshape(256, 512)
                    cols_ref[lc * 2 + sub, :, panel * 512 : (panel + 1) * 512] = strips

    rows = jnp.concatenate([ref[:, 0].reshape(256, 512) for ref in (row0_ref, row1_ref)], axis=1)
    for lc in range(2):
        state = flag_ref[32 + i * 2 + lc]

        @pl.when(state > 0)
        def _():
            blocks = []
            for sc in range(2):
                j = lc * 2 + sc
                value = jnp.concatenate(
                    [f_ref[pl.ds(lc * 4 + sc * 2 + c, 256, stride=8), :] for c in range(2)], axis=1
                )
                product = dot1(rows, cols_ref[j], NT)
                blocks.append(value - jnp.where(flag_ref[i * 4 + j] > 0, product, F32(0)))
            block = jnp.concatenate(blocks, axis=1)

            def put(value):
                for c in range(4):
                    o_ref[pl.ds(lc * 4 + c, 256, stride=8), :] = value[:, c * 128 : (c + 1) * 128]

            @pl.when(state == 1)
            def _():
                put(block)

            if lc == 0:

                @pl.when(state == 2)
                def _():
                    high, low = split(block)
                    wh = wh_ref[...]
                    put(dot1(high, wh, NT) + (dot1(low, wh, NT) + dot1(high, wl_ref[...], NT)))

                @pl.when(state == 3)
                def _():
                    put(l_ref[pl.ds(pl.multiple_of(lax.rem(i, 2) * 256, 256), 256), :])

        @pl.when(state == 0)
        def _():
            for c in range(4):
                o_ref[pl.ds(lc * 4 + c, 256, stride=8), :] = jnp.zeros((256, 128), F32)


def finish(flags, extended, dealt, other, L, high, low):
    def whole(shape, *at):
        return pl.BlockSpec(shape, lambda i, f: at)

    return pl.pallas_call(
        finish_kernel,
        grid_spec=pltpu.PrefetchScalarGridSpec(
            num_scalar_prefetch=1,
            grid=(8,),
            in_specs=[pl.BlockSpec((2048, 128), lambda i, f: (i, 0))]
            + [pl.BlockSpec((16, 1, 16, 512), lambda i, f: (0, i, 0, 0))]
            + [pl.BlockSpec((16, 1, 16, 512), lambda i, f: (0, i + 8, 0, 0))]
            + [whole((16, 4, 16, 512), 0, 4, 0, 0), whole((16, 4, 16, 512), 0, 0, 0, 0)]
            + [whole((512, 512), 0, 0)] * 3,
            out_specs=pl.BlockSpec((2048, 128), lambda i, f: (i, 0)),
            scratch_shapes=[pltpu.VMEM((4, 256, 1024), BF16)],
        ),
        out_shape=jax.ShapeDtypeStruct(extended.shape, F32),
        cost_estimate=pl.CostEstimate(flops=5_000_000_000, bytes_accessed=24 * MIB, transcendentals=0),
        compiler_params=pltpu.CompilerParams(vmem_limit_bytes=48 * MIB),
    )(flags, extended, dealt, dealt, dealt, other, L, high, low)


def slot_of_targets(codes, row_map, rows, cols):
    index = jnp.arange(CNB, dtype=jnp.int32)

    def place(blocks):
        hit = row_map[None] == blocks[:, None, None]
        return jnp.sum(jnp.where(hit, index + 1, 0), axis=-1) - 1

    pi, pj = place(rows), place(cols)
    child = jnp.arange(2, dtype=jnp.int32) * (CNB * CNB)
    wanted = child + pi[:, None, :] * CNB + pj[None, :, :]
    known = (pi[:, None, :] >= 0) & (pj[None, :, :] >= 0)
    wanted = jnp.where(known, wanted, -2).reshape(-1)
    number = jnp.arange(codes.shape[0], dtype=jnp.int32)
    return jnp.sum(jnp.where(wanted[:, None] == codes[None, :], number + 1, 0), axis=-1) - 1


def spread(x, axis, count):
    return lax.all_to_all(jnp.broadcast_to(x[None], (count,) + x.shape), axis, 0, 0, tiled=True)


def local(front, child_blocks, row_map, slot_table, struct_mask):
    prow, pcol = lax.axis_size("prow"), lax.axis_size("pcol")
    p, q = lax.axis_index("prow"), lax.axis_index("pcol")
    core, y = p % 2, p // 2
    at = jnp.stack([core, q, y]).astype(jnp.int32)
    swap = [(i, i ^ 1) for i in range(8)]
    front_rows = front.reshape(16384, 128)
    child = child_blocks[0, 0]

    pair = jnp.arange(2, dtype=jnp.int32)
    row_blocks = jnp.arange(4, dtype=jnp.int32) * prow + p
    col_blocks = jnp.arange(2, dtype=jnp.int32) * pcol + q
    sub_rows = (2 * row_blocks[:, None] + pair).reshape(-1)
    sub_cols = (2 * col_blocks[:, None] + pair).reshape(-1)

    low_cut = cut_low(at, front_rows)
    low_front = lax.psum_scatter(
        low_cut.reshape(80, 16, 1024), "pcol", scatter_dimension=0, tiled=True
    )
    front_top, _ = lax.optimization_barrier((front_rows, low_cut))
    got = lax.all_to_all(cut_top(front_top, child.reshape(48, 256, 256)), "pcol", 0, 0, tiled=True)

    my_codes = lax.dynamic_index_in_dim(slot_table, p, 0, False)
    strip_slots = slot_of_targets(my_codes[:, :2].reshape(-1), row_map, sub_rows, jnp.arange(4, dtype=jnp.int32))
    slots = slot_of_targets(
        lax.dynamic_index_in_dim(my_codes, q, 1, False).reshape(-1), row_map, sub_rows, sub_cols
    )
    row_mask = struct_mask[sub_rows]
    lower = row_blocks[:, None] >= col_blocks[None, :]
    mask = row_mask[:, sub_cols]
    state = jnp.where(lower, 1, 0)
    owner = (q < 2) & (jnp.arange(2) == 0)
    state = jnp.where(owner[None, :] & lower, jnp.where(row_blocks[:, None] == q, 3, 2), state)
    flags = jnp.concatenate([mask.reshape(-1), jnp.repeat(state, 2, axis=0).reshape(-1), jnp.stack([core, 2 - q])])
    flags = flags.astype(jnp.int32)
    keep0 = (sub_rows >= 2).astype(jnp.int32)
    keep1 = jnp.concatenate([(sub_rows >= 4).astype(jnp.int32), row_mask[:, 2:4].reshape(-1)])

    top = join_strips(join_top_kernel, 2, strip_slots, got)

    half_top = lax.all_to_all(jnp.tile(top, (prow // 2, 1, 1)), "prow", 0, 0, tiled=True)
    first = spread(jnp.concatenate([half_top[0, :, :512], half_top[1]], axis=1), "pcol", pcol)
    diag = (first, lax.ppermute(first, "prow", swap))
    child, diag, low_front = lax.optimization_barrier((child, diag, low_front))
    arrived = lax.all_to_all(child, "pcol", 0, 0, tiled=True).reshape(48, 256, 256)

    def gather_columns(strips):
        halves = strips.reshape(4, 2, 16, 512)
        even, odd = halves[:, 0], halves[:, 1]
        sent = lax.ppermute(jnp.where(core == 0, odd, even), "prow", swap)
        kept = jnp.where(core == 0, even, odd)
        chip = jnp.where(core == 0, jnp.stack([kept, sent]), jnp.stack([sent, kept]))
        along = lambda k: [(2 * ((i + k) % 4) + c, 2 * i + c) for i in range(4) for c in range(2)]
        return [chip] + [lax.ppermute(chip, "prow", along(k)) for k in range(1, 4)]

    L0, W0 = factor_first(at, *diag)
    low = join_strips(join_low_kernel, 6, strip_slots, got, low_front)
    P0 = solve_strips(solve_first_kernel, keep0, top, low, W0)
    P0, diag = lax.optimization_barrier((P0, diag))
    cols0 = gather_columns(P0)
    P10, L1, W1 = factor_second(at, struct_mask[2:4, 2:4].reshape(-1), *diag, W0)
    W1, cols0 = lax.optimization_barrier((W1, cols0))
    P1 = solve_strips(solve_second_kernel, keep1, top, low, P0, P10, W1)
    cols1 = gather_columns(P1)

    dealt = deal(at, P0, P1, cols0, cols1)
    dealt, arrived = lax.optimization_barrier((dealt, arrived))
    dealt = lax.all_to_all(dealt, "pcol", 0, 0, tiled=True)
    L = jnp.where(q == 0, L0, L1)
    extended = extend(slots, front_rows, arrived, jnp.where(q == 0, W0, W1))
    dealt, extended, L = lax.optimization_barrier((dealt, extended, L))
    extended, high, low_part = extended
    other = lax.ppermute(dealt[:, 16:], "prow", swap)
    out = finish(flags, extended, dealt, other, L, high, low_part)
    return out.reshape(front.shape)


def solution(mesh):
    in_specs = (
        P(None, "prow", None, None, "pcol", None),
        P("prow", "pcol", None, None, None, None),
        P(),
        P(),
        P(),
    )
    out_specs = P(None, "prow", None, None, "pcol", None)
    return jax.shard_map(local, mesh=mesh, in_specs=in_specs, out_specs=out_specs, check_vma=False)
```
